512 devices in a mesh: tmpl: 128 (over x, y, z_lo), det: 4 (over z_hi, core).
Axes of the slice: x: 4, y: 4, z: 16 (z_hi: 2, z_lo: 8; z = z_hi * 8 + z_lo), core: 2. Of those that a mesh axis runs over, the one named last changes fastest.
Arguments:
- templates: bfloat16 [2, 4, 1024, 1024], P(None, 'det', 'tmpl'), may hold values from -6 to 6
- strain: bfloat16 [2, 3, 1024, 1024], P(None, None, 'tmpl', 'det'), may hold values from -6 to 6
- inverse_psd: float32 [3, 1024, 1024], P(None, 'tmpl'), may hold values from 0.5 to 18.5
- antenna: float32 [3, 64], replicated, may hold values from -1 to 1
- delays: int32 [3, 64], replicated, may hold values from -8 to 8
Outputs:
- sky_max: float32 [4, 1024, 1024], P('det', 'tmpl')
- peak: float32 [4, 64], P('det')
The draws below stay inside these ranges and needn't reach their ends.
All inputs are finite; a program needn't handle non-finite values.
Results may differ from the reference program's by a relative error of at most 0.0038.
Values may be sent and summed in bfloat16 or wider, within the bound.
A program may use at most 64 MiB of HBM per device.

```python
import math
import jax
import jax.numpy as jnp
from jax import lax

NU = 1024
NP = 1024
DET = 3
SKY = 64
DMAX = 8
TEMPLATES = 4


def draw_inverse_psd(key, part):
    key = jax.random.fold_in(key, 5)
    ramp = jnp.arange(NU, dtype=jnp.float32) / (NU - 1)
    level = 1.0 + 2.0 * ramp
    rough = jax.random.uniform(key, (DET, NU, NP), jnp.float32, 0.5, 2.0)
    return rough * level[None, :, None]


def touch_ends(result, rng, low, largest):
    dims = result.shape
    index_at = [jax.random.randint(jax.random.fold_in(rng, axis), (), 0, dims[axis]) for axis in range(len(dims))]
    result = result.at[tuple(index_at)].set(low)
    longest = dims.index(max(dims))
    index_at[longest] = (index_at[longest] + 1) % dims[longest]
    return result.at[tuple(index_at)].set(largest)


def block_scale(stream_key, extent, cuts, least, high):
    factor_of = 1.0
    for dim, shards_of in cuts:
        heights = jax.random.uniform(jax.random.fold_in(jax.random.fold_in(stream_key, 6), dim), (shards_of,), jnp.float32, least / len(cuts), high / len(cuts))
        factor_of = factor_of * jnp.repeat(jnp.exp(heights), extent[dim] // shards_of).reshape((-1,) + (1,) * (len(extent) - 1 - dim))
    return factor_of


def centred(rng, extent, scale, limit, shards=(), kind=jnp.bfloat16):
    level = block_scale(rng, extent, shards, -0.22, 0.18) if shards else 1.0
    entries = jax.random.normal(rng, extent, jnp.float32) * scale * level
    return jnp.minimum(jnp.maximum(entries, -limit), limit).astype(kind)


def setup_inputs(seed: int = 0) -> dict:
    seeds = jax.random.split(jax.random.key(seed), 6)
    return {
        "templates": centred(seeds[0], (2, TEMPLATES, NU, NP), 1.0, 6.0, ((1, 4), (2, 128))),
        "strain": centred(seeds[1], (2, DET, NU, NP), 1.0, 6.0, ((2, 128), (3, 4))),
        "inverse_psd": draw_inverse_psd(jax.random.fold_in(seeds[5], 71), 0),
        "antenna": jnp.clip(jax.random.uniform(seeds[3], (DET, SKY), jnp.float32, -1.0, 1.0), -1.0, 1.0),
        "delays": touch_ends(jax.random.randint(seeds[4], (DET, SKY), -DMAX, DMAX + 1), jax.random.fold_in(seeds[4], 1), -DMAX, DMAX).astype(jnp.int32),
    }


def dft_table(length):
    idx = jnp.arange(length, dtype=jnp.int32)
    phase_ids = idx[:, None] * idx[None, :] % length
    phases = phase_ids.astype(jnp.float32) * (2.0 * math.pi / length)
    return (jnp.cos(phases).astype(jnp.bfloat16), jnp.sin(phases).astype(jnp.bfloat16))

def mult(left, right, form):
    return jnp.einsum(form, left.astype(jnp.float32), right.astype(jnp.float32), precision=lax.Precision.HIGHEST)

def reference(templates, strain, inverse_psd, antenna, delays):
    cos_one, sin_one = dft_table(NP)
    cos_two, sin_two = dft_table(NU)
    full_length = NU * NP
    data_real = strain[0].astype(jnp.float32)
    data_imag = strain[1].astype(jnp.float32)
    phase_ids = jnp.arange(NU, dtype=jnp.int32)[:, None] * jnp.arange(NP, dtype=jnp.int32)[None, :] % full_length
    phases = phase_ids.astype(jnp.float32) * (2.0 * math.pi / full_length)
    twist_cos = jnp.cos(phases)
    twist_sin = jnp.sin(phases)

    def per_template(which):
        tmpl_real = templates[0, which].astype(jnp.float32)[None]
        tmpl_imag = templates[1, which].astype(jnp.float32)[None]
        sigma_sq = lax.optimization_barrier(jnp.sum((tmpl_real * tmpl_real + tmpl_imag * tmpl_imag) * inverse_psd, axis=(1, 2)))
        prod_real = ((tmpl_real * data_real + tmpl_imag * data_imag) * inverse_psd).astype(jnp.bfloat16)
        prod_imag = ((tmpl_real * data_imag - tmpl_imag * data_real) * inverse_psd).astype(jnp.bfloat16)
        section_real = mult(prod_real, cos_one, 'duv,vp->dup') - mult(prod_imag, sin_one, 'duv,vp->dup')
        section_imag = mult(prod_real, sin_one, 'duv,vp->dup') + mult(prod_imag, cos_one, 'duv,vp->dup')
        twist_real = (section_real * twist_cos - section_imag * twist_sin).astype(jnp.bfloat16)
        twist_imag = (section_real * twist_sin + section_imag * twist_cos).astype(jnp.bfloat16)
        out_real = mult(twist_real, cos_two, 'dup,uq->dpq') - mult(twist_imag, sin_two, 'dup,uq->dpq')
        out_imag = mult(twist_real, sin_two, 'dup,uq->dpq') + mult(twist_imag, cos_two, 'dup,uq->dpq')
        scale = 1.0 / jnp.sqrt(sigma_sq)
        out_real = out_real * scale[:, None, None]
        out_imag = out_imag * scale[:, None, None]
        series_real = jnp.transpose(out_real, (0, 2, 1)).reshape(DET, full_length)
        series_imag = jnp.transpose(out_imag, (0, 2, 1)).reshape(DET, full_length)

        def visit(best_power, sky_index):
            sum_real = jnp.zeros((full_length,), jnp.float32)
            sum_imag = jnp.zeros((full_length,), jnp.float32)
            for detector in range(DET):
                offset = delays[detector, sky_index]
                antenna_gain = antenna[detector, sky_index]
                sum_real = sum_real + antenna_gain * jnp.roll(series_real[detector], -offset)
                sum_imag = sum_imag + antenna_gain * jnp.roll(series_imag[detector], -offset)
            snr_power = sum_real * sum_real + sum_imag * sum_imag
            return (jnp.maximum(best_power, snr_power), jnp.max(snr_power))
        best_power, sky_peaks = lax.scan(visit, jnp.zeros((full_length,), jnp.float32), jnp.arange(SKY, dtype=jnp.int32))
        return (best_power.reshape(NU, NP).T, sky_peaks)
    sky_max, peak = lax.map(per_template, jnp.arange(TEMPLATES, dtype=jnp.int32))
    return (sky_max, peak)
```

```python
import math

import jax
import jax.numpy as jnp
import ml_dtypes
import numpy as np
from jax import lax
from jax.experimental import pallas as pl
from jax.experimental.pallas import tpu as pltpu
from jax.sharding import PartitionSpec as P

F32 = jnp.float32
BF16 = jnp.bfloat16
MESH = pl.DeviceIdType.MESH

LEN = 1024
FULL = LEN * LEN
DET = 3
SKY = 64
HALO = 8
CELLS = 16
ZS = 8
GROUPS = 4
ROWS = 8
WIDE = 64 + 2 * HALO
COLS = CELLS * WIDE
CHUNK = 256
NCHUNK = COLS // CHUNK
SIG = 16
LANES = SIG + DET * WIDE


def section_one_table():
    cols = np.arange(COLS)
    samples = 64 * (cols // WIDE) - HALO + cols % WIDE
    angle = 2.0 * np.pi * ((np.arange(LEN)[:, None] * samples[None, :]) % LEN) / LEN
    cos = np.cos(angle).reshape(LEN, NCHUNK, CHUNK)
    sin = np.sin(angle).reshape(LEN, NCHUNK, CHUNK)
    both = np.concatenate([cos, sin], axis=2)
    return np.ascontiguousarray(np.transpose(both, (1, 0, 2))).astype(ml_dtypes.bfloat16)


def last_section_table():
    table = np.zeros((ZS, 2, 2, ROWS, 2, 8, 8, 2))
    z = np.arange(ZS)[:, None, None, None]
    r = np.arange(ROWS)[None, :, None, None]
    m = np.arange(8)[None, None, :, None]
    h = np.arange(8)[None, None, None, :]
    angle = 2.0 * np.pi * (((8 * z + r) * (8 * m + h)) % 64) / 64
    for ql in range(2):
        table[:, ql, 0, :, 0, :, :, ql] = np.cos(angle)
        table[:, ql, 1, :, 0, :, :, ql] = -np.sin(angle)
        table[:, ql, 0, :, 1, :, :, ql] = np.sin(angle)
        table[:, ql, 1, :, 1, :, :, ql] = np.cos(angle)
    return table.reshape(256, 256).astype(ml_dtypes.bfloat16)


def unit_circle(turns):
    turns = turns & (FULL - 1)
    quarter = (turns + FULL // 8) >> 18
    x = (turns - (quarter << 18)).astype(F32) * (2.0 * math.pi / FULL)
    x2 = x * x
    s = x * (1.0 + x2 * (-1.0 / 6 + x2 * (1.0 / 120 + x2 * (-1.0 / 5040 + x2 * (1.0 / 362880)))))
    c = 1.0 + x2 * (-0.5 + x2 * (1.0 / 24 + x2 * (-1.0 / 720 + x2 * (1.0 / 40320))))
    odd = (quarter & 1) == 1
    cos = jnp.where(odd, s, c)
    sin = jnp.where(odd, c, s)
    cos = jnp.where(((quarter + 1) & 2) != 0, -cos, cos)
    sin = jnp.where((quarter & 2) != 0, -sin, sin)
    return cos, sin


def dft_four(a, b, c, d):
    sr, si = a[0] + c[0], a[1] + c[1]
    dr, di = a[0] - c[0], a[1] - c[1]
    tr, ti = b[0] + d[0], b[1] + d[1]
    er, ei = b[0] - d[0], b[1] - d[1]
    return (
        (sr + tr, si + ti),
        (dr - ei, di + er),
        (sr - tr, si - ti),
        (dr + ei, di - er),
    )


def dft_sixteen(cells):
    first = [dft_four(*[cells[4 * a + b] for a in range(4)]) for b in range(4)]
    out = [None] * 16
    for k0 in range(4):
        column = []
        for b in range(4):
            xr, xi = first[b][k0]
            turn = (b * k0) % 16
            if turn:
                wr = math.cos(2 * math.pi * turn / 16)
                wi = math.sin(2 * math.pi * turn / 16)
                xr, xi = xr * wr - xi * wi, xr * wi + xi * wr
            column.append((xr, xi))
        for k1, value in enumerate(dft_four(*column)):
            out[k0 + 4 * k1] = value
    return out


def split_two(x):
    high = x.astype(BF16).astype(F32)
    return high, x - high


def kernel(
    tmpl_hbm, strain_hbm, psd_hbm, ant, delay, tab_hbm, last_hbm,
    sky_out, peak_out,
    tmpl_v, strain_v, psd_v, tab_v, last_v, prod_v, twist_v, turn_v, turn2_v,
    send_xy, recv_xy, send_z, recv_z, fin_v, pk_v, send_r, recv_r, send_p, recv_p,
    load_sem, tab_sem, s_send, s_recv, xy_send, xy_recv, z_send, z_recv, r_send, r_recv, p_send, p_recv,
):
    t = lax.axis_index("tmpl")
    g = lax.axis_index("det")
    cell = lax.div(t, ZS)
    z = lax.rem(t, ZS)

    det_ids = [{"tmpl": t, "det": lax.rem(g + k, GROUPS)} for k in range(1, GROUPS)]
    cell_to = [lax.rem(cell + k, CELLS) for k in range(1, CELLS)]
    xy_ids = [{"tmpl": c * ZS + z, "det": g} for c in cell_to]
    z_to = [lax.rem(z + k, ZS) for k in range(1, ZS)]
    z_ids = [{"tmpl": cell * ZS + k, "det": g} for k in z_to]

    barrier = pltpu.get_barrier_semaphore()
    for who in det_ids + xy_ids + z_ids:
        pl.semaphore_signal(barrier, inc=1, device_id=who, device_id_type=MESH)

    loads = [
        pltpu.make_async_copy(strain_hbm, strain_v.at[g], load_sem.at[0]),
        pltpu.make_async_copy(tmpl_hbm, tmpl_v, load_sem.at[1]),
        pltpu.make_async_copy(psd_hbm, psd_v, load_sem.at[2]),
        pltpu.make_async_copy(last_hbm, last_v, load_sem.at[3]),
    ]
    tab_loads = [pltpu.make_async_copy(tab_hbm.at[n], tab_v.at[n], tab_sem.at[n]) for n in range(NCHUNK)]
    for copy in loads + tab_loads:
        copy.start()

    pl.semaphore_wait(barrier, len(det_ids) + len(xy_ids) + len(z_ids))

    s_copies = [
        pltpu.make_async_remote_copy(
            src_ref=strain_hbm, dst_ref=strain_v.at[g], send_sem=s_send.at[k], recv_sem=s_recv.at[k],
            device_id=det_ids[k], device_id_type=MESH,
        )
        for k in range(GROUPS - 1)
    ]
    for copy in s_copies:
        copy.start()

    row = lax.broadcasted_iota(jnp.int32, (ROWS, COLS), 0)
    col = lax.broadcasted_iota(jnp.int32, (ROWS, COLS), 1)
    sample = col - 2 * HALO * ((col * 52429) >> 22) - HALO
    cos, sin = unit_circle((t * ROWS + row) * sample)
    turn_v[0] = cos
    turn_v[1] = sin
    row = lax.broadcasted_iota(jnp.int32, (ROWS, 128), 0)
    for q in range(16):
        cos, sin = unit_circle((z * ROWS + row) * (q * LEN))
        turn2_v[0, q] = cos
        turn2_v[1, q] = sin

    for copy in loads[1:3]:
        copy.wait()
    both = tmpl_v[...].astype(F32)
    tr, ti = both[:ROWS], both[ROWS:]
    square = tr * tr + ti * ti
    parts = [
        split_two(jnp.sum(square * psd_v[ROWS * d : ROWS * d + ROWS, :], axis=1, keepdims=True))
        for d in range(DET)
    ]
    blank = jnp.zeros((ROWS, SIG - DET), F32)
    sig = [jnp.concatenate([parts[d][c] for d in range(DET)] + [blank], axis=1) for c in range(2)]

    loads[0].wait()
    for copy in s_copies:
        copy.wait_recv()
    for piece in range(GROUPS):
        lanes = slice(CHUNK * piece, CHUNK * piece + CHUNK)
        data = strain_v[piece].astype(F32)
        trl, til = tr[:, lanes], ti[:, lanes]
        real, imag = [], []
        for d in range(DET):
            dr = data[ROWS * d : ROWS * d + ROWS]
            di = data[ROWS * (DET + d) : ROWS * (DET + d) + ROWS]
            weight = psd_v[ROWS * d : ROWS * d + ROWS, lanes]
            real.append((trl * dr + til * di) * weight)
            imag.append((trl * di - til * dr) * weight)
        prod_v[:, lanes] = jnp.concatenate(real + imag, axis=0).astype(BF16)

    half = DET * ROWS
    product = prod_v[...]
    for n in range(NCHUNK):
        tab_loads[n].wait()
        out = jnp.dot(product, tab_v[n], preferred_element_type=F32)
        sec_r = out[:half, :CHUNK] - out[half:, CHUNK:]
        sec_i = out[:half, CHUNK:] + out[half:, :CHUNK]
        lanes = slice(CHUNK * n, CHUNK * n + CHUNK)
        cos, sin = turn_v[0, :, lanes], turn_v[1, :, lanes]
        for d in range(DET):
            rows = slice(ROWS * d, ROWS * d + ROWS)
            twist_v[0, rows, lanes] = sec_r[rows] * cos - sec_i[rows] * sin
            twist_v[1, rows, lanes] = sec_r[rows] * sin + sec_i[rows] * cos

    for c in range(CELLS):
        lanes = slice(WIDE * c, WIDE * c + WIDE)
        block = jnp.concatenate(
            [
                jnp.concatenate(
                    [sig[i]] + [twist_v[i, ROWS * d : ROWS * d + ROWS, lanes] for d in range(DET)], axis=1
                )
                for i in range(2)
            ],
            axis=0,
        ).astype(BF16)
        send_xy[0, c] = block[:, :128]
        send_xy[1, c] = block[:, 128:]

    xy_copies = []
    for part in range(2):
        copies = [
            pltpu.make_async_remote_copy(
                src_ref=send_xy.at[part, cell_to[k]], dst_ref=recv_xy.at[part, cell],
                send_sem=xy_send.at[part, k], recv_sem=xy_recv.at[part, k],
                device_id=xy_ids[k], device_id_type=MESH,
            )
            for k in range(CELLS - 1)
        ]
        for copy in copies:
            copy.start()
        xy_copies.append(copies)
        recv_xy[part, cell] = send_xy[part, cell]

    lane = lax.broadcasted_iota(jnp.int32, (ROWS, 128), 1)
    z_copies = []
    for part in range(2):
        for copy in xy_copies[part]:
            copy.wait_recv()
        cells = []
        for c in range(CELLS):
            value = recv_xy[part, c].astype(F32)
            cells.append((value[:ROWS], value[ROWS:]))
        bins = dft_sixteen(cells)
        if part == 0:
            high, low = split_two(bins[0][0] + bins[0][1])
        for q in range(16):
            xr, xi = bins[q]
            cos, sin = turn2_v[0, q], turn2_v[1, q]
            yr, yi = xr * cos - xi * sin, xr * sin + xi * cos
            if part == 0:
                yr = jnp.where(lane < SIG, high, yr)
                yi = jnp.where(lane < SIG, low, yi)
            send_z[part, q] = jnp.concatenate([yr, yi], axis=0).astype(BF16)
        copies = [
            pltpu.make_async_remote_copy(
                src_ref=send_z.at[part, pl.ds(2 * z_to[k], 2)], dst_ref=recv_z.at[part, z],
                send_sem=z_send.at[part, k], recv_sem=z_recv.at[part, k],
                device_id=z_ids[k], device_id_type=MESH,
            )
            for k in range(ZS - 1)
        ]
        for copy in copies:
            copy.start()
        z_copies.append(copies)
        recv_z[part, z] = send_z[part, pl.ds(2 * z, 2)]

    scales = None
    for part in range(2):
        for copy in z_copies[part]:
            copy.wait_recv()
        got = recv_z[part].reshape(256, 128)
        if part == 0:
            halves = recv_z[part, :, 0].astype(F32)
            total = jnp.sum(jnp.sum(halves, axis=0), axis=0, keepdims=True)
            scales = [1.0 / jnp.sqrt(total[:, d : d + 1]) for d in range(DET)]
        out = lax.dot_general(got, last_v[...] if part else _wait_load(loads[3], last_v), (((0,), (0,)), ((), ())), preferred_element_type=F32)
        for d in range(DET):
            low_row = max(SIG + WIDE * d, 128 * part)
            high_row = min(SIG + WIDE * (d + 1), 128 * part + 128)
            if low_row < high_row:
                block = out[low_row - 128 * part : high_row - 128 * part]
                fin_v[0, low_row:high_row, :] = block[:, :128] * scales[d]
                fin_v[1, low_row:high_row, :] = block[:, 128:] * scales[d]

    def visit(s, best):
        sum_r = sum_i = None
        for d in range(DET):
            rows = pl.ds(SIG + WIDE * d + HALO + delay[d, s], 64)
            gain = ant[d, s]
            real = gain * fin_v[0, rows, :]
            imag = gain * fin_v[1, rows, :]
            sum_r = real if sum_r is None else sum_r + real
            sum_i = imag if sum_i is None else sum_i + imag
        power = sum_r * sum_r + sum_i * sum_i
        pk_v[s] = jnp.max(power.reshape(8, 8, 128), axis=0)
        return jnp.maximum(best, power)

    best = lax.fori_loop(0, SKY, visit, jnp.zeros((64, 128), F32))

    tops = jnp.max(pk_v[...], axis=1)
    tops = jnp.max(jnp.transpose(tops), axis=0, keepdims=True)
    tops = jnp.concatenate([tops, jnp.zeros((1, 128 - SKY), F32)], axis=1)
    tops = jnp.broadcast_to(tops, (8, 128))
    for k in range(ZS):
        send_r[k, :8] = best[8 * k : 8 * k + 8]
        send_r[k, 8:] = tops
    r_copies = [
        pltpu.make_async_remote_copy(
            src_ref=send_r.at[z_to[k]], dst_ref=recv_r.at[z], send_sem=r_send.at[k], recv_sem=r_recv.at[k],
            device_id=z_ids[k], device_id_type=MESH,
        )
        for k in range(ZS - 1)
    ]
    for copy in r_copies:
        copy.start()
    recv_r[z] = send_r[z]
    for copy in r_copies:
        copy.wait_recv()
    tops = jnp.max(recv_r[:, 8:, :], axis=0)
    send_p[...] = tops
    p_copies = [
        pltpu.make_async_remote_copy(
            src_ref=send_p, dst_ref=recv_p.at[cell], send_sem=p_send.at[k], recv_sem=p_recv.at[k],
            device_id=xy_ids[k], device_id_type=MESH,
        )
        for k in range(CELLS - 1)
    ]
    for copy in p_copies:
        copy.start()
    recv_p[cell] = tops

    lane = lax.broadcasted_iota(jnp.int32, (8, 128), 1)
    owner = (lane >> 1) & 7
    for m in range(8):
        index = 16 * m + 2 * (lane >> 4) + (lane & 1)
        acc = jnp.zeros((8, 128), F32)
        for k in range(ZS):
            moved = jnp.take_along_axis(recv_r[k, :8], index, axis=1, mode="promise_in_bounds")
            acc = jnp.where(owner == k, moved, acc)
        sky_out[:, 128 * m : 128 * m + 128] = acc

    for copy in p_copies:
        copy.wait_recv()
    tops = jnp.max(recv_p[...], axis=0)
    peak_out[...] = tops[:1, :SKY]

    for copy in s_copies + xy_copies[0] + xy_copies[1] + z_copies[0] + z_copies[1] + r_copies + p_copies:
        copy.wait_send()


def _wait_load(copy, ref):
    copy.wait()
    return ref[...]


def shards(templates, strain, inverse_psd, antenna, delays):
    tab = jnp.asarray(section_one_table())
    last = jnp.asarray(last_section_table())
    any_spec = pl.BlockSpec(memory_space=pl.ANY)
    smem = pl.BlockSpec(memory_space=pltpu.SMEM)
    vmem = pl.BlockSpec(memory_space=pltpu.VMEM)
    dma = pltpu.SemaphoreType.DMA
    sky, peak = pl.pallas_call(
        kernel,
        out_shape=(
            jax.ShapeDtypeStruct((8, LEN), F32),
            jax.ShapeDtypeStruct((1, SKY), F32),
        ),
        in_specs=[any_spec, any_spec, any_spec, smem, smem, any_spec, any_spec],
        out_specs=(vmem, vmem),
        scratch_shapes=[
            pltpu.VMEM((16, LEN), BF16),
            pltpu.VMEM((GROUPS, 48, CHUNK), BF16),
            pltpu.VMEM((24, LEN), F32),
            pltpu.VMEM((NCHUNK, LEN, 2 * CHUNK), BF16),
            pltpu.VMEM((256, 256), BF16),
            pltpu.VMEM((48, LEN), BF16),
            pltpu.VMEM((2, 24, COLS), F32),
            pltpu.VMEM((2, ROWS, COLS), F32),
            pltpu.VMEM((2, 16, ROWS, 128), F32),
            pltpu.VMEM((2, CELLS, 16, 128), BF16),
            pltpu.VMEM((2, CELLS, 16, 128), BF16),
            pltpu.VMEM((2, 16, 16, 128), BF16),
            pltpu.VMEM((2, ZS, 2, 16, 128), BF16),
            pltpu.VMEM((2, 256, 128), F32),
            pltpu.VMEM((SKY, 8, 128), F32),
            pltpu.VMEM((ZS, 16, 128), F32),
            pltpu.VMEM((ZS, 16, 128), F32),
            pltpu.VMEM((8, 128), F32),
            pltpu.VMEM((CELLS, 8, 128), F32),
            dma((4,)), dma((NCHUNK,)),
            dma((GROUPS - 1,)), dma((GROUPS - 1,)),
            dma((2, CELLS - 1)), dma((2, CELLS - 1)),
            dma((2, ZS - 1)), dma((2, ZS - 1)),
            dma((ZS - 1,)), dma((ZS - 1,)),
            dma((CELLS - 1,)), dma((CELLS - 1,)),
        ],
        compiler_params=pltpu.CompilerParams(
            collective_id=0, has_side_effects=True, vmem_limit_bytes=40 * 1024 * 1024
        ),
        cost_estimate=pl.CostEstimate(flops=400_000_000, bytes_accessed=6_000_000, transcendentals=0),
    )(
        templates.reshape(16, LEN),
        strain.reshape(48, CHUNK),
        inverse_psd.reshape(24, LEN),
        antenna,
        delays,
        tab,
        last,
    )
    return (sky[None], peak)


def solution(mesh):
    return jax.shard_map(
        shards,
        mesh=mesh,
        in_specs=(
            P(None, "det", "tmpl", None),
            P(None, None, "tmpl", "det"),
            P(None, "tmpl", None),
            P(),
            P(),
        ),
        out_specs=(P("det", "tmpl", None), P("det", None)),
        check_vma=False,
    )
```

```python
import math

import jax
import jax.numpy as jnp
import ml_dtypes
import numpy as np
from jax import lax
from jax.experimental import pallas as pl
from jax.experimental.pallas import tpu as pltpu
from jax.sharding import PartitionSpec as P

F32 = jnp.float32
BF16 = jnp.bfloat16
MESH = pl.DeviceIdType.MESH

LEN = 1024
FULL = LEN * LEN
DET = 3
SKY = 64
HALO = 8
CELLS = 16
ZS = 8
GROUPS = 4
ROWS = 8
WIDE = 64 + 2 * HALO
COLS = CELLS * WIDE
CHUNK = 256
NCHUNK = COLS // CHUNK
SIG = 16
LANES = SIG + DET * WIDE


def section_one_table():
    cols = np.arange(COLS)
    samples = 64 * (cols // WIDE) - HALO + cols % WIDE
    angle = 2.0 * np.pi * ((np.arange(LEN)[:, None] * samples[None, :]) % LEN) / LEN
    cos = np.cos(angle).reshape(LEN, NCHUNK, CHUNK)
    sin = np.sin(angle).reshape(LEN, NCHUNK, CHUNK)
    both = np.concatenate([cos, sin], axis=2)
    return np.ascontiguousarray(np.transpose(both, (1, 0, 2))).astype(ml_dtypes.bfloat16)


def last_section_table():
    table = np.zeros((ZS, 2, 2, ROWS, 2, 8, 8, 2))
    z = np.arange(ZS)[:, None, None, None]
    r = np.arange(ROWS)[None, :, None, None]
    m = np.arange(8)[None, None, :, None]
    h = np.arange(8)[None, None, None, :]
    angle = 2.0 * np.pi * (((8 * z + r) * (8 * m + h)) % 64) / 64
    for ql in range(2):
        table[:, ql, 0, :, 0, :, :, ql] = np.cos(angle)
        table[:, ql, 1, :, 0, :, :, ql] = -np.sin(angle)
        table[:, ql, 0, :, 1, :, :, ql] = np.sin(angle)
        table[:, ql, 1, :, 1, :, :, ql] = np.cos(angle)
    return table.reshape(256, 256).astype(ml_dtypes.bfloat16)


def unit_circle(turns):
    turns = turns & (FULL - 1)
    quarter = (turns + FULL // 8) >> 18
    x = (turns - (quarter << 18)).astype(F32) * (2.0 * math.pi / FULL)
    x2 = x * x
    s = x * (1.0 + x2 * (-1.0 / 6 + x2 * (1.0 / 120 + x2 * (-1.0 / 5040 + x2 * (1.0 / 362880)))))
    c = 1.0 + x2 * (-0.5 + x2 * (1.0 / 24 + x2 * (-1.0 / 720 + x2 * (1.0 / 40320))))
    odd = (quarter & 1) == 1
    cos = jnp.where(odd, s, c)
    sin = jnp.where(odd, c, s)
    cos = jnp.where(((quarter + 1) & 2) != 0, -cos, cos)
    sin = jnp.where((quarter & 2) != 0, -sin, sin)
    return cos, sin


def dft_four(a, b, c, d):
    sr, si = a[0] + c[0], a[1] + c[1]
    dr, di = a[0] - c[0], a[1] - c[1]
    tr, ti = b[0] + d[0], b[1] + d[1]
    er, ei = b[0] - d[0], b[1] - d[1]
    return (
        (sr + tr, si + ti),
        (dr - ei, di + er),
        (sr - tr, si - ti),
        (dr + ei, di - er),
    )


def dft_sixteen(cells):
    first = [dft_four(*[cells[4 * a + b] for a in range(4)]) for b in range(4)]
    out = [None] * 16
    for k0 in range(4):
        column = []
        for b in range(4):
            xr, xi = first[b][k0]
            turn = (b * k0) % 16
            if turn:
                wr = math.cos(2 * math.pi * turn / 16)
                wi = math.sin(2 * math.pi * turn / 16)
                xr, xi = xr * wr - xi * wi, xr * wi + xi * wr
            column.append((xr, xi))
        for k1, value in enumerate(dft_four(*column)):
            out[k0 + 4 * k1] = value
    return out


def split_two(x):
    high = x.astype(BF16).astype(F32)
    return high, x - high


def kernel(
    tmpl_hbm, strain_hbm, psd_hbm, ant_hbm, delay_hbm, tab_hbm, last_hbm,
    sky_out, peak_out,
    ant, delay, tmpl_v, strain_v, psd_v, tab_v, last_v, acc_v, twist_v, turn_v, turn2_v,
    send_xy, recv_xy, send_z, recv_z, fin_v, pk_v, send_r, recv_r, send_p, recv_p,
    load_sem, tab_sem, s_send, s_recv, relay_v, relay_send, relay_recv, ready_xy, ready_z, go_xy, go_z, xy_send, xy_recv, z_send, z_recv, r_send, r_recv, p_send, p_recv,
):
    t = lax.axis_index("tmpl")
    g = lax.axis_index("det")
    cell = lax.div(t, ZS)
    z = lax.rem(t, ZS)

    late = lax.div(g, 2)
    near_z = z < ZS // 2
    core_g = g + 1 - 2 * lax.rem(g, 2)
    far_g = lax.rem(g + 2, GROUPS)
    diag_g = lax.rem(core_g + 2, GROUPS)
    core_id = {"tmpl": t, "det": core_g}
    far_id = {"tmpl": t, "det": far_g}
    cell_to = [lax.rem(cell + k, CELLS) for k in range(1, CELLS)]
    xy_ids = [{"tmpl": c * ZS + z, "det": g} for c in cell_to]
    z_to = [lax.rem(z + k, ZS) for k in range(1, ZS)]
    z_ids = [{"tmpl": cell * ZS + k, "det": g} for k in z_to]

    def signal(sem, who):
        pl.semaphore_signal(sem, inc=1, device_id=who, device_id_type=MESH)

    barrier = pltpu.get_barrier_semaphore()

    @pl.when(late == 0)
    def _():
        @pl.when(near_z)
        def _():
            signal(barrier, far_id)
            signal(barrier, {"tmpl": t + ZS // 2, "det": far_g})

    signal(barrier, core_id)

    @pl.when(late == 0)
    def _():
        for who in z_ids + xy_ids:
            signal(barrier, who)

    loads = [
        pltpu.make_async_copy(strain_hbm, strain_v.at[g], load_sem.at[0]),
        pltpu.make_async_copy(tmpl_hbm, tmpl_v, load_sem.at[1]),
        pltpu.make_async_copy(psd_hbm, psd_v, load_sem.at[2]),
        pltpu.make_async_copy(last_hbm, last_v, load_sem.at[3]),
        pltpu.make_async_copy(ant_hbm, ant, load_sem.at[4]),
        pltpu.make_async_copy(delay_hbm, delay, load_sem.at[5]),
    ]
    tab_loads = [pltpu.make_async_copy(tab_hbm.at[n], tab_v.at[n], tab_sem.at[n]) for n in range(NCHUNK)]
    for copy in loads + tab_loads:
        copy.start()

    def remote(source, target, send, recv, who):
        return pltpu.make_async_remote_copy(
            src_ref=source, dst_ref=target, send_sem=send, recv_sem=recv, device_id=who, device_id_type=MESH
        )

    to_core = remote(strain_hbm, strain_v.at[g], s_send.at[0], s_recv.at[0], core_id)
    to_far = remote(strain_hbm, strain_v.at[g], s_send.at[1], s_recv.at[1], far_id)
    to_relay = remote(strain_hbm, relay_v, s_send.at[1], relay_recv, {"tmpl": t - ZS // 2, "det": far_g})
    relayed = remote(relay_v, strain_v.at[far_g], relay_send, s_recv.at[1], {"tmpl": t + ZS // 2, "det": g})
    handed_on = remote(strain_v.at[far_g], strain_v.at[far_g], s_send.at[2], s_recv.at[2], core_id)

    @pl.when(late == 0)
    def _():
        pl.semaphore_wait(barrier, 1 + (ZS - 1) + (CELLS - 1))

    @pl.when(late == 1)
    def _():
        pl.semaphore_wait(barrier, 2)

        @pl.when(near_z)
        def _():
            to_far.start()

        @pl.when(jnp.logical_not(near_z))
        def _():
            to_relay.start()

    to_core.start()

    row = lax.broadcasted_iota(jnp.int32, (ROWS, COLS), 0)
    col = lax.broadcasted_iota(jnp.int32, (ROWS, COLS), 1)
    sample = col - 2 * HALO * ((col * 52429) >> 22) - HALO
    cos, sin = unit_circle((t * ROWS + row) * sample)
    turn_v[0] = cos
    turn_v[1] = sin
    row = lax.broadcasted_iota(jnp.int32, (ROWS, 128), 0)
    for q in range(16):
        cos, sin = unit_circle((z * ROWS + row) * (q * LEN))
        turn2_v[0, q] = cos
        turn2_v[1, q] = sin

    for copy in loads[1:3]:
        copy.wait()
    both = tmpl_v[...].astype(F32)
    tr, ti = both[:ROWS], both[ROWS:]
    square = tr * tr + ti * ti
    parts = [
        split_two(jnp.sum(square * psd_v[ROWS * d : ROWS * d + ROWS, :], axis=1, keepdims=True))
        for d in range(DET)
    ]
    blank = jnp.zeros((ROWS, SIG - DET), F32)
    sig = [jnp.concatenate([parts[d][c] for d in range(DET)] + [blank], axis=1) for c in range(2)]

    half = DET * ROWS
    for order, piece in enumerate([g, core_g, far_g, diag_g]):
        if order == 0:
            loads[0].wait()
            for copy in tab_loads:
                copy.wait()
        elif order == 1:
            to_core.wait_recv()
        elif order == 2:

            @pl.when(jnp.logical_and(late == 0, near_z))
            def _():
                to_relay.wait_recv()
                relayed.start()

            to_far.wait_recv()
            handed_on.start()

            @pl.when(late == 0)
            def _():
                to_far.start()
                for who in xy_ids:
                    signal(ready_xy, who)
                for who in z_ids:
                    signal(ready_z, who)

        else:
            handed_on.wait_recv()
        lanes = pl.ds(pl.multiple_of(CHUNK * piece, CHUNK), CHUNK)
        data = strain_v[piece].astype(F32)
        both = tmpl_v[:, lanes].astype(F32)
        trl, til = both[:ROWS], both[ROWS:]
        real, imag = [], []
        for d in range(DET):
            dr = data[ROWS * d : ROWS * d + ROWS]
            di = data[ROWS * (DET + d) : ROWS * (DET + d) + ROWS]
            weight = psd_v[ROWS * d : ROWS * d + ROWS, lanes]
            real.append((trl * dr + til * di) * weight)
            imag.append((trl * di - til * dr) * weight)
        product = jnp.concatenate(real + imag, axis=0).astype(BF16)
        for n in range(NCHUNK):
            out = jnp.dot(product, tab_v[n, lanes, :], preferred_element_type=F32)
            if order:
                out = out + acc_v[n]
            if order < GROUPS - 1:
                acc_v[n] = out
                continue
            sec_r = out[:half, :CHUNK] - out[half:, CHUNK:]
            sec_i = out[:half, CHUNK:] + out[half:, :CHUNK]
            cols = slice(CHUNK * n, CHUNK * n + CHUNK)
            cos, sin = turn_v[0, :, cols], turn_v[1, :, cols]
            for d in range(DET):
                rows = slice(ROWS * d, ROWS * d + ROWS)
                twist_v[0, rows, cols] = sec_r[rows] * cos - sec_i[rows] * sin
                twist_v[1, rows, cols] = sec_r[rows] * sin + sec_i[rows] * cos

    for c in range(CELLS):
        lanes = slice(WIDE * c, WIDE * c + WIDE)
        block = jnp.concatenate(
            [
                jnp.concatenate(
                    [sig[i]] + [twist_v[i, ROWS * d : ROWS * d + ROWS, lanes] for d in range(DET)], axis=1
                )
                for i in range(2)
            ],
            axis=0,
        ).astype(BF16)
        send_xy[0, c] = block[:, :128]
        send_xy[1, c] = block[:, 128:]

    @pl.when(late == 1)
    def _():
        pl.semaphore_wait(go_xy, 1)

    xy_copies = []
    for part in range(2):
        copies = [
            pltpu.make_async_remote_copy(
                src_ref=send_xy.at[part, cell_to[k]], dst_ref=recv_xy.at[part, cell],
                send_sem=xy_send.at[part, k], recv_sem=xy_recv.at[part, k],
                device_id=xy_ids[k], device_id_type=MESH,
            )
            for k in range(CELLS - 1)
        ]
        for copy in copies:
            copy.start()
        xy_copies.append(copies)
        recv_xy[part, cell] = send_xy[part, cell]

    @pl.when(late == 0)
    def _():
        pl.semaphore_wait(ready_xy, CELLS - 1)
        signal(go_xy, far_id)
        pl.semaphore_wait(ready_z, ZS - 1)
        signal(go_z, far_id)

    lane = lax.broadcasted_iota(jnp.int32, (ROWS, 128), 1)
    z_copies = []
    for part in range(2):
        for copy in xy_copies[part]:
            copy.wait_recv()
        cells = []
        for c in range(CELLS):
            value = recv_xy[part, c].astype(F32)
            cells.append((value[:ROWS], value[ROWS:]))
        bins = dft_sixteen(cells)
        if part == 0:
            high, low = split_two(bins[0][0] + bins[0][1])
        for q in range(16):
            xr, xi = bins[q]
            cos, sin = turn2_v[0, q], turn2_v[1, q]
            yr, yi = xr * cos - xi * sin, xr * sin + xi * cos
            if part == 0:
                yr = jnp.where(lane < SIG, high, yr)
                yi = jnp.where(lane < SIG, low, yi)
            send_z[part, q] = jnp.concatenate([yr, yi], axis=0).astype(BF16)
        copies = [
            pltpu.make_async_remote_copy(
                src_ref=send_z.at[part, pl.ds(2 * z_to[k], 2)], dst_ref=recv_z.at[part, z],
                send_sem=z_send.at[part, k], recv_sem=z_recv.at[part, k],
                device_id=z_ids[k], device_id_type=MESH,
            )
            for k in range(ZS - 1)
        ]
        if part == 0:

            @pl.when(late == 1)
            def _():
                pl.semaphore_wait(go_z, 1)

        for copy in copies:
            copy.start()
        z_copies.append(copies)
        recv_z[part, z] = send_z[part, pl.ds(2 * z, 2)]

    scales = None
    for part in range(2):
        for copy in z_copies[part]:
            copy.wait_recv()
        got = recv_z[part].reshape(256, 128)
        if part == 0:
            halves = recv_z[part, :, 0].astype(F32)
            total = jnp.sum(jnp.sum(halves, axis=0), axis=0, keepdims=True)
            scales = [1.0 / jnp.sqrt(total[:, d : d + 1]) for d in range(DET)]
        out = lax.dot_general(got, last_v[...] if part else _wait_load(loads[3], last_v), (((0,), (0,)), ((), ())), preferred_element_type=F32)
        for d in range(DET):
            low_row = max(SIG + WIDE * d, 128 * part)
            high_row = min(SIG + WIDE * (d + 1), 128 * part + 128)
            if low_row < high_row:
                block = out[low_row - 128 * part : high_row - 128 * part]
                fin_v[0, low_row:high_row, :] = block[:, :128] * scales[d]
                fin_v[1, low_row:high_row, :] = block[:, 128:] * scales[d]

    def visit(s, best):
        sum_r = sum_i = None
        for d in range(DET):
            rows = pl.ds(SIG + WIDE * d + HALO + delay[d, s], 64)
            gain = ant[d, s]
            real = gain * fin_v[0, rows, :]
            imag = gain * fin_v[1, rows, :]
            sum_r = real if sum_r is None else sum_r + real
            sum_i = imag if sum_i is None else sum_i + imag
        power = sum_r * sum_r + sum_i * sum_i
        pk_v[s] = jnp.max(power.reshape(8, 8, 128), axis=0)
        return jnp.maximum(best, power)

    loads[4].wait()
    loads[5].wait()
    best = lax.fori_loop(0, SKY, visit, jnp.zeros((64, 128), F32))

    tops = jnp.max(pk_v[...], axis=1)
    tops = jnp.max(jnp.transpose(tops), axis=0, keepdims=True)
    tops = jnp.concatenate([tops, jnp.zeros((1, 128 - SKY), F32)], axis=1)
    tops = jnp.broadcast_to(tops, (8, 128))
    for k in range(ZS):
        send_r[k, :8] = best[8 * k : 8 * k + 8]
        send_r[k, 8:] = tops
    r_copies = [
        pltpu.make_async_remote_copy(
            src_ref=send_r.at[z_to[k]], dst_ref=recv_r.at[z], send_sem=r_send.at[k], recv_sem=r_recv.at[k],
            device_id=z_ids[k], device_id_type=MESH,
        )
        for k in range(ZS - 1)
    ]
    for copy in r_copies:
        copy.start()
    recv_r[z] = send_r[z]
    for copy in r_copies:
        copy.wait_recv()
    tops = jnp.max(recv_r[:, 8:, :], axis=0)
    send_p[...] = tops
    p_copies = [
        pltpu.make_async_remote_copy(
            src_ref=send_p, dst_ref=recv_p.at[cell], send_sem=p_send.at[k], recv_sem=p_recv.at[k],
            device_id=xy_ids[k], device_id_type=MESH,
        )
        for k in range(CELLS - 1)
    ]
    for copy in p_copies:
        copy.start()
    recv_p[cell] = tops

    lane = lax.broadcasted_iota(jnp.int32, (8, 128), 1)
    owner = (lane >> 1) & 7
    for m in range(8):
        index = 16 * m + 2 * (lane >> 4) + (lane & 1)
        acc = jnp.zeros((8, 128), F32)
        for k in range(ZS):
            moved = jnp.take_along_axis(recv_r[k, :8], index, axis=1, mode="promise_in_bounds")
            acc = jnp.where(owner == k, moved, acc)
        sky_out[:, 128 * m : 128 * m + 128] = acc

    for copy in p_copies:
        copy.wait_recv()
    tops = jnp.max(recv_p[...], axis=0)
    peak_out[...] = tops[:1, :SKY]

    for copy in (to_core, to_far, handed_on):
        copy.wait_send()

    @pl.when(jnp.logical_and(late == 0, near_z))
    def _():
        relayed.wait_send()

    for copy in xy_copies[0] + xy_copies[1] + z_copies[0] + z_copies[1] + r_copies + p_copies:
        copy.wait_send()


def _wait_load(copy, ref):
    copy.wait()
    return ref[...]


def shards(templates, strain, inverse_psd, antenna, delays):
    tab = jnp.asarray(section_one_table())
    last = jnp.asarray(last_section_table())
    hbm = pl.BlockSpec(memory_space=pltpu.HBM)
    vmem = pl.BlockSpec(memory_space=pltpu.VMEM)
    dma = pltpu.SemaphoreType.DMA
    regular = pltpu.SemaphoreType.REGULAR
    sky, peak = pl.pallas_call(
        kernel,
        out_shape=(
            jax.ShapeDtypeStruct((8, LEN), F32),
            jax.ShapeDtypeStruct((1, SKY), F32),
        ),
        in_specs=[hbm] * 7,
        out_specs=(vmem, vmem),
        scratch_shapes=[
            pltpu.SMEM((DET, SKY), F32),
            pltpu.SMEM((DET, SKY), jnp.int32),
            pltpu.VMEM((16, LEN), BF16),
            pltpu.VMEM((GROUPS, 48, CHUNK), BF16),
            pltpu.VMEM((24, LEN), F32),
            pltpu.VMEM((NCHUNK, LEN, 2 * CHUNK), BF16),
            pltpu.VMEM((256, 256), BF16),
            pltpu.VMEM((NCHUNK, 48, 2 * CHUNK), F32),
            pltpu.VMEM((2, 24, COLS), F32),
            pltpu.VMEM((2, ROWS, COLS), F32),
            pltpu.VMEM((2, 16, ROWS, 128), F32),
            pltpu.VMEM((2, CELLS, 16, 128), BF16),
            pltpu.VMEM((2, CELLS, 16, 128), BF16),
            pltpu.VMEM((2, 16, 16, 128), BF16),
            pltpu.VMEM((2, ZS, 2, 16, 128), BF16),
            pltpu.VMEM((2, 256, 128), F32),
            pltpu.VMEM((SKY, 8, 128), F32),
            pltpu.VMEM((ZS, 16, 128), F32),
            pltpu.VMEM((ZS, 16, 128), F32),
            pltpu.VMEM((8, 128), F32),
            pltpu.VMEM((CELLS, 8, 128), F32),
            dma((6,)), dma((NCHUNK,)),
            dma((GROUPS - 1,)), dma((GROUPS - 1,)),
            pltpu.VMEM((48, CHUNK), BF16),
            dma, dma,
            regular, regular, regular, regular,
            dma((2, CELLS - 1)), dma((2, CELLS - 1)),
            dma((2, ZS - 1)), dma((2, ZS - 1)),
            dma((ZS - 1,)), dma((ZS - 1,)),
            dma((CELLS - 1,)), dma((CELLS - 1,)),
        ],
        compiler_params=pltpu.CompilerParams(
            collective_id=0, has_side_effects=True, vmem_limit_bytes=60 * 1024 * 1024
        ),
        cost_estimate=pl.CostEstimate(flops=400_000_000, bytes_accessed=6_000_000, transcendentals=0),
    )(
        templates.reshape(16, LEN),
        strain.reshape(48, CHUNK),
        inverse_psd.reshape(24, LEN),
        antenna,
        delays,
        tab,
        last,
    )
    return (sky[None], peak)


def solution(mesh):
    return jax.shard_map(
        shards,
        mesh=mesh,
        in_specs=(
            P(None, "det", "tmpl", None),
            P(None, None, "tmpl", "det"),
            P(None, "tmpl", None),
            P(),
            P(),
        ),
        out_specs=(P("det", "tmpl", None), P("det", None)),
        check_vma=False,
    )
```

```python
import math

import jax
import jax.numpy as jnp
import ml_dtypes
import numpy as np
from jax import lax
from jax.experimental import pallas as pl
from jax.experimental.pallas import tpu as pltpu
from jax.sharding import PartitionSpec as P

F32 = jnp.float32
BF16 = jnp.bfloat16
MESH = pl.DeviceIdType.MESH

LEN = 1024
FULL = LEN * LEN
DET = 3
SKY = 64
HALO = 8
CELLS = 16
ZS = 8
GROUPS = 4
ROWS = 8
WIDE = 64 + 2 * HALO
COLS = CELLS * WIDE
CHUNK = 256
NCHUNK = COLS // CHUNK
SIG = 16
LANES = SIG + DET * WIDE


def section_one_table():
    cols = np.arange(COLS)
    samples = 64 * (cols // WIDE) - HALO + cols % WIDE
    angle = 2.0 * np.pi * ((np.arange(LEN)[:, None] * samples[None, :]) % LEN) / LEN
    cos = np.cos(angle).reshape(LEN, NCHUNK, CHUNK)
    sin = np.sin(angle).reshape(LEN, NCHUNK, CHUNK)
    both = np.concatenate([cos, sin], axis=2)
    return np.ascontiguousarray(np.transpose(both, (1, 0, 2))).astype(ml_dtypes.bfloat16)


def last_section_table():
    table = np.zeros((ZS, 2, 2, ROWS, 2, 8, 8, 2))
    z = np.arange(ZS)[:, None, None, None]
    r = np.arange(ROWS)[None, :, None, None]
    m = np.arange(8)[None, None, :, None]
    h = np.arange(8)[None, None, None, :]
    angle = 2.0 * np.pi * (((8 * z + r) * (8 * m + h)) % 64) / 64
    for ql in range(2):
        table[:, ql, 0, :, 0, :, :, ql] = np.cos(angle)
        table[:, ql, 1, :, 0, :, :, ql] = -np.sin(angle)
        table[:, ql, 0, :, 1, :, :, ql] = np.sin(angle)
        table[:, ql, 1, :, 1, :, :, ql] = np.cos(angle)
    return table.reshape(256, 256).astype(ml_dtypes.bfloat16)


def unit_circle(turns):
    turns = turns & (FULL - 1)
    quarter = (turns + FULL // 8) >> 18
    x = (turns - (quarter << 18)).astype(F32) * (2.0 * math.pi / FULL)
    x2 = x * x
    s = x * (1.0 + x2 * (-1.0 / 6 + x2 * (1.0 / 120 + x2 * (-1.0 / 5040 + x2 * (1.0 / 362880)))))
    c = 1.0 + x2 * (-0.5 + x2 * (1.0 / 24 + x2 * (-1.0 / 720 + x2 * (1.0 / 40320))))
    odd = (quarter & 1) == 1
    cos = jnp.where(odd, s, c)
    sin = jnp.where(odd, c, s)
    cos = jnp.where(((quarter + 1) & 2) != 0, -cos, cos)
    sin = jnp.where((quarter & 2) != 0, -sin, sin)
    return cos, sin


def dft_four(a, b, c, d):
    sr, si = a[0] + c[0], a[1] + c[1]
    dr, di = a[0] - c[0], a[1] - c[1]
    tr, ti = b[0] + d[0], b[1] + d[1]
    er, ei = b[0] - d[0], b[1] - d[1]
    return (
        (sr + tr, si + ti),
        (dr - ei, di + er),
        (sr - tr, si - ti),
        (dr + ei, di - er),
    )


def dft_sixteen(cells):
    first = [dft_four(*[cells[4 * a + b] for a in range(4)]) for b in range(4)]
    out = [None] * 16
    for k0 in range(4):
        column = []
        for b in range(4):
            xr, xi = first[b][k0]
            turn = (b * k0) % 16
            if turn:
                wr = math.cos(2 * math.pi * turn / 16)
                wi = math.sin(2 * math.pi * turn / 16)
                xr, xi = xr * wr - xi * wi, xr * wi + xi * wr
            column.append((xr, xi))
        for k1, value in enumerate(dft_four(*column)):
            out[k0 + 4 * k1] = value
    return out


def z_far_first(z):
    upper = z >= ZS // 2
    low = jnp.where(upper, ZS - 1 - z, z)
    alone = ZS - 1 - 2 * low
    places = []
    for j in range(ZS - 1):
        step = low - lax.div(jnp.maximum(j - alone, 0), 2)
        side = lax.rem(jnp.maximum(j - alone, 0), 2)
        place = jnp.where(j < alone, ZS - 1 - j, low + step - 2 * step * side)
        places.append(jnp.where(upper, ZS - 1 - place, place))
    return places


def split_two(x):
    high = x.astype(BF16).astype(F32)
    return high, x - high


def kernel(
    tmpl_hbm, strain_hbm, psd_hbm, ant_hbm, delay_hbm, tab_hbm, last_hbm,
    sky_out, peak_out,
    ant, delay, tmpl_v, strain_v, psd_v, tab_v, last_v, acc_v, twist_v, turn_v, turn2_v,
    send_xy, recv_xy, send_z, recv_z, fin_v, pk_v, send_r, recv_r, send_p, recv_p,
    load_sem, tab_sem, s_send, s_recv, relay_v, relay_send, relay_recv, hello, hello_relay, ready_xy, ready_z, go_xy, go_z, xy_send, xy_recv, z_send, z_recv, r_send, r_recv, p_send, p_recv,
):
    t = lax.axis_index("tmpl")
    g = lax.axis_index("det")
    cell = lax.div(t, ZS)
    z = lax.rem(t, ZS)

    late = lax.div(g, 2)
    near_z = z < ZS // 2
    core_g = g + 1 - 2 * lax.rem(g, 2)
    far_g = lax.rem(g + 2, GROUPS)
    diag_g = lax.rem(core_g + 2, GROUPS)
    core_id = {"tmpl": t, "det": core_g}
    far_id = {"tmpl": t, "det": far_g}
    cell_to = [lax.rem(cell + k, CELLS) for k in range(1, CELLS)]
    xy_ids = [{"tmpl": c * ZS + z, "det": g} for c in cell_to]
    z_to = z_far_first(z)
    z_ids = [{"tmpl": cell * ZS + k, "det": g} for k in z_to]

    def signal(sem, who):
        pl.semaphore_signal(sem, inc=1, device_id=who, device_id_type=MESH)

    barrier = pltpu.get_barrier_semaphore()

    @pl.when(late == 0)
    def _():
        @pl.when(near_z)
        def _():
            signal(barrier, far_id)
            signal(barrier, {"tmpl": t + ZS // 2, "det": far_g})

    signal(barrier, core_id)

    @pl.when(late == 0)
    def _():
        for who in z_ids + xy_ids:
            signal(barrier, who)

    loads = [
        pltpu.make_async_copy(strain_hbm, strain_v.at[g], load_sem.at[0]),
        pltpu.make_async_copy(tmpl_hbm, tmpl_v, load_sem.at[1]),
        pltpu.make_async_copy(psd_hbm, psd_v, load_sem.at[2]),
        pltpu.make_async_copy(last_hbm, last_v, load_sem.at[3]),
        pltpu.make_async_copy(ant_hbm, ant, load_sem.at[4]),
        pltpu.make_async_copy(delay_hbm, delay, load_sem.at[5]),
    ]
    tab_loads = [pltpu.make_async_copy(tab_hbm.at[n], tab_v.at[n], tab_sem.at[n]) for n in range(NCHUNK)]
    for copy in loads + tab_loads:
        copy.start()

    def remote(source, target, send, recv, who):
        return pltpu.make_async_remote_copy(
            src_ref=source, dst_ref=target, send_sem=send, recv_sem=recv, device_id=who, device_id_type=MESH
        )

    to_core = remote(strain_hbm, strain_v.at[g], s_send.at[0], s_recv.at[0], core_id)
    to_far = remote(strain_hbm, strain_v.at[g], s_send.at[1], s_recv.at[1], far_id)
    to_relay = remote(strain_hbm, relay_v, s_send.at[1], relay_recv, {"tmpl": t - ZS // 2, "det": far_g})
    relayed = remote(relay_v, strain_v.at[far_g], relay_send, s_recv.at[1], {"tmpl": t + ZS // 2, "det": g})
    handed_on = remote(strain_v.at[far_g], strain_v.at[far_g], s_send.at[2], s_recv.at[2], core_id)

    @pl.when(late == 0)
    def _():
        pl.semaphore_wait(barrier, 1 + (ZS - 1) + (CELLS - 1))

        @pl.when(near_z)
        def _():
            pl.semaphore_wait(hello_relay, 1)
            signal(hello, {"tmpl": t + ZS // 2, "det": g})

    @pl.when(late == 1)
    def _():
        pl.semaphore_wait(barrier, 2)

        @pl.when(near_z)
        def _():
            signal(hello, far_id)
            to_far.start()

        @pl.when(jnp.logical_not(near_z))
        def _():
            signal(hello_relay, {"tmpl": t - ZS // 2, "det": far_g})
            to_relay.start()

    to_core.start()

    row = lax.broadcasted_iota(jnp.int32, (ROWS, COLS), 0)
    col = lax.broadcasted_iota(jnp.int32, (ROWS, COLS), 1)
    sample = col - 2 * HALO * ((col * 52429) >> 22) - HALO
    cos, sin = unit_circle((t * ROWS + row) * sample)
    turn_v[0] = cos
    turn_v[1] = sin
    row = lax.broadcasted_iota(jnp.int32, (ROWS, 128), 0)
    for q in range(16):
        cos, sin = unit_circle((z * ROWS + row) * (q * LEN))
        turn2_v[0, q] = cos
        turn2_v[1, q] = sin

    for copy in loads[1:3]:
        copy.wait()
    both = tmpl_v[...].astype(F32)
    tr, ti = both[:ROWS], both[ROWS:]
    square = tr * tr + ti * ti
    parts = [
        split_two(jnp.sum(square * psd_v[ROWS * d : ROWS * d + ROWS, :], axis=1, keepdims=True))
        for d in range(DET)
    ]
    blank = jnp.zeros((ROWS, SIG - DET), F32)
    sig = [jnp.concatenate([parts[d][c] for d in range(DET)] + [blank], axis=1) for c in range(2)]

    half = DET * ROWS
    for order, piece in enumerate([g, core_g, far_g, diag_g]):
        if order == 0:
            loads[0].wait()
            for copy in tab_loads:
                copy.wait()
        elif order == 1:
            to_core.wait_recv()
        elif order == 2:

            @pl.when(jnp.logical_and(late == 0, near_z))
            def _():
                to_relay.wait_recv()
                relayed.start()

            @pl.when(late == 0)
            def _():
                pl.semaphore_wait(hello, 1)
                to_far.start()
                for who in xy_ids:
                    signal(ready_xy, who)
                for who in z_ids:
                    signal(ready_z, who)

            to_far.wait_recv()
            handed_on.start()
        else:
            handed_on.wait_recv()
        lanes = pl.ds(pl.multiple_of(CHUNK * piece, CHUNK), CHUNK)
        data = strain_v[piece].astype(F32)
        both = tmpl_v[:, lanes].astype(F32)
        trl, til = both[:ROWS], both[ROWS:]
        real, imag = [], []
        for d in range(DET):
            dr = data[ROWS * d : ROWS * d + ROWS]
            di = data[ROWS * (DET + d) : ROWS * (DET + d) + ROWS]
            weight = psd_v[ROWS * d : ROWS * d + ROWS, lanes]
            real.append((trl * dr + til * di) * weight)
            imag.append((trl * di - til * dr) * weight)
        product = jnp.concatenate(real + imag, axis=0).astype(BF16)
        for n in range(NCHUNK):
            out = jnp.dot(product, tab_v[n, lanes, :], preferred_element_type=F32)
            if order:
                out = out + acc_v[n]
            if order < GROUPS - 1:
                acc_v[n] = out
                continue
            sec_r = out[:half, :CHUNK] - out[half:, CHUNK:]
            sec_i = out[:half, CHUNK:] + out[half:, :CHUNK]
            cols = slice(CHUNK * n, CHUNK * n + CHUNK)
            cos, sin = turn_v[0, :, cols], turn_v[1, :, cols]
            for d in range(DET):
                rows = slice(ROWS * d, ROWS * d + ROWS)
                twist_v[0, rows, cols] = sec_r[rows] * cos - sec_i[rows] * sin
                twist_v[1, rows, cols] = sec_r[rows] * sin + sec_i[rows] * cos

    for c in range(CELLS):
        lanes = slice(WIDE * c, WIDE * c + WIDE)
        block = jnp.concatenate(
            [
                jnp.concatenate(
                    [sig[i]] + [twist_v[i, ROWS * d : ROWS * d + ROWS, lanes] for d in range(DET)], axis=1
                )
                for i in range(2)
            ],
            axis=0,
        ).astype(BF16)
        send_xy[0, c] = block[:, :128]
        send_xy[1, c] = block[:, 128:]

    @pl.when(late == 1)
    def _():
        pl.semaphore_wait(go_xy, 1)

    xy_copies = []
    for part in range(2):
        copies = [
            pltpu.make_async_remote_copy(
                src_ref=send_xy.at[part, cell_to[k]], dst_ref=recv_xy.at[part, cell],
                send_sem=xy_send.at[part, k], recv_sem=xy_recv.at[part, k],
                device_id=xy_ids[k], device_id_type=MESH,
            )
            for k in range(CELLS - 1)
        ]
        for copy in copies:
            copy.start()
        xy_copies.append(copies)
        recv_xy[part, cell] = send_xy[part, cell]

    @pl.when(late == 0)
    def _():
        pl.semaphore_wait(ready_xy, CELLS - 1)
        signal(go_xy, far_id)
        pl.semaphore_wait(ready_z, ZS - 1)
        signal(go_z, far_id)

    lane = lax.broadcasted_iota(jnp.int32, (ROWS, 128), 1)
    z_copies = []
    for part in range(2):
        for copy in xy_copies[part]:
            copy.wait_recv()
        cells = []
        for c in range(CELLS):
            value = recv_xy[part, c].astype(F32)
            cells.append((value[:ROWS], value[ROWS:]))
        bins = dft_sixteen(cells)
        if part == 0:
            high, low = split_two(bins[0][0] + bins[0][1])
        for q in range(16):
            xr, xi = bins[q]
            cos, sin = turn2_v[0, q], turn2_v[1, q]
            yr, yi = xr * cos - xi * sin, xr * sin + xi * cos
            if part == 0:
                yr = jnp.where(lane < SIG, high, yr)
                yi = jnp.where(lane < SIG, low, yi)
            send_z[part, q] = jnp.concatenate([yr, yi], axis=0).astype(BF16)
        copies = [
            pltpu.make_async_remote_copy(
                src_ref=send_z.at[part, pl.ds(2 * z_to[k], 2)], dst_ref=recv_z.at[part, z],
                send_sem=z_send.at[part, k], recv_sem=z_recv.at[part, z],
                device_id=z_ids[k], device_id_type=MESH,
            )
            for k in range(ZS - 1)
        ]
        if part == 0:

            @pl.when(late == 1)
            def _():
                pl.semaphore_wait(go_z, 1)

        for copy in copies:
            copy.start()
        z_copies.append(copies)
        recv_z[part, z] = send_z[part, pl.ds(2 * z, 2)]

    scales = None
    for part in range(2):
        for k in z_to:
            pltpu.make_async_copy(recv_z.at[part, k], recv_z.at[part, k], z_recv.at[part, k]).wait()
        got = recv_z[part].reshape(256, 128)
        if part == 0:
            halves = recv_z[part, :, 0].astype(F32)
            total = jnp.sum(jnp.sum(halves, axis=0), axis=0, keepdims=True)
            scales = [1.0 / jnp.sqrt(total[:, d : d + 1]) for d in range(DET)]
        out = lax.dot_general(got, last_v[...] if part else _wait_load(loads[3], last_v), (((0,), (0,)), ((), ())), preferred_element_type=F32)
        for d in range(DET):
            low_row = max(SIG + WIDE * d, 128 * part)
            high_row = min(SIG + WIDE * (d + 1), 128 * part + 128)
            if low_row < high_row:
                block = out[low_row - 128 * part : high_row - 128 * part]
                fin_v[0, low_row:high_row, :] = block[:, :128] * scales[d]
                fin_v[1, low_row:high_row, :] = block[:, 128:] * scales[d]

    def visit(s, best):
        sum_r = sum_i = None
        for d in range(DET):
            rows = pl.ds(SIG + WIDE * d + HALO + delay[d, s], 64)
            gain = ant[d, s]
            real = gain * fin_v[0, rows, :]
            imag = gain * fin_v[1, rows, :]
            sum_r = real if sum_r is None else sum_r + real
            sum_i = imag if sum_i is None else sum_i + imag
        power = sum_r * sum_r + sum_i * sum_i
        pk_v[s] = jnp.max(power.reshape(8, 8, 128), axis=0)
        return jnp.maximum(best, power)

    loads[4].wait()
    loads[5].wait()
    best = lax.fori_loop(0, SKY, visit, jnp.zeros((64, 128), F32))

    for k in range(ZS):
        send_r[k] = best[8 * k : 8 * k + 8]
    r_copies = [
        remote(send_r.at[z_to[k]], recv_r.at[z], r_send.at[k], r_recv.at[z], z_ids[k]) for k in range(ZS - 1)
    ]
    for copy in r_copies:
        copy.start()
    recv_r[z] = send_r[z]

    tops = jnp.max(pk_v[...], axis=1)
    tops = jnp.max(jnp.transpose(tops), axis=0, keepdims=True)
    tops = jnp.concatenate([tops, jnp.zeros((1, 128 - SKY), F32)], axis=1)
    send_p[...] = jnp.broadcast_to(tops, (8, 128))
    others = CELLS * ZS - 1

    def tell(k, carry):
        who = lax.rem(t + k, CELLS * ZS)
        remote(send_p.at[pl.ds(0, 1)], recv_p.at[pl.ds(t, 1)], p_send, p_recv, {"tmpl": who, "det": g}).start()
        return carry

    lax.fori_loop(1, CELLS * ZS, tell, 0)
    recv_p[pl.ds(t, 1), :] = tops

    for k in z_to:
        pltpu.make_async_copy(recv_r.at[k], recv_r.at[k], r_recv.at[k]).wait()
    lane = lax.broadcasted_iota(jnp.int32, (8, 128), 1)
    owner = (lane >> 1) & 7
    for m in range(8):
        index = 16 * m + 2 * (lane >> 4) + (lane & 1)
        acc = jnp.zeros((8, 128), F32)
        for k in range(ZS):
            moved = jnp.take_along_axis(recv_r[k], index, axis=1, mode="promise_in_bounds")
            acc = jnp.where(owner == k, moved, acc)
        sky_out[:, 128 * m : 128 * m + 128] = acc

    rows = pl.ds(0, others)
    pltpu.make_async_copy(recv_p.at[rows], recv_p.at[rows], p_recv).wait()
    peak_out[...] = jnp.max(recv_p[...], axis=0, keepdims=True)[:, :SKY]

    for copy in (to_core, to_far, handed_on):
        copy.wait_send()

    @pl.when(jnp.logical_and(late == 0, near_z))
    def _():
        relayed.wait_send()

    for copy in xy_copies[0] + xy_copies[1] + z_copies[0] + z_copies[1] + r_copies:
        copy.wait_send()
    pltpu.make_async_copy(recv_p.at[rows], recv_p.at[rows], p_send).wait()


def _wait_load(copy, ref):
    copy.wait()
    return ref[...]


def hand_over(sky_in, peak_in, sky_out, peak_out, sem):
    copies = [pltpu.make_async_copy(sky_in, sky_out, sem.at[0]), pltpu.make_async_copy(peak_in, peak_out, sem.at[1])]
    for copy in copies:
        copy.start()
    for copy in copies:
        copy.wait()


def shards(templates, strain, inverse_psd, antenna, delays):
    tab = jnp.asarray(section_one_table())
    last = jnp.asarray(last_section_table())
    hbm = pl.BlockSpec(memory_space=pltpu.HBM)
    vmem = pl.BlockSpec(memory_space=pltpu.VMEM)
    dma = pltpu.SemaphoreType.DMA
    regular = pltpu.SemaphoreType.REGULAR
    sky, peak = pl.pallas_call(
        kernel,
        out_shape=(
            jax.ShapeDtypeStruct((8, LEN), F32),
            jax.ShapeDtypeStruct((1, SKY), F32),
        ),
        in_specs=[hbm] * 7,
        out_specs=(vmem, vmem),
        scratch_shapes=[
            pltpu.SMEM((DET, SKY), F32),
            pltpu.SMEM((DET, SKY), jnp.int32),
            pltpu.VMEM((16, LEN), BF16),
            pltpu.VMEM((GROUPS, 48, CHUNK), BF16),
            pltpu.VMEM((24, LEN), F32),
            pltpu.VMEM((NCHUNK, LEN, 2 * CHUNK), BF16),
            pltpu.VMEM((256, 256), BF16),
            pltpu.VMEM((NCHUNK, 48, 2 * CHUNK), F32),
            pltpu.VMEM((2, 24, COLS), F32),
            pltpu.VMEM((2, ROWS, COLS), F32),
            pltpu.VMEM((2, 16, ROWS, 128), F32),
            pltpu.VMEM((2, CELLS, 16, 128), BF16),
            pltpu.VMEM((2, CELLS, 16, 128), BF16),
            pltpu.VMEM((2, 16, 16, 128), BF16),
            pltpu.VMEM((2, ZS, 2, 16, 128), BF16),
            pltpu.VMEM((2, 256, 128), F32),
            pltpu.VMEM((SKY, 8, 128), F32),
            pltpu.VMEM((ZS, 8, 128), F32),
            pltpu.VMEM((ZS, 8, 128), F32),
            pltpu.VMEM((8, 128), F32),
            pltpu.VMEM((CELLS * ZS, 128), F32),
            dma((6,)), dma((NCHUNK,)),
            dma((GROUPS - 1,)), dma((GROUPS - 1,)),
            pltpu.VMEM((48, CHUNK), BF16),
            dma, dma,
            regular, regular, regular, regular, regular, regular,
            dma((2, CELLS - 1)), dma((2, CELLS - 1)),
            dma((2, ZS - 1)), dma((2, ZS)),
            dma((ZS - 1,)), dma((ZS,)),
            dma, dma,
        ],
        compiler_params=pltpu.CompilerParams(
            collective_id=0, has_side_effects=True, vmem_limit_bytes=60 * 1024 * 1024
        ),
        cost_estimate=pl.CostEstimate(flops=400_000_000, bytes_accessed=6_000_000, transcendentals=0),
    )(
        templates.reshape(16, LEN),
        strain.reshape(48, CHUNK),
        inverse_psd.reshape(24, LEN),
        antenna,
        delays,
        tab,
        last,
    )
    sky, peak = pl.pallas_call(
        hand_over,
        out_shape=(
            jax.ShapeDtypeStruct((8, LEN), F32),
            jax.ShapeDtypeStruct((1, SKY), F32),
        ),
        in_specs=[hbm, hbm],
        out_specs=(hbm, hbm),
        scratch_shapes=[dma((2,))],
    )(sky, peak)
    return (sky[None], peak)


def solution(mesh):
    return jax.shard_map(
        shards,
        mesh=mesh,
        in_specs=(
            P(None, "det", "tmpl", None),
            P(None, None, "tmpl", "det"),
            P(None, "tmpl", None),
            P(),
            P(),
        ),
        out_specs=(P("det", "tmpl", None), P("det", None)),
        check_vma=False,
    )
```

```python
import math

import jax
import jax.numpy as jnp
import ml_dtypes
import numpy as np
from jax import lax
from jax.experimental import pallas as pl
from jax.experimental.pallas import tpu as pltpu
from jax.sharding import PartitionSpec as P

F32 = jnp.float32
BF16 = jnp.bfloat16
MESH = pl.DeviceIdType.MESH

LEN = 1024
FULL = LEN * LEN
DET = 3
SKY = 64
HALO = 8
CELLS = 16
ZS = 8
GROUPS = 4
ROWS = 8
WIDE = 64 + 2 * HALO
COLS = CELLS * WIDE
CHUNK = 256
NCHUNK = COLS // CHUNK
SIG = 16
LANES = SIG + DET * WIDE
UNROLL = 4


def section_one_table():
    cols = np.arange(COLS)
    samples = 64 * (cols // WIDE) - HALO + cols % WIDE
    angle = 2.0 * np.pi * ((np.arange(LEN)[:, None] * samples[None, :]) % LEN) / LEN
    cos = np.cos(angle).reshape(LEN, NCHUNK, CHUNK)
    sin = np.sin(angle).reshape(LEN, NCHUNK, CHUNK)
    both = np.concatenate([cos, sin], axis=2)
    return np.ascontiguousarray(np.transpose(both, (1, 0, 2))).astype(ml_dtypes.bfloat16)


def last_section_table():
    table = np.zeros((ZS, 2, 2, ROWS, 2, 8, 8, 2))
    z = np.arange(ZS)[:, None, None, None]
    r = np.arange(ROWS)[None, :, None, None]
    m = np.arange(8)[None, None, :, None]
    h = np.arange(8)[None, None, None, :]
    angle = 2.0 * np.pi * (((8 * z + r) * (8 * m + h)) % 64) / 64
    for ql in range(2):
        table[:, ql, 0, :, 0, :, :, ql] = np.cos(angle)
        table[:, ql, 1, :, 0, :, :, ql] = -np.sin(angle)
        table[:, ql, 0, :, 1, :, :, ql] = np.sin(angle)
        table[:, ql, 1, :, 1, :, :, ql] = np.cos(angle)
    return table.reshape(256, 256).astype(ml_dtypes.bfloat16)


def unit_circle(turns):
    turns = turns & (FULL - 1)
    quarter = (turns + FULL // 8) >> 18
    x = (turns - (quarter << 18)).astype(F32) * (2.0 * math.pi / FULL)
    x2 = x * x
    s = x * (1.0 + x2 * (-1.0 / 6 + x2 * (1.0 / 120 + x2 * (-1.0 / 5040 + x2 * (1.0 / 362880)))))
    c = 1.0 + x2 * (-0.5 + x2 * (1.0 / 24 + x2 * (-1.0 / 720 + x2 * (1.0 / 40320))))
    odd = (quarter & 1) == 1
    cos = jnp.where(odd, s, c)
    sin = jnp.where(odd, c, s)
    cos = jnp.where(((quarter + 1) & 2) != 0, -cos, cos)
    sin = jnp.where((quarter & 2) != 0, -sin, sin)
    return cos, sin


def dft_four(a, b, c, d):
    sr, si = a[0] + c[0], a[1] + c[1]
    dr, di = a[0] - c[0], a[1] - c[1]
    tr, ti = b[0] + d[0], b[1] + d[1]
    er, ei = b[0] - d[0], b[1] - d[1]
    return (
        (sr + tr, si + ti),
        (dr - ei, di + er),
        (sr - tr, si - ti),
        (dr + ei, di - er),
    )


def dft_sixteen(cells):
    first = [dft_four(*[cells[4 * a + b] for a in range(4)]) for b in range(4)]
    out = [None] * 16
    for k0 in range(4):
        column = []
        for b in range(4):
            xr, xi = first[b][k0]
            turn = (b * k0) % 16
            if turn:
                wr = math.cos(2 * math.pi * turn / 16)
                wi = math.sin(2 * math.pi * turn / 16)
                xr, xi = xr * wr - xi * wi, xr * wi + xi * wr
            column.append((xr, xi))
        for k1, value in enumerate(dft_four(*column)):
            out[k0 + 4 * k1] = value
    return out


def z_far_first(z):
    upper = z >= ZS // 2
    low = jnp.where(upper, ZS - 1 - z, z)
    alone = ZS - 1 - 2 * low
    places = []
    for j in range(ZS - 1):
        step = low - lax.div(jnp.maximum(j - alone, 0), 2)
        side = lax.rem(jnp.maximum(j - alone, 0), 2)
        place = jnp.where(j < alone, ZS - 1 - j, low + step - 2 * step * side)
        places.append(jnp.where(upper, ZS - 1 - place, place))
    return places


def split_two(x):
    high = x.astype(BF16).astype(F32)
    return high, x - high


def kernel(
    tmpl_hbm, strain_hbm, psd_hbm, ant_hbm, delay_hbm, tab_hbm, last_hbm,
    sky_out, peak_out,
    ant, delay, tmpl_v, strain_v, psd_v, tab_v, last_v, acc_v, twist_v, turn_v, turn2_v,
    send_xy, recv_xy, send_z, recv_z, fin_v, pk_v, send_r, recv_r, send_p, recv_p,
    load_sem, tab_sem, s_send, s_recv, relay_v, relay_send, relay_recv, hello, ready, go, xy_send, xy_recv, z_send, z_recv, r_send, r_recv, p_send, p_recv,
):
    t = lax.axis_index("tmpl")
    g = lax.axis_index("det")
    cell = lax.div(t, ZS)
    z = lax.rem(t, ZS)

    late = lax.div(g, 2)
    near_z = z < ZS // 2
    core_g = g + 1 - 2 * lax.rem(g, 2)
    far_g = lax.rem(g + 2, GROUPS)
    diag_g = lax.rem(core_g + 2, GROUPS)
    core_id = {"tmpl": t, "det": core_g}
    far_id = {"tmpl": t, "det": far_g}
    side = 4
    offsets = sorted(
        ((a, b) for a in range(side) for b in range(side) if a or b),
        key=lambda o: -min(o[0], side - o[0]) - min(o[1], side - o[1]),
    )
    cell_x, cell_y = lax.div(cell, side), lax.rem(cell, side)
    cell_to = [lax.rem(cell_x + a, side) * side + lax.rem(cell_y + b, side) for a, b in offsets]
    xy_ids = [{"tmpl": c * ZS + z, "det": g} for c in cell_to]
    z_to = z_far_first(z)
    z_ids = [{"tmpl": cell * ZS + k, "det": g} for k in z_to]

    def signal(sem, who):
        pl.semaphore_signal(sem, inc=1, device_id=who, device_id_type=MESH)

    step = ZS // 2
    above_id = {"tmpl": t + step, "det": g}
    far_above_id = {"tmpl": t + step, "det": far_g}
    near_ids = [{"tmpl": cell * ZS + lax.rem(z + k, step), "det": g} for k in range(1, step)]
    barrier = pltpu.get_barrier_semaphore()

    @pl.when(late == 0)
    def _():
        @pl.when(near_z)
        def _():
            signal(barrier, far_id)
            signal(barrier, far_above_id)

    signal(barrier, core_id)

    @pl.when(late == 0)
    def _():
        for who in z_ids + xy_ids:
            signal(barrier, who)

    def remote(source, target, send, recv, who):
        return pltpu.make_async_remote_copy(
            src_ref=source, dst_ref=target, send_sem=send, recv_sem=recv, device_id=who, device_id_type=MESH
        )

    to_core = remote(strain_hbm, strain_v.at[g], s_send.at[0], s_recv.at[0], core_id)
    to_far = remote(strain_hbm, strain_v.at[g], s_send.at[1], s_recv.at[1], far_id)
    down_far = remote(strain_hbm, relay_v.at[0], s_send.at[1], relay_recv.at[0], {"tmpl": t - step, "det": far_g})
    down = remote(strain_hbm, relay_v.at[1], s_send.at[1], relay_recv.at[1], {"tmpl": t - step, "det": g})
    up = remote(relay_v.at[0], strain_v.at[far_g], relay_send.at[0], s_recv.at[1], above_id)
    up_far = remote(relay_v.at[1], strain_v.at[g], relay_send.at[1], s_recv.at[1], far_above_id)
    handed_on = remote(strain_v.at[far_g], strain_v.at[far_g], s_send.at[2], s_recv.at[2], core_id)
    is_near = jnp.logical_and(late == 0, near_z)

    @pl.when(late == 1)
    def _():
        pl.semaphore_wait(barrier, 2)

        @pl.when(near_z)
        def _():
            to_far.start()
            signal(hello, far_id)

        @pl.when(jnp.logical_not(near_z))
        def _():
            down_far.start()

        to_core.start()

    loads = [
        pltpu.make_async_copy(strain_hbm, strain_v.at[g], load_sem.at[0]),
        pltpu.make_async_copy(tmpl_hbm, tmpl_v, load_sem.at[1]),
        pltpu.make_async_copy(psd_hbm, psd_v, load_sem.at[2]),
        pltpu.make_async_copy(last_hbm, last_v, load_sem.at[3]),
        pltpu.make_async_copy(ant_hbm, ant, load_sem.at[4]),
        pltpu.make_async_copy(delay_hbm, delay, load_sem.at[5]),
    ]
    tab_loads = [pltpu.make_async_copy(tab_hbm.at[n], tab_v.at[n], tab_sem.at[n]) for n in range(NCHUNK)]
    for copy in loads + tab_loads:
        copy.start()

    row = lax.broadcasted_iota(jnp.int32, (ROWS, COLS), 0)
    col = lax.broadcasted_iota(jnp.int32, (ROWS, COLS), 1)
    sample = col - 2 * HALO * ((col * 52429) >> 22) - HALO
    cos, sin = unit_circle((t * ROWS + row) * sample)
    turn_v[0] = cos
    turn_v[1] = sin
    row = lax.broadcasted_iota(jnp.int32, (ROWS, 128), 0)
    for q in range(16):
        cos, sin = unit_circle((z * ROWS + row) * (q * LEN))
        turn2_v[0, q] = cos
        turn2_v[1, q] = sin

    for copy in loads[1:3]:
        copy.wait()
    both = tmpl_v[...].astype(F32)
    tr, ti = both[:ROWS], both[ROWS:]
    square = tr * tr + ti * ti
    parts = [
        split_two(jnp.sum(square * psd_v[ROWS * d : ROWS * d + ROWS, :], axis=1, keepdims=True))
        for d in range(DET)
    ]
    blank = jnp.zeros((ROWS, SIG - DET), F32)
    sig = [jnp.concatenate([parts[d][c] for d in range(DET)] + [blank], axis=1) for c in range(2)]

    half = DET * ROWS
    for order, piece in enumerate([g, core_g, far_g, diag_g]):
        if order == 0:
            loads[0].wait()
            for copy in tab_loads:
                copy.wait()
        elif order == 1:

            @pl.when(late == 0)
            def _():
                pl.semaphore_wait(barrier, 1 + (ZS - 1) + (CELLS - 1))

                @pl.when(near_z)
                def _():
                    down_far.wait_recv()
                    up.start()
                    to_core.start()
                    pl.semaphore_wait(hello, 1)
                    to_far.start()
                    for who in near_ids + xy_ids:
                        signal(ready, who)

                @pl.when(jnp.logical_not(near_z))
                def _():
                    down.start()
                    to_core.start()

            to_core.wait_recv()
        elif order == 2:
            to_far.wait_recv()
            handed_on.start()
        else:
            handed_on.wait_recv()
        lanes = pl.ds(pl.multiple_of(CHUNK * piece, CHUNK), CHUNK)
        data = strain_v[piece].astype(F32)
        both = tmpl_v[:, lanes].astype(F32)
        trl, til = both[:ROWS], both[ROWS:]
        real, imag = [], []
        for d in range(DET):
            dr = data[ROWS * d : ROWS * d + ROWS]
            di = data[ROWS * (DET + d) : ROWS * (DET + d) + ROWS]
            weight = psd_v[ROWS * d : ROWS * d + ROWS, lanes]
            real.append((trl * dr + til * di) * weight)
            imag.append((trl * di - til * dr) * weight)
        product = jnp.concatenate(real + imag, axis=0).astype(BF16)
        for n in range(NCHUNK):
            out = jnp.dot(product, tab_v[n, lanes, :], preferred_element_type=F32)
            if order:
                out = out + acc_v[n]
            if order < GROUPS - 1:
                acc_v[n] = out
                continue
            sec_r = out[:half, :CHUNK] - out[half:, CHUNK:]
            sec_i = out[:half, CHUNK:] + out[half:, :CHUNK]
            cols = slice(CHUNK * n, CHUNK * n + CHUNK)
            cos, sin = turn_v[0, :, cols], turn_v[1, :, cols]
            for d in range(DET):
                rows = slice(ROWS * d, ROWS * d + ROWS)
                twist_v[0, rows, cols] = sec_r[rows] * cos - sec_i[rows] * sin
                twist_v[1, rows, cols] = sec_r[rows] * sin + sec_i[rows] * cos

    for c in range(CELLS):
        lanes = slice(WIDE * c, WIDE * c + WIDE)
        block = jnp.concatenate(
            [
                jnp.concatenate(
                    [sig[i]] + [twist_v[i, ROWS * d : ROWS * d + ROWS, lanes] for d in range(DET)], axis=1
                )
                for i in range(2)
            ],
            axis=0,
        ).astype(BF16)
        send_xy[0, c] = block[:, :128]
        send_xy[1, c] = block[:, 128:]

    @pl.when(late == 1)
    def _():
        pl.semaphore_wait(go, 1)

    xy_copies = [
        remote(send_xy.at[:, cell_to[k]], recv_xy.at[:, cell], xy_send.at[k], xy_recv.at[k], xy_ids[k])
        for k in range(CELLS - 1)
    ]
    for copy in xy_copies:
        copy.start()
    recv_xy[:, cell] = send_xy[:, cell]

    @pl.when(is_near)
    def _():
        down.wait_recv()
        up_far.start()
        pl.semaphore_wait(ready, (step - 1) + (CELLS - 1))
        signal(go, far_id)
        signal(go, far_above_id)

    lane = lax.broadcasted_iota(jnp.int32, (ROWS, 128), 1)
    for copy in xy_copies:
        copy.wait_recv()
    for part in range(2):
        cells = []
        for c in range(CELLS):
            value = recv_xy[part, c].astype(F32)
            cells.append((value[:ROWS], value[ROWS:]))
        bins = dft_sixteen(cells)
        if part == 0:
            high, low = split_two(bins[0][0] + bins[0][1])
        for q in range(16):
            xr, xi = bins[q]
            cos, sin = turn2_v[0, q], turn2_v[1, q]
            yr, yi = xr * cos - xi * sin, xr * sin + xi * cos
            if part == 0:
                yr = jnp.where(lane < SIG, high, yr)
                yi = jnp.where(lane < SIG, low, yi)
            send_z[part, q] = jnp.concatenate([yr, yi], axis=0).astype(BF16)
    z_copies = [
        remote(send_z.at[:, pl.ds(2 * z_to[k], 2)], recv_z.at[:, z], z_send.at[k], z_recv.at[z], z_ids[k])
        for k in range(ZS - 1)
    ]
    for copy in z_copies:
        copy.start()
    recv_z[:, z] = send_z[:, pl.ds(2 * z, 2)]

    scales = None
    for k in z_to:
        pltpu.make_async_copy(recv_z.at[:, k], recv_z.at[:, k], z_recv.at[k]).wait()
    for part in range(2):
        got = recv_z[part].reshape(256, 128)
        if part == 0:
            halves = recv_z[part, :, 0].astype(F32)
            total = jnp.sum(jnp.sum(halves, axis=0), axis=0, keepdims=True)
            scales = [1.0 / jnp.sqrt(total[:, d : d + 1]) for d in range(DET)]
        out = lax.dot_general(got, last_v[...] if part else _wait_load(loads[3], last_v), (((0,), (0,)), ((), ())), preferred_element_type=F32)
        for d in range(DET):
            low_row = max(SIG + WIDE * d, 128 * part)
            high_row = min(SIG + WIDE * (d + 1), 128 * part + 128)
            if low_row < high_row:
                block = out[low_row - 128 * part : high_row - 128 * part]
                fin_v[0, low_row:high_row, :] = block[:, :128] * scales[d]
                fin_v[1, low_row:high_row, :] = block[:, 128:] * scales[d]

    def visit(s, best):
        sum_r = sum_i = None
        for d in range(DET):
            rows = pl.ds(SIG + WIDE * d + HALO + delay[d, s], 64)
            gain = ant[d, s]
            real = gain * fin_v[0, rows, :]
            imag = gain * fin_v[1, rows, :]
            sum_r = real if sum_r is None else sum_r + real
            sum_i = imag if sum_i is None else sum_i + imag
        power = sum_r * sum_r + sum_i * sum_i
        pk_v[s] = jnp.max(power.reshape(8, 8, 128), axis=0)
        return jnp.maximum(best, power)

    loads[4].wait()
    loads[5].wait()
    def visits(n, best):
        for k in range(UNROLL):
            best = visit(UNROLL * n + k, best)
        return best

    best = lax.fori_loop(0, SKY // UNROLL, visits, jnp.zeros((64, 128), F32))

    tops = jnp.max(pk_v[...], axis=1)
    tops = jnp.max(jnp.transpose(tops), axis=0, keepdims=True)
    tops = jnp.concatenate([tops, jnp.zeros((1, 128 - SKY), F32)], axis=1)
    send_p[...] = jnp.broadcast_to(tops, (8, 128))
    others = CELLS * ZS - 1

    for place in z_to + [z]:

        def tell(k, carry):
            who = {"tmpl": lax.rem(cell + k, CELLS) * ZS + place, "det": g}
            remote(send_p.at[pl.ds(0, 1)], recv_p.at[pl.ds(t, 1)], p_send, p_recv, who).start()
            return carry

        lax.fori_loop(1 if place is z else 0, CELLS, tell, 0)
    recv_p[pl.ds(t, 1), :] = tops

    for k in range(ZS):
        send_r[k] = best[8 * k : 8 * k + 8]
    r_copies = [
        remote(send_r.at[z_to[k]], recv_r.at[z], r_send.at[k], r_recv.at[z], z_ids[k]) for k in range(ZS - 1)
    ]
    for copy in r_copies:
        copy.start()
    recv_r[z] = send_r[z]

    for k in z_to:
        pltpu.make_async_copy(recv_r.at[k], recv_r.at[k], r_recv.at[k]).wait()
    lane = lax.broadcasted_iota(jnp.int32, (8, 128), 1)
    owner = (lane >> 1) & 7
    for m in range(8):
        index = 16 * m + 2 * (lane >> 4) + (lane & 1)
        acc = jnp.zeros((8, 128), F32)
        for k in range(ZS):
            moved = jnp.take_along_axis(recv_r[k], index, axis=1, mode="promise_in_bounds")
            acc = jnp.where(owner == k, moved, acc)
        sky_out[:, 128 * m : 128 * m + 128] = acc

    rows = pl.ds(0, others)
    pltpu.make_async_copy(recv_p.at[rows], recv_p.at[rows], p_recv).wait()
    peak_out[...] = jnp.max(recv_p[...], axis=0, keepdims=True)[:, :SKY]

    for copy in (to_core, to_far, handed_on):
        copy.wait_send()

    @pl.when(is_near)
    def _():
        up.wait_send()
        up_far.wait_send()

    for copy in xy_copies + z_copies + r_copies:
        copy.wait_send()
    pltpu.make_async_copy(recv_p.at[rows], recv_p.at[rows], p_send).wait()


def _wait_load(copy, ref):
    copy.wait()
    return ref[...]


def hand_over(sky_in, peak_in, sky_out, peak_out, sem):
    copies = [pltpu.make_async_copy(sky_in, sky_out, sem.at[0]), pltpu.make_async_copy(peak_in, peak_out, sem.at[1])]
    for copy in copies:
        copy.start()
    for copy in copies:
        copy.wait()


def shards(templates, strain, inverse_psd, antenna, delays):
    tab = jnp.asarray(section_one_table())
    last = jnp.asarray(last_section_table())
    hbm = pl.BlockSpec(memory_space=pltpu.HBM)
    anywhere = pl.BlockSpec(memory_space=pl.ANY)
    vmem = pl.BlockSpec(memory_space=pltpu.VMEM)
    dma = pltpu.SemaphoreType.DMA
    regular = pltpu.SemaphoreType.REGULAR
    sky, peak = pl.pallas_call(
        kernel,
        out_shape=(pltpu.VMEM((8, LEN), F32), pltpu.VMEM((1, SKY), F32)),
        in_specs=[hbm] * 7,
        out_specs=(vmem, vmem),
        scratch_shapes=[
            pltpu.SMEM((DET, SKY), F32),
            pltpu.SMEM((DET, SKY), jnp.int32),
            pltpu.VMEM((16, LEN), BF16),
            pltpu.VMEM((GROUPS, 48, CHUNK), BF16),
            pltpu.VMEM((24, LEN), F32),
            pltpu.VMEM((NCHUNK, LEN, 2 * CHUNK), BF16),
            pltpu.VMEM((256, 256), BF16),
            pltpu.VMEM((NCHUNK, 48, 2 * CHUNK), F32),
            pltpu.VMEM((2, 24, COLS), F32),
            pltpu.VMEM((2, ROWS, COLS), F32),
            pltpu.VMEM((2, 16, ROWS, 128), F32),
            pltpu.VMEM((2, CELLS, 16, 128), BF16),
            pltpu.VMEM((2, CELLS, 16, 128), BF16),
            pltpu.VMEM((2, 16, 16, 128), BF16),
            pltpu.VMEM((2, ZS, 2, 16, 128), BF16),
            pltpu.VMEM((2, 256, 128), F32),
            pltpu.VMEM((SKY, 8, 128), F32),
            pltpu.VMEM((ZS, 8, 128), F32),
            pltpu.VMEM((ZS, 8, 128), F32),
            pltpu.VMEM((8, 128), F32),
            pltpu.VMEM((CELLS * ZS, 128), F32),
            dma((6,)), dma((NCHUNK,)),
            dma((GROUPS - 1,)), dma((GROUPS - 1,)),
            pltpu.VMEM((2, 48, CHUNK), BF16),
            dma((2,)), dma((2,)),
            regular, regular, regular,
            dma((CELLS - 1,)), dma((CELLS - 1,)),
            dma((ZS - 1,)), dma((ZS,)),
            dma((ZS - 1,)), dma((ZS,)),
            dma, dma,
        ],
        compiler_params=pltpu.CompilerParams(
            collective_id=0, has_side_effects=True, vmem_limit_bytes=56 * 1024 * 1024
        ),
        cost_estimate=pl.CostEstimate(flops=400_000_000, bytes_accessed=6_000_000, transcendentals=0),
    )(
        templates.reshape(16, LEN),
        strain.reshape(48, CHUNK),
        inverse_psd.reshape(24, LEN),
        antenna,
        delays,
        tab,
        last,
    )
    sky, peak = pl.pallas_call(
        hand_over,
        out_shape=(jax.ShapeDtypeStruct((8, LEN), F32), jax.ShapeDtypeStruct((1, SKY), F32)),
        in_specs=[anywhere, anywhere],
        out_specs=(anywhere, anywhere),
        scratch_shapes=[dma((2,))],
        compiler_params=pltpu.CompilerParams(vmem_limit_bytes=1024 * 1024),
    )(sky, peak)
    return (sky[None], peak)


def solution(mesh):
    return jax.shard_map(
        shards,
        mesh=mesh,
        in_specs=(
            P(None, "det", "tmpl", None),
            P(None, None, "tmpl", "det"),
            P(None, "tmpl", None),
            P(),
            P(),
        ),
        out_specs=(P("det", "tmpl", None), P("det", None)),
        check_vma=False,
    )
```

```python
import math

import jax
import jax.numpy as jnp
import ml_dtypes
import numpy as np
from jax import lax
from jax.experimental import pallas as pl
from jax.experimental.pallas import tpu as pltpu
from jax.sharding import PartitionSpec as P

F32 = jnp.float32
BF16 = jnp.bfloat16
MESH = pl.DeviceIdType.MESH

LEN = 1024
FULL = LEN * LEN
DET = 3
SKY = 64
HALO = 8
CELLS = 16
ZS = 8
GROUPS = 4
ROWS = 8
WIDE = 64 + 2 * HALO
COLS = CELLS * WIDE
CHUNK = 256
NCHUNK = COLS // CHUNK
SIG = 16
LANES = SIG + DET * WIDE
UNROLL = 4


def section_one_table():
    cols = np.arange(COLS)
    samples = 64 * (cols // WIDE) - HALO + cols % WIDE
    angle = 2.0 * np.pi * ((np.arange(LEN)[:, None] * samples[None, :]) % LEN) / LEN
    cos = np.cos(angle).reshape(LEN, NCHUNK, CHUNK)
    sin = np.sin(angle).reshape(LEN, NCHUNK, CHUNK)
    both = np.concatenate([cos, sin], axis=2)
    return np.ascontiguousarray(np.transpose(both, (1, 0, 2))).astype(ml_dtypes.bfloat16)


def last_section_table():
    table = np.zeros((ZS, 2, 2, ROWS, 2, 8, 8, 2))
    z = np.arange(ZS)[:, None, None, None]
    r = np.arange(ROWS)[None, :, None, None]
    m = np.arange(8)[None, None, :, None]
    h = np.arange(8)[None, None, None, :]
    angle = 2.0 * np.pi * (((8 * z + r) * (8 * m + h)) % 64) / 64
    for ql in range(2):
        table[:, ql, 0, :, 0, :, :, ql] = np.cos(angle)
        table[:, ql, 1, :, 0, :, :, ql] = -np.sin(angle)
        table[:, ql, 0, :, 1, :, :, ql] = np.sin(angle)
        table[:, ql, 1, :, 1, :, :, ql] = np.cos(angle)
    return table.reshape(256, 256).astype(ml_dtypes.bfloat16)


def unit_circle(turns):
    turns = turns & (FULL - 1)
    quarter = (turns + FULL // 8) >> 18
    x = (turns - (quarter << 18)).astype(F32) * (2.0 * math.pi / FULL)
    x2 = x * x
    s = x * (1.0 + x2 * (-1.0 / 6 + x2 * (1.0 / 120 + x2 * (-1.0 / 5040 + x2 * (1.0 / 362880)))))
    c = 1.0 + x2 * (-0.5 + x2 * (1.0 / 24 + x2 * (-1.0 / 720 + x2 * (1.0 / 40320))))
    odd = (quarter & 1) == 1
    cos = jnp.where(odd, s, c)
    sin = jnp.where(odd, c, s)
    cos = jnp.where(((quarter + 1) & 2) != 0, -cos, cos)
    sin = jnp.where((quarter & 2) != 0, -sin, sin)
    return cos, sin


def dft_four(a, b, c, d):
    sr, si = a[0] + c[0], a[1] + c[1]
    dr, di = a[0] - c[0], a[1] - c[1]
    tr, ti = b[0] + d[0], b[1] + d[1]
    er, ei = b[0] - d[0], b[1] - d[1]
    return (
        (sr + tr, si + ti),
        (dr - ei, di + er),
        (sr - tr, si - ti),
        (dr + ei, di - er),
    )


def dft_sixteen(cells):
    first = [dft_four(*[cells[4 * a + b] for a in range(4)]) for b in range(4)]
    out = [None] * 16
    for k0 in range(4):
        column = []
        for b in range(4):
            xr, xi = first[b][k0]
            turn = (b * k0) % 16
            if turn:
                wr = math.cos(2 * math.pi * turn / 16)
                wi = math.sin(2 * math.pi * turn / 16)
                xr, xi = xr * wr - xi * wi, xr * wi + xi * wr
            column.append((xr, xi))
        for k1, value in enumerate(dft_four(*column)):
            out[k0 + 4 * k1] = value
    return out


def z_far_first(z):
    upper = z >= ZS // 2
    low = jnp.where(upper, ZS - 1 - z, z)
    alone = ZS - 1 - 2 * low
    places = []
    for j in range(ZS - 1):
        step = low - lax.div(jnp.maximum(j - alone, 0), 2)
        side = lax.rem(jnp.maximum(j - alone, 0), 2)
        place = jnp.where(j < alone, ZS - 1 - j, low + step - 2 * step * side)
        places.append(jnp.where(upper, ZS - 1 - place, place))
    return places


def split_two(x):
    high = x.astype(BF16).astype(F32)
    return high, x - high


def kernel(
    tmpl_hbm, strain_hbm, psd_hbm, ant_hbm, delay_hbm, tab_hbm, last_hbm,
    sky_out, peak_out,
    ant, delay, tmpl_v, strain_v, psd_v, tab_v, last_v, acc_v, twist_v, turn_v, turn2_v,
    send_xy, recv_xy, send_z, recv_z, fin_v, pk_v, send_r, recv_r, send_p, recv_p,
    load_sem, tab_sem, s_send, s_recv, relay_v, relay_send, relay_recv, hello, ready, go, xy_send, xy_recv, z_send, z_recv, r_send, r_recv, p_send, p_recv,
):
    t = lax.axis_index("tmpl")
    g = lax.axis_index("det")
    cell = lax.div(t, ZS)
    z = lax.rem(t, ZS)

    late = lax.div(g, 2)
    near_z = z < ZS // 2
    core_g = g + 1 - 2 * lax.rem(g, 2)
    far_g = lax.rem(g + 2, GROUPS)
    diag_g = lax.rem(core_g + 2, GROUPS)
    core_id = {"tmpl": t, "det": core_g}
    far_id = {"tmpl": t, "det": far_g}
    side = 4
    offsets = sorted(
        ((a, b) for a in range(side) for b in range(side) if a or b),
        key=lambda o: -min(o[0], side - o[0]) - min(o[1], side - o[1]),
    )
    cell_x, cell_y = lax.div(cell, side), lax.rem(cell, side)
    cell_to = [lax.rem(cell_x + a, side) * side + lax.rem(cell_y + b, side) for a, b in offsets]
    xy_ids = [{"tmpl": c * ZS + z, "det": g} for c in cell_to]
    z_to = z_far_first(z)
    z_ids = [{"tmpl": cell * ZS + k, "det": g} for k in z_to]

    def signal(sem, who):
        pl.semaphore_signal(sem, inc=1, device_id=who, device_id_type=MESH)

    step = ZS // 2
    middle = jnp.logical_and(z >= step, z < step + 2)
    top = z >= step + 2
    below_top = jnp.logical_and(z >= 2, z < step)
    above_id = {"tmpl": t + step, "det": g}
    far_above_id = {"tmpl": t + step, "det": far_g}
    near_ids = [{"tmpl": cell * ZS + lax.rem(z + k, step), "det": g} for k in range(1, step)]
    barrier = pltpu.get_barrier_semaphore()

    @pl.when(late == 0)
    def _():
        @pl.when(near_z)
        def _():
            signal(barrier, far_id)
            signal(barrier, far_above_id)

        @pl.when(middle)
        def _():
            signal(barrier, far_id)

        @pl.when(top)
        def _():
            signal(barrier, {"tmpl": t - step, "det": core_g})

    signal(barrier, core_id)

    @pl.when(late == 0)
    def _():
        for who in z_ids + xy_ids:
            signal(barrier, who)

    def remote(source, target, send, recv, who):
        return pltpu.make_async_remote_copy(
            src_ref=source, dst_ref=target, send_sem=send, recv_sem=recv, device_id=who, device_id_type=MESH
        )

    to_core = remote(strain_hbm, strain_v.at[g], s_send.at[0], s_recv.at[0], core_id)
    to_far = remote(strain_hbm, strain_v.at[g], s_send.at[1], s_recv.at[1], far_id)
    down_far = remote(strain_hbm, relay_v.at[0], s_send.at[1], relay_recv.at[0], {"tmpl": t - step, "det": far_g})
    down = remote(strain_hbm, relay_v.at[1], s_send.at[1], relay_recv.at[1], {"tmpl": t - step, "det": g})
    up = remote(relay_v.at[0], strain_v.at[far_g], relay_send.at[0], s_recv.at[1], above_id)
    up_far = remote(relay_v.at[1], strain_v.at[g], relay_send.at[1], s_recv.at[1], far_above_id)
    up_other = remote(
        relay_v.at[0], strain_v.at[far_g], relay_send.at[2], s_recv.at[2], {"tmpl": t + step, "det": core_g}
    )
    handed_on = remote(strain_v.at[far_g], strain_v.at[far_g], s_send.at[2], s_recv.at[2], core_id)
    is_near = jnp.logical_and(late == 0, near_z)
    hands_on = jnp.logical_or(late == 1, z < step + 2)

    @pl.when(late == 1)
    def _():
        pl.semaphore_wait(barrier, jnp.where(middle, 3, 2))

        @pl.when(near_z)
        def _():
            to_far.start()
            signal(hello, far_id)

        @pl.when(middle)
        def _():
            to_far.start()
            signal(hello, {"tmpl": t - step, "det": far_g})

        @pl.when(top)
        def _():
            down_far.start()

        to_core.start()

    loads = [
        pltpu.make_async_copy(strain_hbm, strain_v.at[g], load_sem.at[0]),
        pltpu.make_async_copy(tmpl_hbm, tmpl_v, load_sem.at[1]),
        pltpu.make_async_copy(psd_hbm, psd_v, load_sem.at[2]),
        pltpu.make_async_copy(last_hbm, last_v, load_sem.at[3]),
        pltpu.make_async_copy(ant_hbm, ant, load_sem.at[4]),
        pltpu.make_async_copy(delay_hbm, delay, load_sem.at[5]),
    ]
    tab_loads = [pltpu.make_async_copy(tab_hbm.at[n], tab_v.at[n], tab_sem.at[n]) for n in range(NCHUNK)]
    for copy in loads + tab_loads:
        copy.start()

    row = lax.broadcasted_iota(jnp.int32, (ROWS, COLS), 0)
    col = lax.broadcasted_iota(jnp.int32, (ROWS, COLS), 1)
    sample = col - 2 * HALO * ((col * 52429) >> 22) - HALO
    cos, sin = unit_circle((t * ROWS + row) * sample)
    turn_v[0] = cos
    turn_v[1] = sin
    row = lax.broadcasted_iota(jnp.int32, (ROWS, 128), 0)
    for q in range(16):
        cos, sin = unit_circle((z * ROWS + row) * (q * LEN))
        turn2_v[0, q] = cos
        turn2_v[1, q] = sin

    for copy in loads[1:3]:
        copy.wait()
    both = tmpl_v[...].astype(F32)
    tr, ti = both[:ROWS], both[ROWS:]
    square = tr * tr + ti * ti
    parts = [
        split_two(jnp.sum(square * psd_v[ROWS * d : ROWS * d + ROWS, :], axis=1, keepdims=True))
        for d in range(DET)
    ]
    blank = jnp.zeros((ROWS, SIG - DET), F32)
    sig = [jnp.concatenate([parts[d][c] for d in range(DET)] + [blank], axis=1) for c in range(2)]

    half = DET * ROWS
    for order, piece in enumerate([g, core_g, far_g, diag_g]):
        if order == 0:
            loads[0].wait()
            for copy in tab_loads:
                copy.wait()
        elif order == 1:

            @pl.when(late == 0)
            def _():
                pl.semaphore_wait(barrier, 1 + (ZS - 1) + (CELLS - 1) + jnp.where(below_top, 1, 0))

                @pl.when(near_z)
                def _():
                    @pl.when(below_top)
                    def _():
                        down_far.wait_recv()
                        up.start()
                        up_other.start()

                    to_core.start()
                    pl.semaphore_wait(hello, jnp.where(below_top, 1, 2))
                    to_far.start()
                    for who in near_ids + xy_ids:
                        signal(ready, who)

                @pl.when(jnp.logical_not(near_z))
                def _():
                    down.start()
                    to_core.start()

            to_core.wait_recv()
        elif order == 2:
            to_far.wait_recv()

            @pl.when(hands_on)
            def _():
                handed_on.start()

        else:
            handed_on.wait_recv()
        lanes = pl.ds(pl.multiple_of(CHUNK * piece, CHUNK), CHUNK)
        data = strain_v[piece].astype(F32)
        both = tmpl_v[:, lanes].astype(F32)
        trl, til = both[:ROWS], both[ROWS:]
        real, imag = [], []
        for d in range(DET):
            dr = data[ROWS * d : ROWS * d + ROWS]
            di = data[ROWS * (DET + d) : ROWS * (DET + d) + ROWS]
            weight = psd_v[ROWS * d : ROWS * d + ROWS, lanes]
            real.append((trl * dr + til * di) * weight)
            imag.append((trl * di - til * dr) * weight)
        product = jnp.concatenate(real + imag, axis=0).astype(BF16)
        for n in range(NCHUNK):
            out = jnp.dot(product, tab_v[n, lanes, :], preferred_element_type=F32)
            if order:
                out = out + acc_v[n]
            if order < GROUPS - 1:
                acc_v[n] = out
                continue
            sec_r = out[:half, :CHUNK] - out[half:, CHUNK:]
            sec_i = out[:half, CHUNK:] + out[half:, :CHUNK]
            cols = slice(CHUNK * n, CHUNK * n + CHUNK)
            cos, sin = turn_v[0, :, cols], turn_v[1, :, cols]
            for d in range(DET):
                rows = slice(ROWS * d, ROWS * d + ROWS)
                twist_v[0, rows, cols] = sec_r[rows] * cos - sec_i[rows] * sin
                twist_v[1, rows, cols] = sec_r[rows] * sin + sec_i[rows] * cos

    for c in range(CELLS):
        lanes = slice(WIDE * c, WIDE * c + WIDE)
        block = jnp.concatenate(
            [
                jnp.concatenate(
                    [sig[i]] + [twist_v[i, ROWS * d : ROWS * d + ROWS, lanes] for d in range(DET)], axis=1
                )
                for i in range(2)
            ],
            axis=0,
        ).astype(BF16)
        send_xy[0, c] = block[:, :128]
        send_xy[1, c] = block[:, 128:]

    @pl.when(late == 1)
    def _():
        pl.semaphore_wait(go, 1)

    xy_copies = [
        remote(send_xy.at[:, cell_to[k]], recv_xy.at[:, cell], xy_send.at[k], xy_recv.at[k], xy_ids[k])
        for k in range(CELLS - 1)
    ]
    for copy in xy_copies:
        copy.start()
    recv_xy[:, cell] = send_xy[:, cell]

    @pl.when(is_near)
    def _():
        down.wait_recv()
        up_far.start()
        pl.semaphore_wait(ready, (step - 1) + (CELLS - 1))
        signal(go, far_id)
        signal(go, far_above_id)

    lane = lax.broadcasted_iota(jnp.int32, (ROWS, 128), 1)
    for copy in xy_copies:
        copy.wait_recv()
    for part in range(2):
        cells = []
        for c in range(CELLS):
            value = recv_xy[part, c].astype(F32)
            cells.append((value[:ROWS], value[ROWS:]))
        bins = dft_sixteen(cells)
        if part == 0:
            high, low = split_two(bins[0][0] + bins[0][1])
        for q in range(16):
            xr, xi = bins[q]
            cos, sin = turn2_v[0, q], turn2_v[1, q]
            yr, yi = xr * cos - xi * sin, xr * sin + xi * cos
            if part == 0:
                yr = jnp.where(lane < SIG, high, yr)
                yi = jnp.where(lane < SIG, low, yi)
            send_z[part, q] = jnp.concatenate([yr, yi], axis=0).astype(BF16)
    z_copies = [
        remote(send_z.at[:, pl.ds(2 * z_to[k], 2)], recv_z.at[:, z], z_send.at[k], z_recv.at[z], z_ids[k])
        for k in range(ZS - 1)
    ]
    for copy in z_copies:
        copy.start()
    recv_z[:, z] = send_z[:, pl.ds(2 * z, 2)]

    scales = None
    for k in z_to:
        pltpu.make_async_copy(recv_z.at[:, k], recv_z.at[:, k], z_recv.at[k]).wait()
    for part in range(2):
        got = recv_z[part].reshape(256, 128)
        if part == 0:
            halves = recv_z[part, :, 0].astype(F32)
            total = jnp.sum(jnp.sum(halves, axis=0), axis=0, keepdims=True)
            scales = [1.0 / jnp.sqrt(total[:, d : d + 1]) for d in range(DET)]
        out = lax.dot_general(got, last_v[...] if part else _wait_load(loads[3], last_v), (((0,), (0,)), ((), ())), preferred_element_type=F32)
        for d in range(DET):
            low_row = max(SIG + WIDE * d, 128 * part)
            high_row = min(SIG + WIDE * (d + 1), 128 * part + 128)
            if low_row < high_row:
                block = out[low_row - 128 * part : high_row - 128 * part]
                fin_v[0, low_row:high_row, :] = block[:, :128] * scales[d]
                fin_v[1, low_row:high_row, :] = block[:, 128:] * scales[d]

    def visit(s, best):
        sum_r = sum_i = None
        for d in range(DET):
            rows = pl.ds(SIG + WIDE * d + HALO + delay[d, s], 64)
            gain = ant[d, s]
            real = gain * fin_v[0, rows, :]
            imag = gain * fin_v[1, rows, :]
            sum_r = real if sum_r is None else sum_r + real
            sum_i = imag if sum_i is None else sum_i + imag
        power = sum_r * sum_r + sum_i * sum_i
        pk_v[s] = jnp.max(power.reshape(8, 8, 128), axis=0)
        return jnp.maximum(best, power)

    loads[4].wait()
    loads[5].wait()
    def visits(n, best):
        for k in range(UNROLL):
            best = visit(UNROLL * n + k, best)
        return best

    best = lax.fori_loop(0, SKY // UNROLL, visits, jnp.zeros((64, 128), F32))

    tops = jnp.max(pk_v[...], axis=1)
    tops = jnp.max(jnp.transpose(tops), axis=0, keepdims=True)
    tops = jnp.concatenate([tops, jnp.zeros((1, 128 - SKY), F32)], axis=1)
    send_p[...] = jnp.broadcast_to(tops, (8, 128))
    others = CELLS * ZS - 1

    own = jnp.where(late == 0, z, ZS - 1 - z) * CELLS + cell

    def tell(k, carry):
        turn = k + jnp.where(k >= own, 1, 0)
        place = lax.div(turn, CELLS)
        place = jnp.where(late == 0, place, ZS - 1 - place)
        who = {"tmpl": lax.rem(turn, CELLS) * ZS + place, "det": g}
        remote(send_p.at[pl.ds(0, 1)], recv_p.at[pl.ds(t, 1)], p_send, p_recv, who).start()
        return carry

    lax.fori_loop(0, others, tell, 0)
    recv_p[pl.ds(t, 1), :] = tops

    for k in range(ZS):
        send_r[k] = best[8 * k : 8 * k + 8]
    r_copies = [
        remote(send_r.at[z_to[k]], recv_r.at[z], r_send.at[k], r_recv.at[z], z_ids[k]) for k in range(ZS - 1)
    ]
    for copy in r_copies:
        copy.start()
    recv_r[z] = send_r[z]

    for k in z_to:
        pltpu.make_async_copy(recv_r.at[k], recv_r.at[k], r_recv.at[k]).wait()
    lane = lax.broadcasted_iota(jnp.int32, (8, 128), 1)
    owner = (lane >> 1) & 7
    for m in range(8):
        index = 16 * m + 2 * (lane >> 4) + (lane & 1)
        acc = jnp.zeros((8, 128), F32)
        for k in range(ZS):
            moved = jnp.take_along_axis(recv_r[k], index, axis=1, mode="promise_in_bounds")
            acc = jnp.where(owner == k, moved, acc)
        sky_out[:, 128 * m : 128 * m + 128] = acc

    rows = pl.ds(0, others)
    pltpu.make_async_copy(recv_p.at[rows], recv_p.at[rows], p_recv).wait()
    peak_out[...] = jnp.max(recv_p[...], axis=0, keepdims=True)[:, :SKY]

    for copy in (to_core, to_far):
        copy.wait_send()

    @pl.when(hands_on)
    def _():
        handed_on.wait_send()

    @pl.when(is_near)
    def _():
        up_far.wait_send()

        @pl.when(below_top)
        def _():
            up.wait_send()
            up_other.wait_send()

    for copy in xy_copies + z_copies + r_copies:
        copy.wait_send()
    pltpu.make_async_copy(recv_p.at[rows], recv_p.at[rows], p_send).wait()


def _wait_load(copy, ref):
    copy.wait()
    return ref[...]


def hand_over(sky_in, peak_in, sky_out, peak_out, sem):
    copies = [pltpu.make_async_copy(sky_in, sky_out, sem.at[0]), pltpu.make_async_copy(peak_in, peak_out, sem.at[1])]
    for copy in copies:
        copy.start()
    for copy in copies:
        copy.wait()


def shards(templates, strain, inverse_psd, antenna, delays):
    tab = jnp.asarray(section_one_table())
    last = jnp.asarray(last_section_table())
    hbm = pl.BlockSpec(memory_space=pltpu.HBM)
    anywhere = pl.BlockSpec(memory_space=pl.ANY)
    vmem = pl.BlockSpec(memory_space=pltpu.VMEM)
    dma = pltpu.SemaphoreType.DMA
    regular = pltpu.SemaphoreType.REGULAR
    sky, peak = pl.pallas_call(
        kernel,
        out_shape=(pltpu.VMEM((8, LEN), F32), pltpu.VMEM((1, SKY), F32)),
        in_specs=[hbm] * 7,
        out_specs=(vmem, vmem),
        scratch_shapes=[
            pltpu.SMEM((DET, SKY), F32),
            pltpu.SMEM((DET, SKY), jnp.int32),
            pltpu.VMEM((16, LEN), BF16),
            pltpu.VMEM((GROUPS, 48, CHUNK), BF16),
            pltpu.VMEM((24, LEN), F32),
            pltpu.VMEM((NCHUNK, LEN, 2 * CHUNK), BF16),
            pltpu.VMEM((256, 256), BF16),
            pltpu.VMEM((NCHUNK, 48, 2 * CHUNK), F32),
            pltpu.VMEM((2, 24, COLS), F32),
            pltpu.VMEM((2, ROWS, COLS), F32),
            pltpu.VMEM((2, 16, ROWS, 128), F32),
            pltpu.VMEM((2, CELLS, 16, 128), BF16),
            pltpu.VMEM((2, CELLS, 16, 128), BF16),
            pltpu.VMEM((2, 16, 16, 128), BF16),
            pltpu.VMEM((2, ZS, 2, 16, 128), BF16),
            pltpu.VMEM((2, 256, 128), F32),
            pltpu.VMEM((SKY, 8, 128), F32),
            pltpu.VMEM((ZS, 8, 128), F32),
            pltpu.VMEM((ZS, 8, 128), F32),
            pltpu.VMEM((8, 128), F32),
            pltpu.VMEM((CELLS * ZS, 128), F32),
            dma((6,)), dma((NCHUNK,)),
            dma((GROUPS - 1,)), dma((GROUPS - 1,)),
            pltpu.VMEM((2, 48, CHUNK), BF16),
            dma((3,)), dma((2,)),
            regular, regular, regular,
            dma((CELLS - 1,)), dma((CELLS - 1,)),
            dma((ZS - 1,)), dma((ZS,)),
            dma((ZS - 1,)), dma((ZS,)),
            dma, dma,
        ],
        compiler_params=pltpu.CompilerParams(
            collective_id=0, has_side_effects=True, vmem_limit_bytes=56 * 1024 * 1024
        ),
        cost_estimate=pl.CostEstimate(flops=400_000_000, bytes_accessed=6_000_000, transcendentals=0),
    )(
        templates.reshape(16, LEN),
        strain.reshape(48, CHUNK),
        inverse_psd.reshape(24, LEN),
        antenna,
        delays,
        tab,
        last,
    )
    sky, peak = pl.pallas_call(
        hand_over,
        out_shape=(jax.ShapeDtypeStruct((8, LEN), F32), jax.ShapeDtypeStruct((1, SKY), F32)),
        in_specs=[anywhere, anywhere],
        out_specs=(anywhere, anywhere),
        scratch_shapes=[dma((2,))],
        compiler_params=pltpu.CompilerParams(vmem_limit_bytes=1024 * 1024),
    )(sky, peak)
    return (sky[None], peak)


def solution(mesh):
    return jax.shard_map(
        shards,
        mesh=mesh,
        in_specs=(
            P(None, "det", "tmpl", None),
            P(None, None, "tmpl", "det"),
            P(None, "tmpl", None),
            P(),
            P(),
        ),
        out_specs=(P("det", "tmpl", None), P("det", None)),
        check_vma=False,
    )
```

```python
import math

import jax
import jax.numpy as jnp
import ml_dtypes
import numpy as np
from jax import lax
from jax.experimental import pallas as pl
from jax.experimental.pallas import tpu as pltpu
from jax.sharding import PartitionSpec as P

F32 = jnp.float32
BF16 = jnp.bfloat16
MESH = pl.DeviceIdType.MESH

LEN = 1024
FULL = LEN * LEN
DET = 3
SKY = 64
HALO = 8
CELLS = 16
ZS = 8
GROUPS = 4
ROWS = 8
WIDE = 64 + 2 * HALO
COLS = CELLS * WIDE
CHUNK = 256
NCHUNK = COLS // CHUNK
SIG = 16
LANES = SIG + DET * WIDE
SCAN = 16


def section_one_table():
    cols = np.arange(COLS)
    samples = 64 * (cols // WIDE) - HALO + cols % WIDE
    angle = 2.0 * np.pi * ((np.arange(LEN)[:, None] * samples[None, :]) % LEN) / LEN
    cos = np.cos(angle).reshape(LEN, NCHUNK, CHUNK)
    sin = np.sin(angle).reshape(LEN, NCHUNK, CHUNK)
    both = np.concatenate([cos, sin], axis=2)
    return np.ascontiguousarray(np.transpose(both, (1, 0, 2))).astype(ml_dtypes.bfloat16)


def last_section_table():
    table = np.zeros((ZS, 2, 2, ROWS, 2, 8, 8, 2))
    z = np.arange(ZS)[:, None, None, None]
    r = np.arange(ROWS)[None, :, None, None]
    m = np.arange(8)[None, None, :, None]
    h = np.arange(8)[None, None, None, :]
    angle = 2.0 * np.pi * (((8 * z + r) * (8 * m + h)) % 64) / 64
    for ql in range(2):
        table[:, ql, 0, :, 0, :, :, ql] = np.cos(angle)
        table[:, ql, 1, :, 0, :, :, ql] = -np.sin(angle)
        table[:, ql, 0, :, 1, :, :, ql] = np.sin(angle)
        table[:, ql, 1, :, 1, :, :, ql] = np.cos(angle)
    return table.reshape(256, 256).astype(ml_dtypes.bfloat16)


def unit_circle(turns):
    turns = turns & (FULL - 1)
    quarter = (turns + FULL // 8) >> 18
    x = (turns - (quarter << 18)).astype(F32) * (2.0 * math.pi / FULL)
    x2 = x * x
    s = x * (1.0 + x2 * (-1.0 / 6 + x2 * (1.0 / 120 + x2 * (-1.0 / 5040 + x2 * (1.0 / 362880)))))
    c = 1.0 + x2 * (-0.5 + x2 * (1.0 / 24 + x2 * (-1.0 / 720 + x2 * (1.0 / 40320))))
    odd = (quarter & 1) == 1
    cos = jnp.where(odd, s, c)
    sin = jnp.where(odd, c, s)
    cos = jnp.where(((quarter + 1) & 2) != 0, -cos, cos)
    sin = jnp.where((quarter & 2) != 0, -sin, sin)
    return cos, sin


def dft_four(a, b, c, d):
    sr, si = a[0] + c[0], a[1] + c[1]
    dr, di = a[0] - c[0], a[1] - c[1]
    tr, ti = b[0] + d[0], b[1] + d[1]
    er, ei = b[0] - d[0], b[1] - d[1]
    return (
        (sr + tr, si + ti),
        (dr - ei, di + er),
        (sr - tr, si - ti),
        (dr + ei, di - er),
    )


def dft_sixteen(cells):
    first = [dft_four(*[cells[4 * a + b] for a in range(4)]) for b in range(4)]
    out = [None] * 16
    for k0 in range(4):
        column = []
        for b in range(4):
            xr, xi = first[b][k0]
            turn = (b * k0) % 16
            if turn:
                wr = math.cos(2 * math.pi * turn / 16)
                wi = math.sin(2 * math.pi * turn / 16)
                xr, xi = xr * wr - xi * wi, xr * wi + xi * wr
            column.append((xr, xi))
        for k1, value in enumerate(dft_four(*column)):
            out[k0 + 4 * k1] = value
    return out


def z_far_first(z):
    upper = z >= ZS // 2
    low = jnp.where(upper, ZS - 1 - z, z)
    alone = ZS - 1 - 2 * low
    places = []
    for j in range(ZS - 1):
        step = low - lax.div(jnp.maximum(j - alone, 0), 2)
        side = lax.rem(jnp.maximum(j - alone, 0), 2)
        place = jnp.where(j < alone, ZS - 1 - j, low + step - 2 * step * side)
        places.append(jnp.where(upper, ZS - 1 - place, place))
    return places


def split_two(x):
    high = x.astype(BF16).astype(F32)
    return high, x - high


def kernel(
    tmpl_hbm, strain_hbm, psd_hbm, ant_hbm, delay_hbm, tab_hbm, last_hbm,
    sky_out, peak_out,
    ant, delay, tmpl_v, strain_v, psd_v, tab_v, last_v, acc_v, twist_v, turn_v, turn2_v,
    send_xy, recv_xy, send_z, recv_z, sky_v, fin_v, pk_v, send_r, recv_r, send_p, recv_p,
    load_sem, tab_sem, s_send, s_recv, relay_v, relay_send, relay_recv, hello, ready, go, xy_send, xy_recv, z_send, z_recv, r_send, r_recv, p_send, p_recv,
):
    t = lax.axis_index("tmpl")
    g = lax.axis_index("det")
    cell = lax.div(t, ZS)
    z = lax.rem(t, ZS)

    late = lax.div(g, 2)
    near_z = z < ZS // 2
    core_g = g + 1 - 2 * lax.rem(g, 2)
    far_g = lax.rem(g + 2, GROUPS)
    diag_g = lax.rem(core_g + 2, GROUPS)
    core_id = {"tmpl": t, "det": core_g}
    far_id = {"tmpl": t, "det": far_g}
    side = 4
    offsets = sorted(
        ((a, b) for a in range(side) for b in range(side) if a or b),
        key=lambda o: -min(o[0], side - o[0]) - min(o[1], side - o[1]),
    )
    cell_x, cell_y = lax.div(cell, side), lax.rem(cell, side)
    cell_to = [lax.rem(cell_x + a, side) * side + lax.rem(cell_y + b, side) for a, b in offsets]
    xy_ids = [{"tmpl": c * ZS + z, "det": g} for c in cell_to]
    z_to = z_far_first(z)
    z_ids = [{"tmpl": cell * ZS + k, "det": g} for k in z_to]

    def signal(sem, who):
        pl.semaphore_signal(sem, inc=1, device_id=who, device_id_type=MESH)

    step = ZS // 2
    middle = jnp.logical_and(z >= step, z < step + 2)
    top = z >= step + 2
    below_top = jnp.logical_and(z >= 2, z < step)
    above_id = {"tmpl": t + step, "det": g}
    far_above_id = {"tmpl": t + step, "det": far_g}
    near_ids = [{"tmpl": cell * ZS + lax.rem(z + k, step), "det": g} for k in range(1, step)]
    barrier = pltpu.get_barrier_semaphore()

    @pl.when(late == 0)
    def _():
        @pl.when(near_z)
        def _():
            signal(barrier, far_id)
            signal(barrier, far_above_id)

        @pl.when(middle)
        def _():
            signal(barrier, far_id)

        @pl.when(top)
        def _():
            signal(barrier, {"tmpl": t - step, "det": core_g})

    signal(barrier, core_id)

    @pl.when(late == 0)
    def _():
        for who in z_ids + xy_ids:
            signal(barrier, who)

    def remote(source, target, send, recv, who):
        return pltpu.make_async_remote_copy(
            src_ref=source, dst_ref=target, send_sem=send, recv_sem=recv, device_id=who, device_id_type=MESH
        )

    to_core = remote(strain_hbm, strain_v.at[g], s_send.at[0], s_recv.at[0], core_id)
    to_far = remote(strain_hbm, strain_v.at[g], s_send.at[1], s_recv.at[1], far_id)
    down_far = remote(strain_hbm, relay_v.at[0], s_send.at[1], relay_recv.at[0], {"tmpl": t - step, "det": far_g})
    down = remote(strain_hbm, relay_v.at[1], s_send.at[1], relay_recv.at[1], {"tmpl": t - step, "det": g})
    up = remote(relay_v.at[0], strain_v.at[far_g], relay_send.at[0], s_recv.at[1], above_id)
    up_far = remote(relay_v.at[1], strain_v.at[g], relay_send.at[1], s_recv.at[1], far_above_id)
    up_other = remote(
        relay_v.at[0], strain_v.at[far_g], relay_send.at[2], s_recv.at[2], {"tmpl": t + step, "det": core_g}
    )
    handed_on = remote(strain_v.at[far_g], strain_v.at[far_g], s_send.at[2], s_recv.at[2], core_id)
    is_near = jnp.logical_and(late == 0, near_z)
    hands_on = jnp.logical_or(late == 1, z < step + 2)

    @pl.when(late == 1)
    def _():
        pl.semaphore_wait(barrier, jnp.where(middle, 3, 2))

        @pl.when(near_z)
        def _():
            to_far.start()
            signal(hello, far_id)

        @pl.when(middle)
        def _():
            to_far.start()
            signal(hello, {"tmpl": t - step, "det": far_g})

        @pl.when(top)
        def _():
            down_far.start()

        to_core.start()

    loads = [
        pltpu.make_async_copy(strain_hbm, strain_v.at[g], load_sem.at[0]),
        pltpu.make_async_copy(tmpl_hbm, tmpl_v, load_sem.at[1]),
        pltpu.make_async_copy(psd_hbm, psd_v, load_sem.at[2]),
        pltpu.make_async_copy(last_hbm, last_v, load_sem.at[3]),
        pltpu.make_async_copy(ant_hbm, ant, load_sem.at[4]),
        pltpu.make_async_copy(delay_hbm, delay, load_sem.at[5]),
    ]
    tab_loads = [pltpu.make_async_copy(tab_hbm.at[n], tab_v.at[n], tab_sem.at[n]) for n in range(NCHUNK)]
    for copy in loads + tab_loads:
        copy.start()

    row = lax.broadcasted_iota(jnp.int32, (ROWS, COLS), 0)
    col = lax.broadcasted_iota(jnp.int32, (ROWS, COLS), 1)
    sample = col - 2 * HALO * ((col * 52429) >> 22) - HALO
    cos, sin = unit_circle((t * ROWS + row) * sample)
    turn_v[0] = cos
    turn_v[1] = sin
    row = lax.broadcasted_iota(jnp.int32, (ROWS, 128), 0)
    for q in range(16):
        cos, sin = unit_circle((z * ROWS + row) * (q * LEN))
        turn2_v[0, q] = cos
        turn2_v[1, q] = sin

    for copy in loads[1:3]:
        copy.wait()
    both = tmpl_v[...].astype(F32)
    tr, ti = both[:ROWS], both[ROWS:]
    square = tr * tr + ti * ti
    parts = [
        split_two(jnp.sum(square * psd_v[ROWS * d : ROWS * d + ROWS, :], axis=1, keepdims=True))
        for d in range(DET)
    ]
    blank = jnp.zeros((ROWS, SIG - DET), F32)
    sig = [jnp.concatenate([parts[d][c] for d in range(DET)] + [blank], axis=1) for c in range(2)]

    loads[4].wait()
    loads[5].wait()
    distance = lax.broadcasted_iota(jnp.int32, (64, 256), 1) - lax.broadcasted_iota(jnp.int32, (64, 256), 0)

    def weigh(s, carry):
        weights = jnp.zeros((64, 256), F32)
        for d in range(DET):
            weights = jnp.where(distance == SIG + WIDE * d + HALO + delay[d, s], ant[d, s], weights)
        sky_v[pl.ds(pl.multiple_of(64 * s, 64), 64), :] = weights.astype(BF16)
        return carry

    lax.fori_loop(0, SKY, weigh, 0)

    half = DET * ROWS
    for order, piece in enumerate([g, core_g, far_g, diag_g]):
        if order == 0:
            loads[0].wait()
            for copy in tab_loads:
                copy.wait()
        elif order == 1:

            @pl.when(late == 0)
            def _():
                pl.semaphore_wait(barrier, 1 + (ZS - 1) + (CELLS - 1) + jnp.where(below_top, 1, 0))

                @pl.when(near_z)
                def _():
                    @pl.when(below_top)
                    def _():
                        down_far.wait_recv()
                        up.start()
                        up_other.start()

                    to_core.start()
                    pl.semaphore_wait(hello, jnp.where(below_top, 1, 2))
                    to_far.start()
                    for who in near_ids + xy_ids:
                        signal(ready, who)

                @pl.when(jnp.logical_not(near_z))
                def _():
                    down.start()
                    to_core.start()

            to_core.wait_recv()
        elif order == 2:
            to_far.wait_recv()

            @pl.when(hands_on)
            def _():
                handed_on.start()

        else:
            handed_on.wait_recv()
        lanes = pl.ds(pl.multiple_of(CHUNK * piece, CHUNK), CHUNK)
        data = strain_v[piece].astype(F32)
        both = tmpl_v[:, lanes].astype(F32)
        trl, til = both[:ROWS], both[ROWS:]
        real, imag = [], []
        for d in range(DET):
            dr = data[ROWS * d : ROWS * d + ROWS]
            di = data[ROWS * (DET + d) : ROWS * (DET + d) + ROWS]
            weight = psd_v[ROWS * d : ROWS * d + ROWS, lanes]
            real.append((trl * dr + til * di) * weight)
            imag.append((trl * di - til * dr) * weight)
        product = jnp.concatenate(real + imag, axis=0).astype(BF16)
        for n in range(NCHUNK):
            out = jnp.dot(product, tab_v[n, lanes, :], preferred_element_type=F32)
            if order:
                out = out + acc_v[n]
            if order < GROUPS - 1:
                acc_v[n] = out
                continue
            sec_r = out[:half, :CHUNK] - out[half:, CHUNK:]
            sec_i = out[:half, CHUNK:] + out[half:, :CHUNK]
            cols = slice(CHUNK * n, CHUNK * n + CHUNK)
            cos, sin = turn_v[0, :, cols], turn_v[1, :, cols]
            for d in range(DET):
                rows = slice(ROWS * d, ROWS * d + ROWS)
                twist_v[0, rows, cols] = sec_r[rows] * cos - sec_i[rows] * sin
                twist_v[1, rows, cols] = sec_r[rows] * sin + sec_i[rows] * cos

    for c in range(CELLS):
        lanes = slice(WIDE * c, WIDE * c + WIDE)
        block = jnp.concatenate(
            [
                jnp.concatenate(
                    [sig[i]] + [twist_v[i, ROWS * d : ROWS * d + ROWS, lanes] for d in range(DET)], axis=1
                )
                for i in range(2)
            ],
            axis=0,
        ).astype(BF16)
        send_xy[0, c] = block[:, :128]
        send_xy[1, c] = block[:, 128:]

    @pl.when(late == 1)
    def _():
        pl.semaphore_wait(go, 1)

    xy_copies = [
        remote(send_xy.at[:, cell_to[k]], recv_xy.at[:, cell], xy_send.at[k], xy_recv.at[k], xy_ids[k])
        for k in range(CELLS - 1)
    ]
    for copy in xy_copies:
        copy.start()
    recv_xy[:, cell] = send_xy[:, cell]

    @pl.when(is_near)
    def _():
        down.wait_recv()
        up_far.start()
        pl.semaphore_wait(ready, (step - 1) + (CELLS - 1))
        signal(go, far_id)
        signal(go, far_above_id)

    lane = lax.broadcasted_iota(jnp.int32, (ROWS, 128), 1)
    for copy in xy_copies:
        copy.wait_recv()
    for part in range(2):
        cells = []
        for c in range(CELLS):
            value = recv_xy[part, c].astype(F32)
            cells.append((value[:ROWS], value[ROWS:]))
        bins = dft_sixteen(cells)
        if part == 0:
            high, low = split_two(bins[0][0] + bins[0][1])
        for q in range(16):
            xr, xi = bins[q]
            cos, sin = turn2_v[0, q], turn2_v[1, q]
            yr, yi = xr * cos - xi * sin, xr * sin + xi * cos
            if part == 0:
                yr = jnp.where(lane < SIG, high, yr)
                yi = jnp.where(lane < SIG, low, yi)
            send_z[part, q] = jnp.concatenate([yr, yi], axis=0).astype(BF16)
    z_copies = [
        remote(send_z.at[:, pl.ds(2 * z_to[k], 2)], recv_z.at[:, z], z_send.at[k], z_recv.at[z], z_ids[k])
        for k in range(ZS - 1)
    ]
    for copy in z_copies:
        copy.start()
    recv_z[:, z] = send_z[:, pl.ds(2 * z, 2)]

    scales = None
    for k in z_to:
        pltpu.make_async_copy(recv_z.at[:, k], recv_z.at[:, k], z_recv.at[k]).wait()
    for part in range(2):
        got = recv_z[part].reshape(256, 128)
        if part == 0:
            halves = recv_z[part, :, 0].astype(F32)
            total = jnp.sum(jnp.sum(halves, axis=0), axis=0, keepdims=True)
            scales = [1.0 / jnp.sqrt(total[:, d : d + 1]) for d in range(DET)]
        out = lax.dot_general(got, last_v[...] if part else _wait_load(loads[3], last_v), (((0,), (0,)), ((), ())), preferred_element_type=F32)
        for d in range(DET):
            low_row = max(SIG + WIDE * d, 128 * part)
            high_row = min(SIG + WIDE * (d + 1), 128 * part + 128)
            if low_row < high_row:
                block = out[low_row - 128 * part : high_row - 128 * part]
                fin_v[low_row:high_row, :] = (block * scales[d]).astype(BF16)

    fin_v[:SIG, :] = jnp.zeros((SIG, 256), BF16)
    detectors = fin_v[...]
    best = jnp.zeros((64, 128), F32)
    for first in range(0, SKY, SCAN):
        both = jnp.dot(sky_v[64 * first : 64 * (first + SCAN), :], detectors, preferred_element_type=F32)
        real, imag = both[:, :128], both[:, 128:]
        power = (real * real + imag * imag).reshape(SCAN, 64, 128)
        pk_v[first : first + SCAN] = jnp.max(power.reshape(SCAN, 8, 8, 128), axis=1)
        best = jnp.maximum(best, jnp.max(power, axis=0))

    tops = jnp.max(pk_v[...], axis=1)
    tops = jnp.max(jnp.transpose(tops), axis=0, keepdims=True)
    tops = jnp.concatenate([tops, jnp.zeros((1, 128 - SKY), F32)], axis=1)
    send_p[...] = jnp.broadcast_to(tops, (8, 128))
    others = CELLS * ZS - 1

    own = jnp.where(late == 0, z, ZS - 1 - z) * CELLS + cell

    def tell(k, carry):
        turn = k + jnp.where(k >= own, 1, 0)
        place = lax.div(turn, CELLS)
        place = jnp.where(late == 0, place, ZS - 1 - place)
        who = {"tmpl": lax.rem(turn, CELLS) * ZS + place, "det": g}
        remote(send_p.at[pl.ds(0, 1)], recv_p.at[pl.ds(t, 1)], p_send, p_recv, who).start()
        return carry

    lax.fori_loop(0, others, tell, 0)
    recv_p[pl.ds(t, 1), :] = tops

    for k in range(ZS):
        send_r[k] = best[8 * k : 8 * k + 8]
    r_copies = [
        remote(send_r.at[z_to[k]], recv_r.at[z], r_send.at[k], r_recv.at[z], z_ids[k]) for k in range(ZS - 1)
    ]
    for copy in r_copies:
        copy.start()
    recv_r[z] = send_r[z]

    for k in z_to:
        pltpu.make_async_copy(recv_r.at[k], recv_r.at[k], r_recv.at[k]).wait()
    lane = lax.broadcasted_iota(jnp.int32, (8, 128), 1)
    owner = (lane >> 1) & 7
    for m in range(8):
        index = 16 * m + 2 * (lane >> 4) + (lane & 1)
        acc = jnp.zeros((8, 128), F32)
        for k in range(ZS):
            moved = jnp.take_along_axis(recv_r[k], index, axis=1, mode="promise_in_bounds")
            acc = jnp.where(owner == k, moved, acc)
        sky_out[:, 128 * m : 128 * m + 128] = acc

    rows = pl.ds(0, others)
    pltpu.make_async_copy(recv_p.at[rows], recv_p.at[rows], p_recv).wait()
    peak_out[...] = jnp.max(recv_p[...], axis=0, keepdims=True)[:, :SKY]

    for copy in (to_core, to_far):
        copy.wait_send()

    @pl.when(hands_on)
    def _():
        handed_on.wait_send()

    @pl.when(is_near)
    def _():
        up_far.wait_send()

        @pl.when(below_top)
        def _():
            up.wait_send()
            up_other.wait_send()

    for copy in xy_copies + z_copies + r_copies:
        copy.wait_send()
    pltpu.make_async_copy(recv_p.at[rows], recv_p.at[rows], p_send).wait()


def _wait_load(copy, ref):
    copy.wait()
    return ref[...]


def hand_over(sky_in, peak_in, sky_out, peak_out, sem):
    copies = [pltpu.make_async_copy(sky_in, sky_out, sem.at[0]), pltpu.make_async_copy(peak_in, peak_out, sem.at[1])]
    for copy in copies:
        copy.start()
    for copy in copies:
        copy.wait()


def shards(templates, strain, inverse_psd, antenna, delays):
    tab = jnp.asarray(section_one_table())
    last = jnp.asarray(last_section_table())
    hbm = pl.BlockSpec(memory_space=pltpu.HBM)
    anywhere = pl.BlockSpec(memory_space=pl.ANY)
    vmem = pl.BlockSpec(memory_space=pltpu.VMEM)
    dma = pltpu.SemaphoreType.DMA
    regular = pltpu.SemaphoreType.REGULAR
    sky, peak = pl.pallas_call(
        kernel,
        out_shape=(pltpu.VMEM((8, LEN), F32), pltpu.VMEM((1, SKY), F32)),
        in_specs=[hbm] * 7,
        out_specs=(vmem, vmem),
        scratch_shapes=[
            pltpu.SMEM((DET, SKY), F32),
            pltpu.SMEM((DET, SKY), jnp.int32),
            pltpu.VMEM((16, LEN), BF16),
            pltpu.VMEM((GROUPS, 48, CHUNK), BF16),
            pltpu.VMEM((24, LEN), F32),
            pltpu.VMEM((NCHUNK, LEN, 2 * CHUNK), BF16),
            pltpu.VMEM((256, 256), BF16),
            pltpu.VMEM((NCHUNK, 48, 2 * CHUNK), F32),
            pltpu.VMEM((2, 24, COLS), F32),
            pltpu.VMEM((2, ROWS, COLS), F32),
            pltpu.VMEM((2, 16, ROWS, 128), F32),
            pltpu.VMEM((2, CELLS, 16, 128), BF16),
            pltpu.VMEM((2, CELLS, 16, 128), BF16),
            pltpu.VMEM((2, 16, 16, 128), BF16),
            pltpu.VMEM((2, ZS, 2, 16, 128), BF16),
            pltpu.VMEM((SKY * 64, 256), BF16),
            pltpu.VMEM((256, 256), BF16),
            pltpu.VMEM((SKY, 8, 128), F32),
            pltpu.VMEM((ZS, 8, 128), F32),
            pltpu.VMEM((ZS, 8, 128), F32),
            pltpu.VMEM((8, 128), F32),
            pltpu.VMEM((CELLS * ZS, 128), F32),
            dma((6,)), dma((NCHUNK,)),
            dma((GROUPS - 1,)), dma((GROUPS - 1,)),
            pltpu.VMEM((2, 48, CHUNK), BF16),
            dma((3,)), dma((2,)),
            regular, regular, regular,
            dma((CELLS - 1,)), dma((CELLS - 1,)),
            dma((ZS - 1,)), dma((ZS,)),
            dma((ZS - 1,)), dma((ZS,)),
            dma, dma,
        ],
        compiler_params=pltpu.CompilerParams(
            collective_id=0, has_side_effects=True, vmem_limit_bytes=56 * 1024 * 1024
        ),
        cost_estimate=pl.CostEstimate(flops=400_000_000, bytes_accessed=6_000_000, transcendentals=0),
    )(
        templates.reshape(16, LEN),
        strain.reshape(48, CHUNK),
        inverse_psd.reshape(24, LEN),
        antenna,
        delays,
        tab,
        last,
    )
    sky, peak = pl.pallas_call(
        hand_over,
        out_shape=(jax.ShapeDtypeStruct((8, LEN), F32), jax.ShapeDtypeStruct((1, SKY), F32)),
        in_specs=[anywhere, anywhere],
        out_specs=(anywhere, anywhere),
        scratch_shapes=[dma((2,))],
        compiler_params=pltpu.CompilerParams(vmem_limit_bytes=1024 * 1024),
    )(sky, peak)
    return (sky[None], peak)


def solution(mesh):
    return jax.shard_map(
        shards,
        mesh=mesh,
        in_specs=(
            P(None, "det", "tmpl", None),
            P(None, None, "tmpl", "det"),
            P(None, "tmpl", None),
            P(),
            P(),
        ),
        out_specs=(P("det", "tmpl", None), P("det", None)),
        check_vma=False,
    )
```

```python
import math

import jax
import jax.numpy as jnp
import ml_dtypes
import numpy as np
from jax import lax
from jax.experimental import pallas as pl
from jax.experimental.pallas import tpu as pltpu
from jax.sharding import PartitionSpec as P

F32 = jnp.float32
BF16 = jnp.bfloat16
MESH = pl.DeviceIdType.MESH

LEN = 1024
FULL = LEN * LEN
DET = 3
SKY = 64
HALO = 8
CELLS = 16
ZS = 8
GROUPS = 4
ROWS = 8
WIDE = 64 + 2 * HALO
COLS = CELLS * WIDE
CHUNK = 256
NCHUNK = COLS // CHUNK
SIG = 16
LANES = SIG + DET * WIDE
SCAN = 16


def section_one_table():
    cols = np.arange(COLS)
    samples = 64 * (cols // WIDE) - HALO + cols % WIDE
    angle = 2.0 * np.pi * ((np.arange(LEN)[:, None] * samples[None, :]) % LEN) / LEN
    cos = np.cos(angle).reshape(LEN, NCHUNK, CHUNK)
    sin = np.sin(angle).reshape(LEN, NCHUNK, CHUNK)
    both = np.concatenate([cos, sin], axis=2)
    return np.ascontiguousarray(np.transpose(both, (1, 0, 2))).astype(ml_dtypes.bfloat16)


def last_section_table():
    table = np.zeros((ZS, 2, 2, ROWS, 2, 8, 8, 2))
    z = np.arange(ZS)[:, None, None, None]
    r = np.arange(ROWS)[None, :, None, None]
    m = np.arange(8)[None, None, :, None]
    h = np.arange(8)[None, None, None, :]
    angle = 2.0 * np.pi * (((8 * z + r) * (8 * m + h)) % 64) / 64
    for ql in range(2):
        table[:, ql, 0, :, 0, :, :, ql] = np.cos(angle)
        table[:, ql, 1, :, 0, :, :, ql] = -np.sin(angle)
        table[:, ql, 0, :, 1, :, :, ql] = np.sin(angle)
        table[:, ql, 1, :, 1, :, :, ql] = np.cos(angle)
    return table.reshape(256, 256).astype(ml_dtypes.bfloat16)


def unit_circle(turns):
    turns = turns & (FULL - 1)
    quarter = (turns + FULL // 8) >> 18
    x = (turns - (quarter << 18)).astype(F32) * (2.0 * math.pi / FULL)
    x2 = x * x
    s = x * (1.0 + x2 * (-1.0 / 6 + x2 * (1.0 / 120 + x2 * (-1.0 / 5040 + x2 * (1.0 / 362880)))))
    c = 1.0 + x2 * (-0.5 + x2 * (1.0 / 24 + x2 * (-1.0 / 720 + x2 * (1.0 / 40320))))
    odd = (quarter & 1) == 1
    cos = jnp.where(odd, s, c)
    sin = jnp.where(odd, c, s)
    cos = jnp.where(((quarter + 1) & 2) != 0, -cos, cos)
    sin = jnp.where((quarter & 2) != 0, -sin, sin)
    return cos, sin


def dft_four(a, b, c, d):
    sr, si = a[0] + c[0], a[1] + c[1]
    dr, di = a[0] - c[0], a[1] - c[1]
    tr, ti = b[0] + d[0], b[1] + d[1]
    er, ei = b[0] - d[0], b[1] - d[1]
    return (
        (sr + tr, si + ti),
        (dr - ei, di + er),
        (sr - tr, si - ti),
        (dr + ei, di - er),
    )


def dft_sixteen(cells):
    first = [dft_four(*[cells[4 * a + b] for a in range(4)]) for b in range(4)]
    out = [None] * 16
    for k0 in range(4):
        column = []
        for b in range(4):
            xr, xi = first[b][k0]
            turn = (b * k0) % 16
            if turn:
                wr = math.cos(2 * math.pi * turn / 16)
                wi = math.sin(2 * math.pi * turn / 16)
                xr, xi = xr * wr - xi * wi, xr * wi + xi * wr
            column.append((xr, xi))
        for k1, value in enumerate(dft_four(*column)):
            out[k0 + 4 * k1] = value
    return out


def z_far_first(z):
    upper = z >= ZS // 2
    low = jnp.where(upper, ZS - 1 - z, z)
    alone = ZS - 1 - 2 * low
    places = []
    for j in range(ZS - 1):
        step = low - lax.div(jnp.maximum(j - alone, 0), 2)
        side = lax.rem(jnp.maximum(j - alone, 0), 2)
        place = jnp.where(j < alone, ZS - 1 - j, low + step - 2 * step * side)
        places.append(jnp.where(upper, ZS - 1 - place, place))
    return places


def split_two(x):
    high = x.astype(BF16).astype(F32)
    return high, x - high


def kernel(
    tmpl_hbm, strain_hbm, psd_hbm, ant_hbm, delay_hbm, tab_hbm, last_hbm,
    sky_out, peak_out,
    ant, delay, tmpl_v, strain_v, psd_v, tab_v, last_v, acc_v, twist_v, turn_v, turn2_v,
    send_xy, recv_xy, send_z, recv_z, sky_v, fin_v, pk_v, send_r, recv_r, send_p, recv_p,
    load_sem, tab_sem, s_send, s_recv, relay_v, relay_send, relay_recv, hello, ready, go, xy_send, xy_recv, z_send, z_recv, r_send, r_recv, p_send, p_recv,
):
    t = lax.axis_index("tmpl")
    g = lax.axis_index("det")
    cell = lax.div(t, ZS)
    z = lax.rem(t, ZS)

    late = lax.div(g, 2)
    near_z = z < ZS // 2
    core_g = g + 1 - 2 * lax.rem(g, 2)
    far_g = lax.rem(g + 2, GROUPS)
    diag_g = lax.rem(core_g + 2, GROUPS)
    core_id = {"tmpl": t, "det": core_g}
    far_id = {"tmpl": t, "det": far_g}
    side = 4
    offsets = sorted(
        ((a, b) for a in range(side) for b in range(side) if a or b),
        key=lambda o: -min(o[0], side - o[0]) - min(o[1], side - o[1]),
    )
    cell_x, cell_y = lax.div(cell, side), lax.rem(cell, side)
    cell_to = [lax.rem(cell_x + a, side) * side + lax.rem(cell_y + b, side) for a, b in offsets]
    xy_ids = [{"tmpl": c * ZS + z, "det": g} for c in cell_to]
    z_to = z_far_first(z)
    z_ids = [{"tmpl": cell * ZS + k, "det": g} for k in z_to]

    def signal(sem, who):
        pl.semaphore_signal(sem, inc=1, device_id=who, device_id_type=MESH)

    step = ZS // 2
    middle = jnp.logical_and(z >= step, z < step + 2)
    top = z >= step + 2
    below_top = jnp.logical_and(z >= 2, z < step)
    above_id = {"tmpl": t + step, "det": g}
    far_above_id = {"tmpl": t + step, "det": far_g}
    near_ids = [{"tmpl": cell * ZS + lax.rem(z + k, step), "det": g} for k in range(1, step)]
    barrier = pltpu.get_barrier_semaphore()

    @pl.when(late == 0)
    def _():
        @pl.when(near_z)
        def _():
            signal(barrier, far_id)
            signal(barrier, far_above_id)

        @pl.when(middle)
        def _():
            signal(barrier, far_id)

        @pl.when(top)
        def _():
            signal(barrier, {"tmpl": t - step, "det": core_g})

    signal(barrier, core_id)

    @pl.when(late == 0)
    def _():
        for who in z_ids + xy_ids:
            signal(barrier, who)

    def remote(source, target, send, recv, who):
        return pltpu.make_async_remote_copy(
            src_ref=source, dst_ref=target, send_sem=send, recv_sem=recv, device_id=who, device_id_type=MESH
        )

    to_core = remote(strain_hbm, strain_v.at[g], s_send.at[0], s_recv.at[0], core_id)
    to_far = remote(strain_hbm, strain_v.at[g], s_send.at[1], s_recv.at[1], far_id)
    down_far = remote(strain_hbm, relay_v.at[0], s_send.at[1], relay_recv.at[0], {"tmpl": t - step, "det": far_g})
    down = remote(strain_hbm, relay_v.at[1], s_send.at[1], relay_recv.at[1], {"tmpl": t - step, "det": g})
    up = remote(relay_v.at[0], strain_v.at[far_g], relay_send.at[0], s_recv.at[1], above_id)
    up_far = remote(relay_v.at[1], strain_v.at[g], relay_send.at[1], s_recv.at[1], far_above_id)
    up_other = remote(
        relay_v.at[0], strain_v.at[far_g], relay_send.at[2], s_recv.at[2], {"tmpl": t + step, "det": core_g}
    )
    handed_on = remote(strain_v.at[far_g], strain_v.at[far_g], s_send.at[2], s_recv.at[2], core_id)
    is_near = jnp.logical_and(late == 0, near_z)
    hands_on = jnp.logical_or(late == 1, z < step + 2)

    @pl.when(late == 1)
    def _():
        pl.semaphore_wait(barrier, jnp.where(middle, 3, 2))

        @pl.when(near_z)
        def _():
            to_far.start()
            signal(hello, far_id)

        @pl.when(middle)
        def _():
            to_far.start()
            signal(hello, {"tmpl": t - step, "det": far_g})

        @pl.when(top)
        def _():
            down_far.start()

        to_core.start()

    loads = [
        pltpu.make_async_copy(strain_hbm, strain_v.at[g], load_sem.at[0]),
        pltpu.make_async_copy(tmpl_hbm, tmpl_v, load_sem.at[1]),
        pltpu.make_async_copy(psd_hbm, psd_v, load_sem.at[2]),
        pltpu.make_async_copy(last_hbm, last_v, load_sem.at[3]),
        pltpu.make_async_copy(ant_hbm, ant, load_sem.at[4]),
        pltpu.make_async_copy(delay_hbm, delay, load_sem.at[5]),
    ]
    tab_loads = [pltpu.make_async_copy(tab_hbm.at[n], tab_v.at[n], tab_sem.at[n]) for n in range(NCHUNK)]
    for copy in loads + tab_loads:
        copy.start()

    row = lax.broadcasted_iota(jnp.int32, (ROWS, COLS), 0)
    col = lax.broadcasted_iota(jnp.int32, (ROWS, COLS), 1)
    sample = col - 2 * HALO * ((col * 52429) >> 22) - HALO
    cos, sin = unit_circle((t * ROWS + row) * sample)
    turn_v[0] = cos
    turn_v[1] = sin
    row = lax.broadcasted_iota(jnp.int32, (ROWS, 128), 0)
    for q in range(16):
        cos, sin = unit_circle((z * ROWS + row) * (q * LEN))
        turn2_v[0, q] = cos
        turn2_v[1, q] = sin

    for copy in loads[1:3]:
        copy.wait()
    both = tmpl_v[...].astype(F32)
    tr, ti = both[:ROWS], both[ROWS:]
    square = tr * tr + ti * ti
    parts = [
        split_two(jnp.sum(square * psd_v[ROWS * d : ROWS * d + ROWS, :], axis=1, keepdims=True))
        for d in range(DET)
    ]
    blank = jnp.zeros((ROWS, SIG - DET), F32)
    sig = [jnp.concatenate([parts[d][c] for d in range(DET)] + [blank], axis=1) for c in range(2)]

    loads[4].wait()
    loads[5].wait()
    distance = lax.broadcasted_iota(jnp.int32, (64, 256), 1) - lax.broadcasted_iota(jnp.int32, (64, 256), 0)

    def weigh(s, carry):
        weights = jnp.zeros((64, 256), F32)
        for d in range(DET):
            weights = jnp.where(distance == SIG + WIDE * d + HALO + delay[d, s], ant[d, s], weights)
        high, low = split_two(weights)
        rows = pl.ds(pl.multiple_of(64 * s, 64), 64)
        sky_v[rows, :256] = high.astype(BF16)
        sky_v[rows, 256:] = low.astype(BF16)
        return carry

    lax.fori_loop(0, SKY, weigh, 0)

    half = DET * ROWS
    for order, piece in enumerate([g, core_g, far_g, diag_g]):
        if order == 0:
            loads[0].wait()
            for copy in tab_loads:
                copy.wait()
        elif order == 1:

            @pl.when(late == 0)
            def _():
                pl.semaphore_wait(barrier, 1 + (ZS - 1) + (CELLS - 1) + jnp.where(below_top, 1, 0))

                @pl.when(near_z)
                def _():
                    @pl.when(below_top)
                    def _():
                        down_far.wait_recv()
                        up.start()
                        up_other.start()

                    to_core.start()
                    pl.semaphore_wait(hello, jnp.where(below_top, 1, 2))
                    to_far.start()
                    for who in near_ids + xy_ids:
                        signal(ready, who)

                @pl.when(jnp.logical_not(near_z))
                def _():
                    down.start()
                    to_core.start()

            to_core.wait_recv()
        elif order == 2:
            to_far.wait_recv()

            @pl.when(hands_on)
            def _():
                handed_on.start()

        else:
            handed_on.wait_recv()
        lanes = pl.ds(pl.multiple_of(CHUNK * piece, CHUNK), CHUNK)
        data = strain_v[piece].astype(F32)
        both = tmpl_v[:, lanes].astype(F32)
        trl, til = both[:ROWS], both[ROWS:]
        real, imag = [], []
        for d in range(DET):
            dr = data[ROWS * d : ROWS * d + ROWS]
            di = data[ROWS * (DET + d) : ROWS * (DET + d) + ROWS]
            weight = psd_v[ROWS * d : ROWS * d + ROWS, lanes]
            real.append((trl * dr + til * di) * weight)
            imag.append((trl * di - til * dr) * weight)
        product = jnp.concatenate(real + imag, axis=0).astype(BF16)
        for n in range(NCHUNK):
            out = jnp.dot(product, tab_v[n, lanes, :], preferred_element_type=F32)
            if order:
                out = out + acc_v[n]
            if order < GROUPS - 1:
                acc_v[n] = out
                continue
            sec_r = out[:half, :CHUNK] - out[half:, CHUNK:]
            sec_i = out[:half, CHUNK:] + out[half:, :CHUNK]
            cols = slice(CHUNK * n, CHUNK * n + CHUNK)
            cos, sin = turn_v[0, :, cols], turn_v[1, :, cols]
            for d in range(DET):
                rows = slice(ROWS * d, ROWS * d + ROWS)
                twist_v[0, rows, cols] = sec_r[rows] * cos - sec_i[rows] * sin
                twist_v[1, rows, cols] = sec_r[rows] * sin + sec_i[rows] * cos

    for c in range(CELLS):
        lanes = slice(WIDE * c, WIDE * c + WIDE)
        block = jnp.concatenate(
            [
                jnp.concatenate(
                    [sig[i]] + [twist_v[i, ROWS * d : ROWS * d + ROWS, lanes] for d in range(DET)], axis=1
                )
                for i in range(2)
            ],
            axis=0,
        ).astype(BF16)
        send_xy[0, c] = block[:, :128]
        send_xy[1, c] = block[:, 128:]

    @pl.when(late == 1)
    def _():
        pl.semaphore_wait(go, 1)

    xy_copies = [
        remote(send_xy.at[:, cell_to[k]], recv_xy.at[:, cell], xy_send.at[k], xy_recv.at[k], xy_ids[k])
        for k in range(CELLS - 1)
    ]
    for copy in xy_copies:
        copy.start()
    recv_xy[:, cell] = send_xy[:, cell]

    @pl.when(is_near)
    def _():
        down.wait_recv()
        up_far.start()
        pl.semaphore_wait(ready, (step - 1) + (CELLS - 1))
        signal(go, far_id)
        signal(go, far_above_id)

    lane = lax.broadcasted_iota(jnp.int32, (ROWS, 128), 1)
    for copy in xy_copies:
        copy.wait_recv()
    for part in range(2):
        cells = []
        for c in range(CELLS):
            value = recv_xy[part, c].astype(F32)
            cells.append((value[:ROWS], value[ROWS:]))
        bins = dft_sixteen(cells)
        if part == 0:
            high, low = split_two(bins[0][0] + bins[0][1])
        for q in range(16):
            xr, xi = bins[q]
            cos, sin = turn2_v[0, q], turn2_v[1, q]
            yr, yi = xr * cos - xi * sin, xr * sin + xi * cos
            if part == 0:
                yr = jnp.where(lane < SIG, high, yr)
                yi = jnp.where(lane < SIG, low, yi)
            send_z[part, q] = jnp.concatenate([yr, yi], axis=0).astype(BF16)
    z_copies = [
        remote(send_z.at[:, pl.ds(2 * z_to[k], 2)], recv_z.at[:, z], z_send.at[k], z_recv.at[z], z_ids[k])
        for k in range(ZS - 1)
    ]
    for copy in z_copies:
        copy.start()
    recv_z[:, z] = send_z[:, pl.ds(2 * z, 2)]

    scales = None
    for k in z_to:
        pltpu.make_async_copy(recv_z.at[:, k], recv_z.at[:, k], z_recv.at[k]).wait()
    for part in range(2):
        got = recv_z[part].reshape(256, 128)
        if part == 0:
            halves = recv_z[part, :, 0].astype(F32)
            total = jnp.sum(jnp.sum(halves, axis=0), axis=0, keepdims=True)
            scales = [1.0 / jnp.sqrt(total[:, d : d + 1]) for d in range(DET)]
        out = lax.dot_general(got, last_v[...] if part else _wait_load(loads[3], last_v), (((0,), (0,)), ((), ())), preferred_element_type=F32)
        for d in range(DET):
            low_row = max(SIG + WIDE * d, 128 * part)
            high_row = min(SIG + WIDE * (d + 1), 128 * part + 128)
            if low_row < high_row:
                block = out[low_row - 128 * part : high_row - 128 * part]
                fin_v[low_row:high_row, :] = (block * scales[d]).astype(BF16)

    fin_v[:SIG, :] = jnp.zeros((SIG, 256), BF16)
    detectors = fin_v[...]
    best = jnp.zeros((64, 128), F32)
    for first in range(0, SKY, SCAN):
        rows = slice(64 * first, 64 * (first + SCAN))
        both = jnp.dot(sky_v[rows, :256], detectors, preferred_element_type=F32)
        both = both + jnp.dot(sky_v[rows, 256:], detectors, preferred_element_type=F32)
        real, imag = both[:, :128], both[:, 128:]
        power = (real * real + imag * imag).reshape(SCAN, 64, 128)
        pk_v[first : first + SCAN] = jnp.max(power.reshape(SCAN, 8, 8, 128), axis=1)
        best = jnp.maximum(best, jnp.max(power, axis=0))

    tops = jnp.max(pk_v[...], axis=1)
    tops = jnp.max(jnp.transpose(tops), axis=0, keepdims=True)
    tops = jnp.concatenate([tops, jnp.zeros((1, 128 - SKY), F32)], axis=1)
    send_p[...] = jnp.broadcast_to(tops, (8, 128))
    others = CELLS * ZS - 1

    own = jnp.where(late == 0, z, ZS - 1 - z) * CELLS + cell

    def tell(k, carry):
        turn = k + jnp.where(k >= own, 1, 0)
        place = lax.div(turn, CELLS)
        place = jnp.where(late == 0, place, ZS - 1 - place)
        who = {"tmpl": lax.rem(turn, CELLS) * ZS + place, "det": g}
        remote(send_p.at[pl.ds(0, 1)], recv_p.at[pl.ds(t, 1)], p_send, p_recv, who).start()
        return carry

    lax.fori_loop(0, others, tell, 0)
    recv_p[pl.ds(t, 1), :] = tops

    for k in range(ZS):
        send_r[k] = best[8 * k : 8 * k + 8]
    r_copies = [
        remote(send_r.at[z_to[k]], recv_r.at[z], r_send.at[k], r_recv.at[z], z_ids[k]) for k in range(ZS - 1)
    ]
    for copy in r_copies:
        copy.start()
    recv_r[z] = send_r[z]

    for k in z_to:
        pltpu.make_async_copy(recv_r.at[k], recv_r.at[k], r_recv.at[k]).wait()
    lane = lax.broadcasted_iota(jnp.int32, (8, 128), 1)
    owner = (lane >> 1) & 7
    for m in range(8):
        index = 16 * m + 2 * (lane >> 4) + (lane & 1)
        acc = jnp.zeros((8, 128), F32)
        for k in range(ZS):
            moved = jnp.take_along_axis(recv_r[k], index, axis=1, mode="promise_in_bounds")
            acc = jnp.where(owner == k, moved, acc)
        sky_out[:, 128 * m : 128 * m + 128] = acc

    rows = pl.ds(0, others)
    pltpu.make_async_copy(recv_p.at[rows], recv_p.at[rows], p_recv).wait()
    peak_out[...] = jnp.max(recv_p[...], axis=0, keepdims=True)[:, :SKY]

    for copy in (to_core, to_far):
        copy.wait_send()

    @pl.when(hands_on)
    def _():
        handed_on.wait_send()

    @pl.when(is_near)
    def _():
        up_far.wait_send()

        @pl.when(below_top)
        def _():
            up.wait_send()
            up_other.wait_send()

    for copy in xy_copies + z_copies + r_copies:
        copy.wait_send()
    pltpu.make_async_copy(recv_p.at[rows], recv_p.at[rows], p_send).wait()


def _wait_load(copy, ref):
    copy.wait()
    return ref[...]


def hand_over(sky_in, peak_in, sky_out, peak_out, sem):
    copies = [pltpu.make_async_copy(sky_in, sky_out, sem.at[0]), pltpu.make_async_copy(peak_in, peak_out, sem.at[1])]
    for copy in copies:
        copy.start()
    for copy in copies:
        copy.wait()


def shards(templates, strain, inverse_psd, antenna, delays):
    tab = jnp.asarray(section_one_table())
    last = jnp.asarray(last_section_table())
    hbm = pl.BlockSpec(memory_space=pltpu.HBM)
    anywhere = pl.BlockSpec(memory_space=pl.ANY)
    vmem = pl.BlockSpec(memory_space=pltpu.VMEM)
    dma = pltpu.SemaphoreType.DMA
    regular = pltpu.SemaphoreType.REGULAR
    sky, peak = pl.pallas_call(
        kernel,
        out_shape=(pltpu.VMEM((8, LEN), F32), pltpu.VMEM((1, SKY), F32)),
        in_specs=[hbm] * 7,
        out_specs=(vmem, vmem),
        scratch_shapes=[
            pltpu.SMEM((DET, SKY), F32),
            pltpu.SMEM((DET, SKY), jnp.int32),
            pltpu.VMEM((16, LEN), BF16),
            pltpu.VMEM((GROUPS, 48, CHUNK), BF16),
            pltpu.VMEM((24, LEN), F32),
            pltpu.VMEM((NCHUNK, LEN, 2 * CHUNK), BF16),
            pltpu.VMEM((256, 256), BF16),
            pltpu.VMEM((NCHUNK, 48, 2 * CHUNK), F32),
            pltpu.VMEM((2, 24, COLS), F32),
            pltpu.VMEM((2, ROWS, COLS), F32),
            pltpu.VMEM((2, 16, ROWS, 128), F32),
            pltpu.VMEM((2, CELLS, 16, 128), BF16),
            pltpu.VMEM((2, CELLS, 16, 128), BF16),
            pltpu.VMEM((2, 16, 16, 128), BF16),
            pltpu.VMEM((2, ZS, 2, 16, 128), BF16),
            pltpu.VMEM((SKY * 64, 512), BF16),
            pltpu.VMEM((256, 256), BF16),
            pltpu.VMEM((SKY, 8, 128), F32),
            pltpu.VMEM((ZS, 8, 128), F32),
            pltpu.VMEM((ZS, 8, 128), F32),
            pltpu.VMEM((8, 128), F32),
            pltpu.VMEM((CELLS * ZS, 128), F32),
            dma((6,)), dma((NCHUNK,)),
            dma((GROUPS - 1,)), dma((GROUPS - 1,)),
            pltpu.VMEM((2, 48, CHUNK), BF16),
            dma((3,)), dma((2,)),
            regular, regular, regular,
            dma((CELLS - 1,)), dma((CELLS - 1,)),
            dma((ZS - 1,)), dma((ZS,)),
            dma((ZS - 1,)), dma((ZS,)),
            dma, dma,
        ],
        compiler_params=pltpu.CompilerParams(
            collective_id=0, has_side_effects=True, vmem_limit_bytes=56 * 1024 * 1024
        ),
        cost_estimate=pl.CostEstimate(flops=400_000_000, bytes_accessed=6_000_000, transcendentals=0),
    )(
        templates.reshape(16, LEN),
        strain.reshape(48, CHUNK),
        inverse_psd.reshape(24, LEN),
        antenna,
        delays,
        tab,
        last,
    )
    sky, peak = pl.pallas_call(
        hand_over,
        out_shape=(jax.ShapeDtypeStruct((8, LEN), F32), jax.ShapeDtypeStruct((1, SKY), F32)),
        in_specs=[anywhere, anywhere],
        out_specs=(anywhere, anywhere),
        scratch_shapes=[dma((2,))],
        compiler_params=pltpu.CompilerParams(vmem_limit_bytes=1024 * 1024),
    )(sky, peak)
    return (sky[None], peak)


def solution(mesh):
    return jax.shard_map(
        shards,
        mesh=mesh,
        in_specs=(
            P(None, "det", "tmpl", None),
            P(None, None, "tmpl", "det"),
            P(None, "tmpl", None),
            P(),
            P(),
        ),
        out_specs=(P("det", "tmpl", None), P("det", None)),
        check_vma=False,
    )
```

```python
import math

import jax
import jax.numpy as jnp
import ml_dtypes
import numpy as np
from jax import lax
from jax.experimental import pallas as pl
from jax.experimental.pallas import tpu as pltpu
from jax.sharding import PartitionSpec as P

F32 = jnp.float32
BF16 = jnp.bfloat16
MESH = pl.DeviceIdType.MESH

LEN = 1024
FULL = LEN * LEN
DET = 3
SKY = 64
HALO = 8
CELLS = 16
ZS = 8
GROUPS = 4
ROWS = 8
WIDE = 64 + 2 * HALO
COLS = CELLS * WIDE
CHUNK = 256
NCHUNK = COLS // CHUNK
SIG = 16
LANES = SIG + DET * WIDE
SCAN = 16


def section_one_table():
    cols = np.arange(COLS)
    samples = 64 * (cols // WIDE) - HALO + cols % WIDE
    angle = 2.0 * np.pi * ((np.arange(LEN)[:, None] * samples[None, :]) % LEN) / LEN
    cos = np.cos(angle).reshape(LEN, NCHUNK, CHUNK)
    sin = np.sin(angle).reshape(LEN, NCHUNK, CHUNK)
    both = np.concatenate([cos, sin], axis=2)
    return np.ascontiguousarray(np.transpose(both, (1, 0, 2))).astype(ml_dtypes.bfloat16)


def last_section_table():
    table = np.zeros((ZS, 2, 2, ROWS, 2, 8, 8, 2))
    z = np.arange(ZS)[:, None, None, None]
    r = np.arange(ROWS)[None, :, None, None]
    m = np.arange(8)[None, None, :, None]
    h = np.arange(8)[None, None, None, :]
    angle = 2.0 * np.pi * (((8 * z + r) * (8 * m + h)) % 64) / 64
    for ql in range(2):
        table[:, ql, 0, :, 0, :, :, ql] = np.cos(angle)
        table[:, ql, 1, :, 0, :, :, ql] = -np.sin(angle)
        table[:, ql, 0, :, 1, :, :, ql] = np.sin(angle)
        table[:, ql, 1, :, 1, :, :, ql] = np.cos(angle)
    table = table.reshape(256, 256)
    high = table.astype(ml_dtypes.bfloat16)
    return np.stack([high, (table - high.astype(np.float64)).astype(ml_dtypes.bfloat16)])


def unit_circle(turns):
    turns = turns & (FULL - 1)
    quarter = (turns + FULL // 8) >> 18
    x = (turns - (quarter << 18)).astype(F32) * (2.0 * math.pi / FULL)
    x2 = x * x
    s = x * (1.0 + x2 * (-1.0 / 6 + x2 * (1.0 / 120 + x2 * (-1.0 / 5040 + x2 * (1.0 / 362880)))))
    c = 1.0 + x2 * (-0.5 + x2 * (1.0 / 24 + x2 * (-1.0 / 720 + x2 * (1.0 / 40320))))
    odd = (quarter & 1) == 1
    cos = jnp.where(odd, s, c)
    sin = jnp.where(odd, c, s)
    cos = jnp.where(((quarter + 1) & 2) != 0, -cos, cos)
    sin = jnp.where((quarter & 2) != 0, -sin, sin)
    return cos, sin


def dft_four(a, b, c, d):
    sr, si = a[0] + c[0], a[1] + c[1]
    dr, di = a[0] - c[0], a[1] - c[1]
    tr, ti = b[0] + d[0], b[1] + d[1]
    er, ei = b[0] - d[0], b[1] - d[1]
    return (
        (sr + tr, si + ti),
        (dr - ei, di + er),
        (sr - tr, si - ti),
        (dr + ei, di - er),
    )


def dft_sixteen(cells):
    first = [dft_four(*[cells[4 * a + b] for a in range(4)]) for b in range(4)]
    out = [None] * 16
    for k0 in range(4):
        column = []
        for b in range(4):
            xr, xi = first[b][k0]
            turn = (b * k0) % 16
            if turn:
                wr = math.cos(2 * math.pi * turn / 16)
                wi = math.sin(2 * math.pi * turn / 16)
                xr, xi = xr * wr - xi * wi, xr * wi + xi * wr
            column.append((xr, xi))
        for k1, value in enumerate(dft_four(*column)):
            out[k0 + 4 * k1] = value
    return out


def z_far_first(z):
    upper = z >= ZS // 2
    low = jnp.where(upper, ZS - 1 - z, z)
    alone = ZS - 1 - 2 * low
    places = []
    for j in range(ZS - 1):
        step = low - lax.div(jnp.maximum(j - alone, 0), 2)
        side = lax.rem(jnp.maximum(j - alone, 0), 2)
        place = jnp.where(j < alone, ZS - 1 - j, low + step - 2 * step * side)
        places.append(jnp.where(upper, ZS - 1 - place, place))
    return places


def split_two(x):
    high = x.astype(BF16).astype(F32)
    return high, x - high


def kernel(
    tmpl_hbm, strain_hbm, psd_hbm, ant_hbm, delay_hbm, tab_hbm, last_hbm,
    sky_out, peak_out,
    ant, delay, tmpl_v, strain_v, psd_v, tab_v, last_v, acc_v, twist_v, turn_v, turn2_v,
    send_xy, recv_xy, send_z, recv_z, sky_v, fin_v, pk_v, send_r, recv_r, send_p, recv_p,
    load_sem, tab_sem, s_send, s_recv, relay_v, relay_send, relay_recv, hello, ready, go, xy_send, xy_recv, z_send, z_recv, r_send, r_recv, p_send, p_recv,
):
    t = lax.axis_index("tmpl")
    g = lax.axis_index("det")
    cell = lax.div(t, ZS)
    z = lax.rem(t, ZS)

    late = lax.div(g, 2)
    near_z = z < ZS // 2
    core_g = g + 1 - 2 * lax.rem(g, 2)
    far_g = lax.rem(g + 2, GROUPS)
    diag_g = lax.rem(core_g + 2, GROUPS)
    core_id = {"tmpl": t, "det": core_g}
    far_id = {"tmpl": t, "det": far_g}
    side = 4
    offsets = sorted(
        ((a, b) for a in range(side) for b in range(side) if a or b),
        key=lambda o: -min(o[0], side - o[0]) - min(o[1], side - o[1]),
    )
    cell_x, cell_y = lax.div(cell, side), lax.rem(cell, side)
    cell_to = [lax.rem(cell_x + a, side) * side + lax.rem(cell_y + b, side) for a, b in offsets]
    xy_ids = [{"tmpl": c * ZS + z, "det": g} for c in cell_to]
    z_to = z_far_first(z)
    z_ids = [{"tmpl": cell * ZS + k, "det": g} for k in z_to]

    def signal(sem, who):
        pl.semaphore_signal(sem, inc=1, device_id=who, device_id_type=MESH)

    step = ZS // 2
    middle = jnp.logical_and(z >= step, z < step + 2)
    top = z >= step + 2
    below_top = jnp.logical_and(z >= 2, z < step)
    above_id = {"tmpl": t + step, "det": g}
    far_above_id = {"tmpl": t + step, "det": far_g}
    near_ids = [{"tmpl": cell * ZS + lax.rem(z + k, step), "det": g} for k in range(1, step)]
    barrier = pltpu.get_barrier_semaphore()

    @pl.when(late == 0)
    def _():
        @pl.when(near_z)
        def _():
            signal(barrier, far_id)
            signal(barrier, far_above_id)

        @pl.when(middle)
        def _():
            signal(barrier, far_id)

        @pl.when(top)
        def _():
            signal(barrier, {"tmpl": t - step, "det": core_g})

    signal(barrier, core_id)

    @pl.when(late == 0)
    def _():
        for who in z_ids + xy_ids:
            signal(barrier, who)

    def remote(source, target, send, recv, who):
        return pltpu.make_async_remote_copy(
            src_ref=source, dst_ref=target, send_sem=send, recv_sem=recv, device_id=who, device_id_type=MESH
        )

    to_core = remote(strain_hbm, strain_v.at[g], s_send.at[0], s_recv.at[0], core_id)
    to_far = remote(strain_hbm, strain_v.at[g], s_send.at[1], s_recv.at[1], far_id)
    down_far = remote(strain_hbm, relay_v.at[0], s_send.at[1], relay_recv.at[0], {"tmpl": t - step, "det": far_g})
    down = remote(strain_hbm, relay_v.at[1], s_send.at[1], relay_recv.at[1], {"tmpl": t - step, "det": g})
    up = remote(relay_v.at[0], strain_v.at[far_g], relay_send.at[0], s_recv.at[1], above_id)
    up_far = remote(relay_v.at[1], strain_v.at[g], relay_send.at[1], s_recv.at[1], far_above_id)
    up_other = remote(
        relay_v.at[0], strain_v.at[far_g], relay_send.at[2], s_recv.at[2], {"tmpl": t + step, "det": core_g}
    )
    handed_on = remote(strain_v.at[far_g], strain_v.at[far_g], s_send.at[2], s_recv.at[2], core_id)
    is_near = jnp.logical_and(late == 0, near_z)
    hands_on = jnp.logical_or(late == 1, z < step + 2)

    @pl.when(late == 1)
    def _():
        pl.semaphore_wait(barrier, jnp.where(middle, 3, 2))

        @pl.when(near_z)
        def _():
            to_far.start()
            signal(hello, far_id)

        @pl.when(middle)
        def _():
            to_far.start()
            signal(hello, {"tmpl": t - step, "det": far_g})

        @pl.when(top)
        def _():
            down_far.start()

        to_core.start()

    loads = [
        pltpu.make_async_copy(strain_hbm, strain_v.at[g], load_sem.at[0]),
        pltpu.make_async_copy(tmpl_hbm, tmpl_v, load_sem.at[1]),
        pltpu.make_async_copy(psd_hbm, psd_v, load_sem.at[2]),
        pltpu.make_async_copy(last_hbm, last_v, load_sem.at[3]),
        pltpu.make_async_copy(ant_hbm, ant, load_sem.at[4]),
        pltpu.make_async_copy(delay_hbm, delay, load_sem.at[5]),
    ]
    tab_loads = [pltpu.make_async_copy(tab_hbm.at[n], tab_v.at[n], tab_sem.at[n]) for n in range(NCHUNK)]
    for copy in loads + tab_loads:
        copy.start()

    row = lax.broadcasted_iota(jnp.int32, (ROWS, COLS), 0)
    col = lax.broadcasted_iota(jnp.int32, (ROWS, COLS), 1)
    sample = col - 2 * HALO * ((col * 52429) >> 22) - HALO
    cos, sin = unit_circle((t * ROWS + row) * sample)
    turn_v[0] = cos
    turn_v[1] = sin
    row = lax.broadcasted_iota(jnp.int32, (ROWS, 128), 0)
    for q in range(16):
        cos, sin = unit_circle((z * ROWS + row) * (q * LEN))
        turn2_v[0, q] = cos
        turn2_v[1, q] = sin

    for copy in loads[1:3]:
        copy.wait()
    both = tmpl_v[...].astype(F32)
    tr, ti = both[:ROWS], both[ROWS:]
    square = tr * tr + ti * ti
    parts = [
        split_two(jnp.sum(square * psd_v[ROWS * d : ROWS * d + ROWS, :], axis=1, keepdims=True))
        for d in range(DET)
    ]
    blank = jnp.zeros((ROWS, SIG - DET), F32)
    sig = [jnp.concatenate([parts[d][c] for d in range(DET)] + [blank], axis=1) for c in range(2)]

    loads[4].wait()
    loads[5].wait()
    distance = lax.broadcasted_iota(jnp.int32, (64, 256), 1) - lax.broadcasted_iota(jnp.int32, (64, 256), 0)

    def weigh(s, carry):
        weights = jnp.zeros((64, 256), F32)
        for d in range(DET):
            weights = jnp.where(distance == SIG + WIDE * d + HALO + delay[d, s], ant[d, s], weights)
        sky_v[pl.ds(pl.multiple_of(64 * s, 64), 64), :] = weights.astype(BF16)
        return carry

    lax.fori_loop(0, SKY, weigh, 0)

    half = DET * ROWS
    for order, piece in enumerate([g, core_g, far_g, diag_g]):
        if order == 0:
            loads[0].wait()
            for copy in tab_loads:
                copy.wait()
        elif order == 1:

            @pl.when(late == 0)
            def _():
                pl.semaphore_wait(barrier, 1 + (ZS - 1) + (CELLS - 1) + jnp.where(below_top, 1, 0))

                @pl.when(near_z)
                def _():
                    @pl.when(below_top)
                    def _():
                        down_far.wait_recv()
                        up.start()
                        up_other.start()

                    to_core.start()
                    pl.semaphore_wait(hello, jnp.where(below_top, 1, 2))
                    to_far.start()
                    for who in near_ids + xy_ids:
                        signal(ready, who)

                @pl.when(jnp.logical_not(near_z))
                def _():
                    down.start()
                    to_core.start()

            to_core.wait_recv()
        elif order == 2:
            to_far.wait_recv()

            @pl.when(hands_on)
            def _():
                handed_on.start()

        else:
            handed_on.wait_recv()
        lanes = pl.ds(pl.multiple_of(CHUNK * piece, CHUNK), CHUNK)
        data = strain_v[piece].astype(F32)
        both = tmpl_v[:, lanes].astype(F32)
        trl, til = both[:ROWS], both[ROWS:]
        real, imag = [], []
        for d in range(DET):
            dr = data[ROWS * d : ROWS * d + ROWS]
            di = data[ROWS * (DET + d) : ROWS * (DET + d) + ROWS]
            weight = psd_v[ROWS * d : ROWS * d + ROWS, lanes]
            real.append((trl * dr + til * di) * weight)
            imag.append((trl * di - til * dr) * weight)
        product = jnp.concatenate(real + imag, axis=0).astype(BF16)
        for n in range(NCHUNK):
            out = jnp.dot(product, tab_v[n, lanes, :], preferred_element_type=F32)
            if order:
                out = out + acc_v[n]
            if order < GROUPS - 1:
                acc_v[n] = out
                continue
            sec_r = out[:half, :CHUNK] - out[half:, CHUNK:]
            sec_i = out[:half, CHUNK:] + out[half:, :CHUNK]
            cols = slice(CHUNK * n, CHUNK * n + CHUNK)
            cos, sin = turn_v[0, :, cols], turn_v[1, :, cols]
            for d in range(DET):
                rows = slice(ROWS * d, ROWS * d + ROWS)
                twist_v[0, rows, cols] = sec_r[rows] * cos - sec_i[rows] * sin
                twist_v[1, rows, cols] = sec_r[rows] * sin + sec_i[rows] * cos

    for c in range(CELLS):
        lanes = slice(WIDE * c, WIDE * c + WIDE)
        block = jnp.concatenate(
            [
                jnp.concatenate(
                    [sig[i]] + [twist_v[i, ROWS * d : ROWS * d + ROWS, lanes] for d in range(DET)], axis=1
                )
                for i in range(2)
            ],
            axis=0,
        ).astype(BF16)
        send_xy[0, c] = block[:, :128]
        send_xy[1, c] = block[:, 128:]

    @pl.when(late == 1)
    def _():
        pl.semaphore_wait(go, 1)

    xy_copies = [
        remote(send_xy.at[:, cell_to[k]], recv_xy.at[:, cell], xy_send.at[k], xy_recv.at[k], xy_ids[k])
        for k in range(CELLS - 1)
    ]
    for copy in xy_copies:
        copy.start()
    recv_xy[:, cell] = send_xy[:, cell]

    @pl.when(is_near)
    def _():
        down.wait_recv()
        up_far.start()
        pl.semaphore_wait(ready, (step - 1) + (CELLS - 1))
        signal(go, far_id)
        signal(go, far_above_id)

    lane = lax.broadcasted_iota(jnp.int32, (ROWS, 128), 1)
    for copy in xy_copies:
        copy.wait_recv()
    for part in range(2):
        cells = []
        for c in range(CELLS):
            value = recv_xy[part, c].astype(F32)
            cells.append((value[:ROWS], value[ROWS:]))
        bins = dft_sixteen(cells)
        if part == 0:
            high, low = split_two(bins[0][0] + bins[0][1])
        for q in range(16):
            xr, xi = bins[q]
            cos, sin = turn2_v[0, q], turn2_v[1, q]
            yr, yi = xr * cos - xi * sin, xr * sin + xi * cos
            if part == 0:
                yr = jnp.where(lane < SIG, high, yr)
                yi = jnp.where(lane < SIG, low, yi)
            send_z[part, q] = jnp.concatenate([yr, yi], axis=0).astype(BF16)
    z_copies = [
        remote(send_z.at[:, pl.ds(2 * z_to[k], 2)], recv_z.at[:, z], z_send.at[k], z_recv.at[z], z_ids[k])
        for k in range(ZS - 1)
    ]
    for copy in z_copies:
        copy.start()
    recv_z[:, z] = send_z[:, pl.ds(2 * z, 2)]

    scales = None
    for k in z_to:
        pltpu.make_async_copy(recv_z.at[:, k], recv_z.at[:, k], z_recv.at[k]).wait()
    for part in range(2):
        got = recv_z[part].reshape(256, 128)
        if part == 0:
            halves = recv_z[part, :, 0].astype(F32)
            total = jnp.sum(jnp.sum(halves, axis=0), axis=0, keepdims=True)
            scales = [1.0 / jnp.sqrt(total[:, d : d + 1]) for d in range(DET)]
        if part == 0:
            loads[3].wait()
        out = sum(
            lax.dot_general(got, last_v[k], (((0,), (0,)), ((), ())), preferred_element_type=F32) for k in range(2)
        )
        for d in range(DET):
            low_row = max(SIG + WIDE * d, 128 * part)
            high_row = min(SIG + WIDE * (d + 1), 128 * part + 128)
            if low_row < high_row:
                block = out[low_row - 128 * part : high_row - 128 * part]
                fin_v[low_row:high_row, :] = (block * scales[d]).astype(BF16)

    fin_v[:SIG, :] = jnp.zeros((SIG, 256), BF16)
    detectors = fin_v[...]
    best = jnp.zeros((64, 128), F32)
    for first in range(0, SKY, SCAN):
        both = jnp.dot(sky_v[64 * first : 64 * (first + SCAN), :], detectors, preferred_element_type=F32)
        real, imag = both[:, :128], both[:, 128:]
        power = (real * real + imag * imag).reshape(SCAN, 64, 128)
        pk_v[first : first + SCAN] = jnp.max(power.reshape(SCAN, 8, 8, 128), axis=1)
        best = jnp.maximum(best, jnp.max(power, axis=0))

    tops = jnp.max(pk_v[...], axis=1)
    tops = jnp.max(jnp.transpose(tops), axis=0, keepdims=True)
    tops = jnp.concatenate([tops, jnp.zeros((1, 128 - SKY), F32)], axis=1)
    send_p[...] = jnp.broadcast_to(tops, (8, 128))
    others = CELLS * ZS - 1

    own = jnp.where(late == 0, z, ZS - 1 - z) * CELLS + cell

    def tell(k, carry):
        turn = k + jnp.where(k >= own, 1, 0)
        place = lax.div(turn, CELLS)
        place = jnp.where(late == 0, place, ZS - 1 - place)
        who = {"tmpl": lax.rem(turn, CELLS) * ZS + place, "det": g}
        remote(send_p.at[pl.ds(0, 1)], recv_p.at[pl.ds(t, 1)], p_send, p_recv, who).start()
        return carry

    lax.fori_loop(0, others, tell, 0)
    recv_p[pl.ds(t, 1), :] = tops

    for k in range(ZS):
        send_r[k] = best[8 * k : 8 * k + 8]
    r_copies = [
        remote(send_r.at[z_to[k]], recv_r.at[z], r_send.at[k], r_recv.at[z], z_ids[k]) for k in range(ZS - 1)
    ]
    for copy in r_copies:
        copy.start()
    recv_r[z] = send_r[z]

    for k in z_to:
        pltpu.make_async_copy(recv_r.at[k], recv_r.at[k], r_recv.at[k]).wait()
    lane = lax.broadcasted_iota(jnp.int32, (8, 128), 1)
    owner = (lane >> 1) & 7
    for m in range(8):
        index = 16 * m + 2 * (lane >> 4) + (lane & 1)
        acc = jnp.zeros((8, 128), F32)
        for k in range(ZS):
            moved = jnp.take_along_axis(recv_r[k], index, axis=1, mode="promise_in_bounds")
            acc = jnp.where(owner == k, moved, acc)
        sky_out[:, 128 * m : 128 * m + 128] = acc

    rows = pl.ds(0, others)
    pltpu.make_async_copy(recv_p.at[rows], recv_p.at[rows], p_recv).wait()
    peak_out[...] = jnp.max(recv_p[...], axis=0, keepdims=True)[:, :SKY]

    for copy in (to_core, to_far):
        copy.wait_send()

    @pl.when(hands_on)
    def _():
        handed_on.wait_send()

    @pl.when(is_near)
    def _():
        up_far.wait_send()

        @pl.when(below_top)
        def _():
            up.wait_send()
            up_other.wait_send()

    for copy in xy_copies + z_copies + r_copies:
        copy.wait_send()
    pltpu.make_async_copy(recv_p.at[rows], recv_p.at[rows], p_send).wait()


def hand_over(sky_in, peak_in, sky_out, peak_out, sem):
    copies = [pltpu.make_async_copy(sky_in, sky_out, sem.at[0]), pltpu.make_async_copy(peak_in, peak_out, sem.at[1])]
    for copy in copies:
        copy.start()
    for copy in copies:
        copy.wait()


def shards(templates, strain, inverse_psd, antenna, delays):
    tab = jnp.asarray(section_one_table())
    last = jnp.asarray(last_section_table())
    hbm = pl.BlockSpec(memory_space=pltpu.HBM)
    anywhere = pl.BlockSpec(memory_space=pl.ANY)
    vmem = pl.BlockSpec(memory_space=pltpu.VMEM)
    dma = pltpu.SemaphoreType.DMA
    regular = pltpu.SemaphoreType.REGULAR
    sky, peak = pl.pallas_call(
        kernel,
        out_shape=(pltpu.VMEM((8, LEN), F32), pltpu.VMEM((1, SKY), F32)),
        in_specs=[hbm] * 7,
        out_specs=(vmem, vmem),
        scratch_shapes=[
            pltpu.SMEM((DET, SKY), F32),
            pltpu.SMEM((DET, SKY), jnp.int32),
            pltpu.VMEM((16, LEN), BF16),
            pltpu.VMEM((GROUPS, 48, CHUNK), BF16),
            pltpu.VMEM((24, LEN), F32),
            pltpu.VMEM((NCHUNK, LEN, 2 * CHUNK), BF16),
            pltpu.VMEM((2, 256, 256), BF16),
            pltpu.VMEM((NCHUNK, 48, 2 * CHUNK), F32),
            pltpu.VMEM((2, 24, COLS), F32),
            pltpu.VMEM((2, ROWS, COLS), F32),
            pltpu.VMEM((2, 16, ROWS, 128), F32),
            pltpu.VMEM((2, CELLS, 16, 128), BF16),
            pltpu.VMEM((2, CELLS, 16, 128), BF16),
            pltpu.VMEM((2, 16, 16, 128), BF16),
            pltpu.VMEM((2, ZS, 2, 16, 128), BF16),
            pltpu.VMEM((SKY * 64, 256), BF16),
            pltpu.VMEM((256, 256), BF16),
            pltpu.VMEM((SKY, 8, 128), F32),
            pltpu.VMEM((ZS, 8, 128), F32),
            pltpu.VMEM((ZS, 8, 128), F32),
            pltpu.VMEM((8, 128), F32),
            pltpu.VMEM((CELLS * ZS, 128), F32),
            dma((6,)), dma((NCHUNK,)),
            dma((GROUPS - 1,)), dma((GROUPS - 1,)),
            pltpu.VMEM((2, 48, CHUNK), BF16),
            dma((3,)), dma((2,)),
            regular, regular, regular,
            dma((CELLS - 1,)), dma((CELLS - 1,)),
            dma((ZS - 1,)), dma((ZS,)),
            dma((ZS - 1,)), dma((ZS,)),
            dma, dma,
        ],
        compiler_params=pltpu.CompilerParams(
            collective_id=0, has_side_effects=True, vmem_limit_bytes=56 * 1024 * 1024
        ),
        cost_estimate=pl.CostEstimate(flops=400_000_000, bytes_accessed=6_000_000, transcendentals=0),
    )(
        templates.reshape(16, LEN),
        strain.reshape(48, CHUNK),
        inverse_psd.reshape(24, LEN),
        antenna,
        delays,
        tab,
        last,
    )
    sky, peak = pl.pallas_call(
        hand_over,
        out_shape=(jax.ShapeDtypeStruct((8, LEN), F32), jax.ShapeDtypeStruct((1, SKY), F32)),
        in_specs=[anywhere, anywhere],
        out_specs=(anywhere, anywhere),
        scratch_shapes=[dma((2,))],
        compiler_params=pltpu.CompilerParams(vmem_limit_bytes=1024 * 1024),
    )(sky, peak)
    return (sky[None], peak)


def solution(mesh):
    return jax.shard_map(
        shards,
        mesh=mesh,
        in_specs=(
            P(None, "det", "tmpl", None),
            P(None, None, "tmpl", "det"),
            P(None, "tmpl", None),
            P(),
            P(),
        ),
        out_specs=(P("det", "tmpl", None), P("det", None)),
        check_vma=False,
    )
```

```python
import math

import jax
import jax.numpy as jnp
import ml_dtypes
import numpy as np
from jax import lax
from jax.experimental import pallas as pl
from jax.experimental.pallas import tpu as pltpu
from jax.sharding import PartitionSpec as P

F32 = jnp.float32
BF16 = jnp.bfloat16
MESH = pl.DeviceIdType.MESH

LEN = 1024
FULL = LEN * LEN
DET = 3
SKY = 64
HALO = 8
CELLS = 16
ZS = 8
GROUPS = 4
ROWS = 8
WIDE = 64 + 2 * HALO
COLS = CELLS * WIDE
CHUNK = 256
NCHUNK = COLS // CHUNK
SIG = 16
LANES = SIG + DET * WIDE
SCAN = 64


def section_one_table():
    cols = np.arange(COLS)
    samples = 64 * (cols // WIDE) - HALO + cols % WIDE
    angle = 2.0 * np.pi * ((np.arange(LEN)[:, None] * samples[None, :]) % LEN) / LEN
    cos = np.cos(angle).reshape(LEN, NCHUNK, CHUNK)
    sin = np.sin(angle).reshape(LEN, NCHUNK, CHUNK)
    both = np.concatenate([cos, sin], axis=2)
    return np.ascontiguousarray(np.transpose(both, (1, 0, 2))).astype(ml_dtypes.bfloat16)


def last_section_table():
    table = np.zeros((ZS, 2, 2, ROWS, 2, 8, 8, 2))
    z = np.arange(ZS)[:, None, None, None]
    r = np.arange(ROWS)[None, :, None, None]
    m = np.arange(8)[None, None, :, None]
    h = np.arange(8)[None, None, None, :]
    angle = 2.0 * np.pi * (((8 * z + r) * (8 * m + h)) % 64) / 64
    for ql in range(2):
        table[:, ql, 0, :, 0, :, :, ql] = np.cos(angle)
        table[:, ql, 1, :, 0, :, :, ql] = -np.sin(angle)
        table[:, ql, 0, :, 1, :, :, ql] = np.sin(angle)
        table[:, ql, 1, :, 1, :, :, ql] = np.cos(angle)
    return table.reshape(256, 256).astype(ml_dtypes.bfloat16)


def unit_circle(turns):
    turns = turns & (FULL - 1)
    quarter = (turns + FULL // 8) >> 18
    x = (turns - (quarter << 18)).astype(F32) * (2.0 * math.pi / FULL)
    x2 = x * x
    s = x * (1.0 + x2 * (-1.0 / 6 + x2 * (1.0 / 120 + x2 * (-1.0 / 5040 + x2 * (1.0 / 362880)))))
    c = 1.0 + x2 * (-0.5 + x2 * (1.0 / 24 + x2 * (-1.0 / 720 + x2 * (1.0 / 40320))))
    odd = (quarter & 1) == 1
    cos = jnp.where(odd, s, c)
    sin = jnp.where(odd, c, s)
    cos = jnp.where(((quarter + 1) & 2) != 0, -cos, cos)
    sin = jnp.where((quarter & 2) != 0, -sin, sin)
    return cos, sin


def dft_four(a, b, c, d):
    sr, si = a[0] + c[0], a[1] + c[1]
    dr, di = a[0] - c[0], a[1] - c[1]
    tr, ti = b[0] + d[0], b[1] + d[1]
    er, ei = b[0] - d[0], b[1] - d[1]
    return (
        (sr + tr, si + ti),
        (dr - ei, di + er),
        (sr - tr, si - ti),
        (dr + ei, di - er),
    )


def dft_sixteen(cells):
    first = [dft_four(*[cells[4 * a + b] for a in range(4)]) for b in range(4)]
    out = [None] * 16
    for k0 in range(4):
        column = []
        for b in range(4):
            xr, xi = first[b][k0]
            turn = (b * k0) % 16
            if turn:
                wr = math.cos(2 * math.pi * turn / 16)
                wi = math.sin(2 * math.pi * turn / 16)
                xr, xi = xr * wr - xi * wi, xr * wi + xi * wr
            column.append((xr, xi))
        for k1, value in enumerate(dft_four(*column)):
            out[k0 + 4 * k1] = value
    return out


def z_far_first(z):
    upper = z >= ZS // 2
    low = jnp.where(upper, ZS - 1 - z, z)
    alone = ZS - 1 - 2 * low
    places = []
    for j in range(ZS - 1):
        step = low - lax.div(jnp.maximum(j - alone, 0), 2)
        side = lax.rem(jnp.maximum(j - alone, 0), 2)
        place = jnp.where(j < alone, ZS - 1 - j, low + step - 2 * step * side)
        places.append(jnp.where(upper, ZS - 1 - place, place))
    return places


def split_two(x):
    high = x.astype(BF16).astype(F32)
    return high, x - high


def kernel(
    tmpl_hbm, strain_hbm, psd_hbm, ant_hbm, delay_hbm, tab_hbm, last_hbm,
    sky_out, peak_out,
    ant, delay, tmpl_v, strain_v, psd_v, tab_v, last_v, acc_v, twist_v, turn_v, turn2_v,
    send_xy, recv_xy, send_z, recv_z, sky_v, fin_v, pk_v, send_r, recv_r, send_p, recv_p,
    load_sem, tab_sem, s_send, s_recv, relay_v, relay_send, relay_recv, hello, ready, go, xy_send, xy_recv, z_send, z_recv, r_send, r_recv, p_send, p_recv,
):
    t = lax.axis_index("tmpl")
    g = lax.axis_index("det")
    cell = lax.div(t, ZS)
    z = lax.rem(t, ZS)

    late = lax.div(g, 2)
    near_z = z < ZS // 2
    core_g = g + 1 - 2 * lax.rem(g, 2)
    far_g = lax.rem(g + 2, GROUPS)
    diag_g = lax.rem(core_g + 2, GROUPS)
    core_id = {"tmpl": t, "det": core_g}
    far_id = {"tmpl": t, "det": far_g}
    side = 4
    offsets = sorted(
        ((a, b) for a in range(side) for b in range(side) if a or b),
        key=lambda o: -min(o[0], side - o[0]) - min(o[1], side - o[1]),
    )
    cell_x, cell_y = lax.div(cell, side), lax.rem(cell, side)
    cell_to = [lax.rem(cell_x + a, side) * side + lax.rem(cell_y + b, side) for a, b in offsets]
    xy_ids = [{"tmpl": c * ZS + z, "det": g} for c in cell_to]
    z_to = z_far_first(z)
    z_ids = [{"tmpl": cell * ZS + k, "det": g} for k in z_to]

    def signal(sem, who):
        pl.semaphore_signal(sem, inc=1, device_id=who, device_id_type=MESH)

    step = ZS // 2
    middle = jnp.logical_and(z >= step, z < step + 2)
    top = z >= step + 2
    below_top = jnp.logical_and(z >= 2, z < step)
    above_id = {"tmpl": t + step, "det": g}
    far_above_id = {"tmpl": t + step, "det": far_g}
    near_ids = [{"tmpl": cell * ZS + lax.rem(z + k, step), "det": g} for k in range(1, step)]
    barrier = pltpu.get_barrier_semaphore()

    @pl.when(late == 0)
    def _():
        @pl.when(near_z)
        def _():
            signal(barrier, far_id)
            signal(barrier, far_above_id)

        @pl.when(middle)
        def _():
            signal(barrier, far_id)

        @pl.when(top)
        def _():
            signal(barrier, {"tmpl": t - step, "det": core_g})

    signal(barrier, core_id)

    @pl.when(late == 0)
    def _():
        for who in z_ids + xy_ids:
            signal(barrier, who)

    def remote(source, target, send, recv, who):
        return pltpu.make_async_remote_copy(
            src_ref=source, dst_ref=target, send_sem=send, recv_sem=recv, device_id=who, device_id_type=MESH
        )

    to_core = remote(strain_hbm, strain_v.at[g], s_send.at[0], s_recv.at[0], core_id)
    to_far = remote(strain_hbm, strain_v.at[g], s_send.at[1], s_recv.at[1], far_id)
    down_far = remote(strain_hbm, relay_v.at[0], s_send.at[1], relay_recv.at[0], {"tmpl": t - step, "det": far_g})
    down = remote(strain_hbm, relay_v.at[1], s_send.at[1], relay_recv.at[1], {"tmpl": t - step, "det": g})
    up = remote(relay_v.at[0], strain_v.at[far_g], relay_send.at[0], s_recv.at[1], above_id)
    up_far = remote(relay_v.at[1], strain_v.at[g], relay_send.at[1], s_recv.at[1], far_above_id)
    up_other = remote(
        relay_v.at[0], strain_v.at[far_g], relay_send.at[2], s_recv.at[2], {"tmpl": t + step, "det": core_g}
    )
    handed_on = remote(strain_v.at[far_g], strain_v.at[far_g], s_send.at[2], s_recv.at[2], core_id)
    is_near = jnp.logical_and(late == 0, near_z)
    hands_on = jnp.logical_or(late == 1, z < step + 2)

    @pl.when(late == 1)
    def _():
        pl.semaphore_wait(barrier, jnp.where(middle, 3, 2))

        @pl.when(near_z)
        def _():
            to_far.start()
            signal(hello, far_id)

        @pl.when(middle)
        def _():
            to_far.start()
            signal(hello, {"tmpl": t - step, "det": far_g})

        @pl.when(top)
        def _():
            down_far.start()

        to_core.start()

    loads = [
        pltpu.make_async_copy(strain_hbm, strain_v.at[g], load_sem.at[0]),
        pltpu.make_async_copy(tmpl_hbm, tmpl_v, load_sem.at[1]),
        pltpu.make_async_copy(psd_hbm, psd_v, load_sem.at[2]),
        pltpu.make_async_copy(last_hbm, last_v, load_sem.at[3]),
        pltpu.make_async_copy(ant_hbm, ant, load_sem.at[4]),
        pltpu.make_async_copy(delay_hbm, delay, load_sem.at[5]),
    ]
    tab_loads = [pltpu.make_async_copy(tab_hbm.at[n], tab_v.at[n], tab_sem.at[n]) for n in range(NCHUNK)]
    for copy in loads + tab_loads:
        copy.start()

    row = lax.broadcasted_iota(jnp.int32, (ROWS, COLS), 0)
    col = lax.broadcasted_iota(jnp.int32, (ROWS, COLS), 1)
    sample = col - 2 * HALO * ((col * 52429) >> 22) - HALO
    cos, sin = unit_circle((t * ROWS + row) * sample)
    turn_v[0] = cos
    turn_v[1] = sin
    row = lax.broadcasted_iota(jnp.int32, (ROWS, 128), 0)
    for q in range(16):
        cos, sin = unit_circle((z * ROWS + row) * (q * LEN))
        turn2_v[0, q] = cos
        turn2_v[1, q] = sin

    for copy in loads[1:3]:
        copy.wait()
    both = tmpl_v[...].astype(F32)
    tr, ti = both[:ROWS], both[ROWS:]
    square = tr * tr + ti * ti
    parts = [
        split_two(jnp.sum(square * psd_v[ROWS * d : ROWS * d + ROWS, :], axis=1, keepdims=True))
        for d in range(DET)
    ]
    blank = jnp.zeros((ROWS, SIG - DET), F32)
    sig = [jnp.concatenate([parts[d][c] for d in range(DET)] + [blank], axis=1) for c in range(2)]

    loads[4].wait()
    loads[5].wait()
    distance = lax.broadcasted_iota(jnp.int32, (64, 256), 1) - lax.broadcasted_iota(jnp.int32, (64, 256), 0)

    def weigh(s, carry):
        weights = jnp.zeros((64, 256), F32)
        for d in range(DET):
            weights = jnp.where(distance == SIG + WIDE * d + HALO + delay[d, s], ant[d, s], weights)
        high, low = split_two(weights)
        rows = pl.ds(pl.multiple_of(64 * s, 64), 64)
        sky_v[rows, :256] = high.astype(BF16)
        sky_v[rows, 256:] = low.astype(BF16)
        return carry

    lax.fori_loop(0, SKY, weigh, 0)

    half = DET * ROWS
    for order, piece in enumerate([g, core_g, far_g, diag_g]):
        if order == 0:
            loads[0].wait()
            for copy in tab_loads:
                copy.wait()
        elif order == 1:

            @pl.when(late == 0)
            def _():
                pl.semaphore_wait(barrier, 1 + (ZS - 1) + (CELLS - 1) + jnp.where(below_top, 1, 0))

                @pl.when(near_z)
                def _():
                    @pl.when(below_top)
                    def _():
                        down_far.wait_recv()
                        up.start()
                        up_other.start()

                    to_core.start()
                    pl.semaphore_wait(hello, jnp.where(below_top, 1, 2))
                    to_far.start()
                    for who in near_ids + xy_ids:
                        signal(ready, who)

                @pl.when(jnp.logical_not(near_z))
                def _():
                    down.start()
                    to_core.start()

            to_core.wait_recv()
        elif order == 2:
            to_far.wait_recv()

            @pl.when(hands_on)
            def _():
                handed_on.start()

        else:
            handed_on.wait_recv()
        lanes = pl.ds(pl.multiple_of(CHUNK * piece, CHUNK), CHUNK)
        data = strain_v[piece].astype(F32)
        both = tmpl_v[:, lanes].astype(F32)
        trl, til = both[:ROWS], both[ROWS:]
        real, imag = [], []
        for d in range(DET):
            dr = data[ROWS * d : ROWS * d + ROWS]
            di = data[ROWS * (DET + d) : ROWS * (DET + d) + ROWS]
            weight = psd_v[ROWS * d : ROWS * d + ROWS, lanes]
            real.append((trl * dr + til * di) * weight)
            imag.append((trl * di - til * dr) * weight)
        product = jnp.concatenate(real + imag, axis=0).astype(BF16)
        for n in range(NCHUNK):
            out = jnp.dot(product, tab_v[n, lanes, :], preferred_element_type=F32)
            if order:
                out = out + acc_v[n]
            if order < GROUPS - 1:
                acc_v[n] = out
                continue
            sec_r = out[:half, :CHUNK] - out[half:, CHUNK:]
            sec_i = out[:half, CHUNK:] + out[half:, :CHUNK]
            cols = slice(CHUNK * n, CHUNK * n + CHUNK)
            cos, sin = turn_v[0, :, cols], turn_v[1, :, cols]
            for d in range(DET):
                rows = slice(ROWS * d, ROWS * d + ROWS)
                twist_v[0, rows, cols] = sec_r[rows] * cos - sec_i[rows] * sin
                twist_v[1, rows, cols] = sec_r[rows] * sin + sec_i[rows] * cos

    for c in range(CELLS):
        lanes = slice(WIDE * c, WIDE * c + WIDE)
        block = jnp.concatenate(
            [
                jnp.concatenate(
                    [sig[i]] + [twist_v[i, ROWS * d : ROWS * d + ROWS, lanes] for d in range(DET)], axis=1
                )
                for i in range(2)
            ],
            axis=0,
        ).astype(BF16)
        send_xy[0, c] = block[:, :128]
        send_xy[1, c] = block[:, 128:]

    @pl.when(late == 1)
    def _():
        pl.semaphore_wait(go, 1)

    xy_copies = [
        remote(send_xy.at[:, cell_to[k]], recv_xy.at[:, cell], xy_send.at[k], xy_recv.at[k], xy_ids[k])
        for k in range(CELLS - 1)
    ]
    for copy in xy_copies:
        copy.start()
    recv_xy[:, cell] = send_xy[:, cell]

    @pl.when(is_near)
    def _():
        down.wait_recv()
        up_far.start()
        pl.semaphore_wait(ready, (step - 1) + (CELLS - 1))
        signal(go, far_id)
        signal(go, far_above_id)

    lane = lax.broadcasted_iota(jnp.int32, (ROWS, 128), 1)
    for copy in xy_copies:
        copy.wait_recv()
    for part in range(2):
        cells = []
        for c in range(CELLS):
            value = recv_xy[part, c].astype(F32)
            cells.append((value[:ROWS], value[ROWS:]))
        bins = dft_sixteen(cells)
        if part == 0:
            high, low = split_two(bins[0][0] + bins[0][1])
        for q in range(16):
            xr, xi = bins[q]
            cos, sin = turn2_v[0, q], turn2_v[1, q]
            yr, yi = xr * cos - xi * sin, xr * sin + xi * cos
            if part == 0:
                yr = jnp.where(lane < SIG, high, yr)
                yi = jnp.where(lane < SIG, low, yi)
            send_z[part, q] = jnp.concatenate([yr, yi], axis=0).astype(BF16)
    z_copies = [
        remote(send_z.at[:, pl.ds(2 * z_to[k], 2)], recv_z.at[:, z], z_send.at[k], z_recv.at[z], z_ids[k])
        for k in range(ZS - 1)
    ]
    for copy in z_copies:
        copy.start()
    recv_z[:, z] = send_z[:, pl.ds(2 * z, 2)]

    scales = None
    for k in z_to:
        pltpu.make_async_copy(recv_z.at[:, k], recv_z.at[:, k], z_recv.at[k]).wait()
    for part in range(2):
        got = recv_z[part].reshape(256, 128)
        if part == 0:
            halves = recv_z[part, :, 0].astype(F32)
            total = jnp.sum(jnp.sum(halves, axis=0), axis=0, keepdims=True)
            scales = [1.0 / jnp.sqrt(total[:, d : d + 1]) for d in range(DET)]
        out = lax.dot_general(got, last_v[...] if part else _wait_load(loads[3], last_v), (((0,), (0,)), ((), ())), preferred_element_type=F32)
        for d in range(DET):
            low_row = max(SIG + WIDE * d, 128 * part)
            high_row = min(SIG + WIDE * (d + 1), 128 * part + 128)
            if low_row < high_row:
                block = out[low_row - 128 * part : high_row - 128 * part]
                fin_v[low_row:high_row, :] = (block * scales[d]).astype(BF16)

    fin_v[:SIG, :] = jnp.zeros((SIG, 256), BF16)
    detectors = jnp.concatenate([fin_v[...], fin_v[...]], axis=0)
    best = jnp.zeros((64, 128), F32)
    for first in range(0, SKY, SCAN):
        rows = slice(64 * first, 64 * (first + SCAN))
        both = jnp.dot(sky_v[rows, :], detectors, preferred_element_type=F32)
        real, imag = both[:, :128], both[:, 128:]
        power = (real * real + imag * imag).reshape(SCAN, 64, 128)
        pk_v[first : first + SCAN] = jnp.max(power.reshape(SCAN, 8, 8, 128), axis=1)
        best = jnp.maximum(best, jnp.max(power, axis=0))

    tops = jnp.max(pk_v[...], axis=1)
    tops = jnp.max(jnp.transpose(tops), axis=0, keepdims=True)
    tops = jnp.concatenate([tops, jnp.zeros((1, 128 - SKY), F32)], axis=1)
    send_p[...] = jnp.broadcast_to(tops, (8, 128))
    others = CELLS * ZS - 1

    own = jnp.where(late == 0, z, ZS - 1 - z) * CELLS + cell

    def tell(k, carry):
        turn = k + jnp.where(k >= own, 1, 0)
        place = lax.div(turn, CELLS)
        place = jnp.where(late == 0, place, ZS - 1 - place)
        who = {"tmpl": lax.rem(turn, CELLS) * ZS + place, "det": g}
        remote(send_p.at[pl.ds(0, 1)], recv_p.at[pl.ds(t, 1)], p_send, p_recv, who).start()
        return carry

    lax.fori_loop(0, others, tell, 0)
    recv_p[pl.ds(t, 1), :] = tops

    for k in range(ZS):
        send_r[k] = best[8 * k : 8 * k + 8]
    r_copies = [
        remote(send_r.at[z_to[k]], recv_r.at[z], r_send.at[k], r_recv.at[z], z_ids[k]) for k in range(ZS - 1)
    ]
    for copy in r_copies:
        copy.start()
    recv_r[z] = send_r[z]

    for k in z_to:
        pltpu.make_async_copy(recv_r.at[k], recv_r.at[k], r_recv.at[k]).wait()
    lane = lax.broadcasted_iota(jnp.int32, (8, 128), 1)
    owner = (lane >> 1) & 7
    for m in range(8):
        index = 16 * m + 2 * (lane >> 4) + (lane & 1)
        acc = jnp.zeros((8, 128), F32)
        for k in range(ZS):
            moved = jnp.take_along_axis(recv_r[k], index, axis=1, mode="promise_in_bounds")
            acc = jnp.where(owner == k, moved, acc)
        sky_out[:, 128 * m : 128 * m + 128] = acc

    rows = pl.ds(0, others)
    pltpu.make_async_copy(recv_p.at[rows], recv_p.at[rows], p_recv).wait()
    peak_out[...] = jnp.max(recv_p[...], axis=0, keepdims=True)[:, :SKY]

    for copy in (to_core, to_far):
        copy.wait_send()

    @pl.when(hands_on)
    def _():
        handed_on.wait_send()

    @pl.when(is_near)
    def _():
        up_far.wait_send()

        @pl.when(below_top)
        def _():
            up.wait_send()
            up_other.wait_send()

    for copy in xy_copies + z_copies + r_copies:
        copy.wait_send()
    pltpu.make_async_copy(recv_p.at[rows], recv_p.at[rows], p_send).wait()


def _wait_load(copy, ref):
    copy.wait()
    return ref[...]


def hand_over(sky_in, peak_in, sky_out, peak_out, sem):
    copies = [pltpu.make_async_copy(sky_in, sky_out, sem.at[0]), pltpu.make_async_copy(peak_in, peak_out, sem.at[1])]
    for copy in copies:
        copy.start()
    for copy in copies:
        copy.wait()


def shards(templates, strain, inverse_psd, antenna, delays):
    tab = jnp.asarray(section_one_table())
    last = jnp.asarray(last_section_table())
    hbm = pl.BlockSpec(memory_space=pltpu.HBM)
    anywhere = pl.BlockSpec(memory_space=pl.ANY)
    vmem = pl.BlockSpec(memory_space=pltpu.VMEM)
    dma = pltpu.SemaphoreType.DMA
    regular = pltpu.SemaphoreType.REGULAR
    sky, peak = pl.pallas_call(
        kernel,
        out_shape=(pltpu.VMEM((8, LEN), F32), pltpu.VMEM((1, SKY), F32)),
        in_specs=[hbm] * 7,
        out_specs=(vmem, vmem),
        scratch_shapes=[
            pltpu.SMEM((DET, SKY), F32),
            pltpu.SMEM((DET, SKY), jnp.int32),
            pltpu.VMEM((16, LEN), BF16),
            pltpu.VMEM((GROUPS, 48, CHUNK), BF16),
            pltpu.VMEM((24, LEN), F32),
            pltpu.VMEM((NCHUNK, LEN, 2 * CHUNK), BF16),
            pltpu.VMEM((256, 256), BF16),
            pltpu.VMEM((NCHUNK, 48, 2 * CHUNK), F32),
            pltpu.VMEM((2, 24, COLS), F32),
            pltpu.VMEM((2, ROWS, COLS), F32),
            pltpu.VMEM((2, 16, ROWS, 128), F32),
            pltpu.VMEM((2, CELLS, 16, 128), BF16),
            pltpu.VMEM((2, CELLS, 16, 128), BF16),
            pltpu.VMEM((2, 16, 16, 128), BF16),
            pltpu.VMEM((2, ZS, 2, 16, 128), BF16),
            pltpu.VMEM((SKY * 64, 512), BF16),
            pltpu.VMEM((256, 256), BF16),
            pltpu.VMEM((SKY, 8, 128), F32),
            pltpu.VMEM((ZS, 8, 128), F32),
            pltpu.VMEM((ZS, 8, 128), F32),
            pltpu.VMEM((8, 128), F32),
            pltpu.VMEM((CELLS * ZS, 128), F32),
            dma((6,)), dma((NCHUNK,)),
            dma((GROUPS - 1,)), dma((GROUPS - 1,)),
            pltpu.VMEM((2, 48, CHUNK), BF16),
            dma((3,)), dma((2,)),
            regular, regular, regular,
            dma((CELLS - 1,)), dma((CELLS - 1,)),
            dma((ZS - 1,)), dma((ZS,)),
            dma((ZS - 1,)), dma((ZS,)),
            dma, dma,
        ],
        compiler_params=pltpu.CompilerParams(
            collective_id=0, has_side_effects=True, vmem_limit_bytes=56 * 1024 * 1024
        ),
        cost_estimate=pl.CostEstimate(flops=400_000_000, bytes_accessed=6_000_000, transcendentals=0),
    )(
        templates.reshape(16, LEN),
        strain.reshape(48, CHUNK),
        inverse_psd.reshape(24, LEN),
        antenna,
        delays,
        tab,
        last,
    )
    sky, peak = pl.pallas_call(
        hand_over,
        out_shape=(jax.ShapeDtypeStruct((8, LEN), F32), jax.ShapeDtypeStruct((1, SKY), F32)),
        in_specs=[anywhere, anywhere],
        out_specs=(anywhere, anywhere),
        scratch_shapes=[dma((2,))],
        compiler_params=pltpu.CompilerParams(vmem_limit_bytes=1024 * 1024),
    )(sky, peak)
    return (sky[None], peak)


def solution(mesh):
    return jax.shard_map(
        shards,
        mesh=mesh,
        in_specs=(
            P(None, "det", "tmpl", None),
            P(None, None, "tmpl", "det"),
            P(None, "tmpl", None),
            P(),
            P(),
        ),
        out_specs=(P("det", "tmpl", None), P("det", None)),
        check_vma=False,
    )
```
